32 devices in a mesh: dp: 8 (over z, y), row: 2 (over core), col: 2 (over x).
Axes of the slice: x: 2, y: 2, z: 4, core: 2. Of those that a mesh axis runs over, the one named last changes fastest.
Arguments:
- tokens: bfloat16 [8192, 2048], P(('dp', 'row', 'col')), may hold values from -6 to 6
- segments: int32 [8, 1024], P('dp'), may hold values from 0 to 7, never falling along the last dimension, each value on 1 to 512 neighbouring positions
- attn_gain: float32 [2048], replicated, may hold values from 0.5 to 1.5
- w_query: bfloat16 [2048, 2048], P(None, ('row', 'col')), may hold values from -0.125 to 0.125
- w_key: bfloat16 [2048, 256], P(None, ('row', 'col')), may hold values from -0.125 to 0.125
- w_value: bfloat16 [2048, 256], P(None, ('row', 'col')), may hold values from -0.125 to 0.125
- w_out: bfloat16 [2048, 2048], P(('row', 'col')), may hold values from -0.75 to 0.75
- ffn_gain: float32 [2048], replicated, may hold values from 0.5 to 1.5
- w_gate: bfloat16 [2048, 5632], P(None, ('row', 'col')), may hold values from -0.125 to 0.125
- w_up: bfloat16 [2048, 5632], P(None, ('row', 'col')), may hold values from -0.125 to 0.125
- w_down: bfloat16 [5632, 2048], P(('row', 'col')), may hold values from -0.078125 to 0.078125
- out_cotangent: bfloat16 [8192, 2048], P(('dp', 'row', 'col')), may hold values from -6 to 6
Outputs:
- mixed: bfloat16 [8192, 2048], P(('dp', 'row', 'col'))
- input_grad: float32 [8192, 2048], P(('dp', 'row', 'col'))
- attn_gain_grad: float32 [2048], replicated
- query_grad: float32 [2048, 2048], P('dp', ('row', 'col'))
- key_grad: float32 [2048, 256], P('dp', ('row', 'col'))
- value_grad: float32 [2048, 256], P('dp', ('row', 'col'))
- out_proj_grad: float32 [2048, 2048], P(('row', 'col'), 'dp')
- ffn_gain_grad: float32 [2048], replicated
- gate_grad: float32 [2048, 5632], P('dp', ('row', 'col'))
- up_grad: float32 [2048, 5632], P('dp', ('row', 'col'))
- down_grad: float32 [5632, 2048], P(('row', 'col'), 'dp')
The draws below stay inside these ranges and needn't reach their ends.
Inputs may be any that keep to these rules, and one draw needn't show every extreme that they name: `segments`: within each sequence document numbers never fall; each document has 1 to 512 tokens, and one has exactly 512.
All inputs are finite; a program needn't handle non-finite values.
Results may differ from the reference program's by a relative error of at most 0.02.
Values may be sent and summed in bfloat16 or wider, within the bound.
No kernel may reach another device: no remote copies, remote signals or barrier semaphores. Data moves between devices by JAX's collectives and lax.ppermute only.
A program may use at most 256 MiB of HBM per device.

```python
import math
import jax
import jax.numpy as jnp
import numpy as np
from jax import lax

D = 2048
HQ = 32
KV = 4
HD = 64
FF = 5632
LEN = 1024
SEQS = 8
TOKENS = 8192


def strengthened(entries, key, source, target, blocks, factor):
    def block_of(dim):
        return (jnp.arange(entries.shape[dim]) // (entries.shape[dim] // blocks)).reshape((-1,) + (1,) * (entries.ndim - 1 - dim))

    first = jax.random.permutation(key, blocks)[block_of(target)]
    second = (block_of(target) + blocks // 2) % blocks
    return jnp.where((block_of(source) == first) | (block_of(source) == second), factor * entries, entries)


def level_of(key, extent, split, least, top_value):
    def one(dim, shards_of):
        steps = jax.random.uniform(jax.random.fold_in(jax.random.fold_in(key, 6), dim), (shards_of,), jnp.float32, least / len(split), top_value / len(split))
        return jnp.repeat(jnp.exp(steps), extent[dim] // shards_of).reshape((-1,) + (1,) * (len(extent) - dim - 1))

    level = one(*split[0])
    for cut in split[1:]:
        level = level * one(*cut)
    return level


def length_profile(number_of, total, most, skew):
    loads = [(1 << 20) // math.isqrt(standing ** skew) + 1 for standing in range(2, number_of + 1)]
    surplus, holding = total - most - (number_of - 1), [1] * (number_of - 1)
    while surplus > 0:
        movable = [i for i in range(number_of - 1) if holding[i] < most]
        pool, budget = sum([loads[i] for i in movable]), surplus
        for i in movable:
            addition = min(most - holding[i], max(1, budget * loads[i] // pool), surplus)
            holding[i] = holding[i] + addition
            surplus = surplus - addition
    return np.array([most] + holding)


def ragged(key, amount, total, bound, skew):
    if amount == 2:
        one = jax.random.randint(key, (), max(1, total - bound), min(bound, total - 1) + 1)
        return jnp.stack([one, total - one])
    tallies = jnp.asarray(length_profile(amount, total, bound, skew), jnp.int32)
    twos = (amount - 1) // 2
    donor, taker = tallies[1:1 + 2 * twos:2], tallies[2:2 + 2 * twos:2]
    slack = jnp.minimum(donor - 1, bound - taker)
    moved = jax.random.randint(jax.random.fold_in(key, 1), (twos,), 0, 1 << 20) % (slack + 1)
    tallies = tallies.at[1:1 + 2 * twos:2].set(donor - moved).at[2:2 + 2 * twos:2].set(taker + moved)
    return tallies[jax.random.permutation(jax.random.fold_in(key, 2), amount)]


def bell_draw(own_key, extent, spread, limit, shards=(), held_as=jnp.bfloat16):
    array = jax.random.normal(own_key, extent, jnp.float32) * spread
    if len(shards) > 0:
        array = level_of(own_key, extent, shards, -0.22, 0.18) * array
    return jnp.clip(array, min=-limit, max=limit).astype(held_as)


def heavy_noise(stream_key, shape, scale, bound, pieces, heavy, kind=jnp.bfloat16):
    drawn = scale * jax.random.normal(stream_key, shape, jnp.float32)
    if pieces:
        drawn = drawn * level_of(stream_key, shape, pieces, -0.22, 0.18)
    return jnp.clip(strengthened(drawn, jax.random.fold_in(stream_key, 3), *heavy), -bound, bound).astype(kind)


def setup_inputs(seed: int = 0) -> dict:
    arg_keys = jax.random.split(jax.random.key(seed), 13)
    return {
        "tokens": heavy_noise(arg_keys[0], (TOKENS, D), 1.0, 6.0, ((0, 32),), (0, 1, 32, 2.75)),
        "segments": jax.vmap(lambda own: jnp.searchsorted(jnp.cumsum(ragged(own, max(4, LEN // 128), LEN, LEN // 2, 1)), jnp.arange(LEN), side="right"))(jax.random.split(arg_keys[1], SEQS)).reshape((SEQS, LEN)).astype(jnp.int32),
        "attn_gain": jnp.clip(1.0 + 0.1 * jax.random.normal(arg_keys[2], (D,), jnp.float32), 0.5, 1.5),
        "w_query": bell_draw(arg_keys[3], (D, HQ * HD), D ** -0.5, 0.125, ((1, 4),)),
        "w_key": bell_draw(arg_keys[4], (D, KV * HD), D ** -0.5, 0.125, ((1, 4),)),
        "w_value": bell_draw(arg_keys[5], (D, KV * HD), D ** -0.5, 0.125, ((1, 4),)),
        "w_out": bell_draw(arg_keys[6], (HQ * HD, D), (HQ * HD // 32) ** -0.5, 0.75, ((0, 4),)),
        "ffn_gain": jnp.clip(1.0 + 0.1 * jax.random.normal(arg_keys[7], (D,), jnp.float32), 0.5, 1.5),
        "w_gate": bell_draw(arg_keys[8], (D, FF), D ** -0.5, 0.125, ((1, 4),)),
        "w_up": bell_draw(arg_keys[9], (D, FF), D ** -0.5, 0.125, ((1, 4),)),
        "w_down": bell_draw(arg_keys[10], (FF, D), FF ** -0.5, 0.078125, ((0, 4),)),
        "out_cotangent": heavy_noise(arg_keys[11], (TOKENS, D), 1.0, 6.0, ((0, 32),), (0, 1, 32, 2.75)),
    }


PRECISE = lax.Precision.HIGHEST
EPSILON = 1e-05
MASKED_SCORE = -1e+30

@jax.custom_vjp
def low(v):
    return lax.optimization_barrier(v.astype(jnp.bfloat16)).astype(jnp.float32)

@jax.custom_vjp
def low_back(v):
    return v

def low_keep(v):
    return (low(v), None)

def low_pass(kept, grad):
    return (grad,)

def back_keep(v):
    return (v, None)

def back_low(kept, grad):
    return (low(grad),)
low.defvjp(low_keep, low_pass)
low_back.defvjp(back_keep, back_low)

def positions(segment_ids):
    indices = jnp.arange(segment_ids.shape[-1], dtype=jnp.int32)
    previous = jnp.concatenate([segment_ids[..., :1] - 1, segment_ids[..., :-1]], axis=-1)
    starts = jnp.where(segment_ids != previous, indices, 0).astype(jnp.int32)
    return indices - lax.cummax(starts, axis=segment_ids.ndim - 1)

def rotate(values, position, direction):
    half_dim = values.shape[-1] // 2
    exponent = jnp.arange(half_dim, dtype=jnp.float32) * (-2.0 / values.shape[-1])
    angles = position.astype(jnp.float32)[:, None] * (10000.0 ** exponent)[None, :]
    cosine = jnp.concatenate([jnp.cos(angles), jnp.cos(angles)], axis=-1)[:, None, :]
    sine = jnp.concatenate([jnp.sin(angles), jnp.sin(angles)], axis=-1)[:, None, :]
    first_half = values[..., :half_dim]
    second_half = values[..., half_dim:]
    turned = jnp.concatenate([-second_half, first_half], axis=-1)
    return values * cosine + turned * (direction * sine)

def normalize(values, gain):
    return values * lax.rsqrt(lax.optimization_barrier(jnp.mean(values * values, axis=-1, keepdims=True)) + EPSILON) * gain

def attend_one(queries, key_rows, value_rows, segment_ids):
    length = queries.shape[0]
    position = positions(segment_ids)
    kv_heads = key_rows.shape[1] // HD
    queries = low(rotate(queries.reshape(length, -1, HD), position, 1.0))
    queries = queries.reshape(length, kv_heads, -1, HD)
    key_rows = low(rotate(key_rows.reshape(length, kv_heads, HD), position, 1.0))
    value_rows = value_rows.reshape(length, kv_heads, HD)
    scores = low_back(jnp.einsum('qhgd,khd->hgqk', queries, key_rows, precision=PRECISE) * HD ** (-0.5))
    indices = jnp.arange(length)
    allowed = (segment_ids[:, None] == segment_ids[None, :]) & (indices[None, :] <= indices[:, None])
    scores = jnp.where(allowed, scores, MASKED_SCORE)
    shifted = jnp.exp(scores - lax.optimization_barrier(jnp.max(scores, axis=-1, keepdims=True)))
    weights = low(shifted / lax.optimization_barrier(jnp.sum(shifted, axis=-1, keepdims=True)))
    mixture = jnp.einsum('hgqk,khd->qhgd', weights, value_rows, precision=PRECISE)
    return mixture.reshape(length, -1)

def reference(tokens, segments, attn_gain, w_query, w_key, w_value, w_out, ffn_gain, w_gate, w_up, w_down, out_cotangent):
    total_rows = tokens.shape[0]
    sequences = segments.shape[0]

    def forward(inputs, gain_one, query_w, key_w, value_w, out_w, gain_two, gate_w, up_w, down_w):
        normed = low(normalize(inputs, gain_one))
        queries = low_back(jnp.dot(normed, query_w, precision=PRECISE))
        key_rows = low_back(jnp.dot(normed, key_w, precision=PRECISE))
        value_rows = low(low_back(jnp.dot(normed, value_w, precision=PRECISE)))
        attend = jax.checkpoint(attend_one)
        mixture = lax.map(lambda members: attend(*members), (queries.reshape(sequences, LEN, -1), key_rows.reshape(sequences, LEN, -1), value_rows.reshape(sequences, LEN, -1), segments))
        mixture = low(low_back(mixture.reshape(total_rows, -1)))
        middle = inputs + low_back(jnp.dot(mixture, out_w, precision=PRECISE))
        normed_two = low(normalize(middle, gain_two))
        gate_pre = low_back(jnp.dot(normed_two, gate_w, precision=PRECISE))
        up_pre = low_back(jnp.dot(normed_two, up_w, precision=PRECISE))
        hidden = low(gate_pre * jax.nn.sigmoid(gate_pre) * up_pre)
        return middle + low_back(jnp.dot(hidden, down_w, precision=PRECISE))
    floats = [member.astype(jnp.float32) for member in (tokens, attn_gain, w_query, w_key, w_value, w_out, ffn_gain, w_gate, w_up, w_down)]
    result, pullback = jax.vjp(forward, *floats)
    grads = pullback(out_cotangent.astype(jnp.float32))
    return (result.astype(jnp.bfloat16), grads[0], grads[1], grads[2], grads[3], grads[4], grads[5], grads[6], grads[7], grads[8], grads[9])
```

```python
import jax
import jax.numpy as jnp
from jax import lax
from jax.experimental import pallas as pl
from jax.experimental.pallas import tpu as pltpu
from jax.sharding import PartitionSpec as P

HD = 64
EPSILON = 1e-05
MASKED_SCORE = -1e30
BLOCK = 256
TILE = 128
SWAP = ((0, 1), (1, 0))


def positions(segment_ids):
    indices = jnp.arange(segment_ids.shape[-1], dtype=jnp.int32)
    previous = jnp.concatenate([segment_ids[..., :1] - 1, segment_ids[..., :-1]], axis=-1)
    starts = jnp.where(segment_ids != previous, indices, 0)
    return indices - lax.cummax(starts, axis=segment_ids.ndim - 1)


def rope_tables(position):
    exponent = jnp.arange(HD // 2, dtype=jnp.float32) * (-2.0 / HD)
    angles = position.astype(jnp.float32)[:, None] * (10000.0**exponent)[None, :]
    cosine, sine = jnp.cos(angles), jnp.sin(angles)
    return (
        jnp.concatenate([cosine] * 4, axis=1),
        jnp.concatenate([-sine, sine, -sine, sine], axis=1),
    )


def nt(left, right):
    return lax.dot_general(
        left, right, (((1,), (1,)), ((), ())), preferred_element_type=jnp.float32
    )


def nn(left, right):
    return lax.dot_general(
        left, right, (((1,), (0,)), ((), ())), preferred_element_type=jnp.float32
    )


def tn(left, right):
    return lax.dot_general(
        left, right, (((0,), (0,)), ((), ())), preferred_element_type=jnp.float32
    )


def lane_marks():
    lane = lax.broadcasted_iota(jnp.int32, (BLOCK, TILE), 1)
    return lane, lane < HD, lane % HD < HD // 2


def turn_by(values, cosine, sine, first):
    turned = jnp.where(
        first, pltpu.roll(values, TILE - HD // 2, 1), pltpu.roll(values, HD // 2, 1)
    )
    return values * cosine + turned * sine


def rows_of(places, block):
    return pl.ds(pl.multiple_of(places[block], BLOCK), BLOCK)


def attend_kernel(
    places, proj, cosine, sine, seg_col, seg_row, mixed, rotated, log_sums, keys, values
):
    length = proj.shape[0]
    width = mixed.shape[1]
    blocks = length // BLOCK
    lane, low, first = lane_marks()
    for block in range(blocks):
        rows = rows_of(places, block)
        at = slice(block * BLOCK, (block + 1) * BLOCK)
        pair = proj[rows, width:]
        turned = jnp.where(low, turn_by(pair, cosine[at], sine[at], first), pair)
        swapped = pltpu.roll(turned, HD, 1)
        rotated[rows, width:] = turned.astype(jnp.bfloat16)
        keys[at] = jnp.where(low, turned, swapped).astype(jnp.bfloat16)
        values[at] = jnp.where(low, swapped, turned).astype(jnp.bfloat16)
    for block in range(blocks):
        rows = rows_of(places, block)
        at = slice(block * BLOCK, (block + 1) * BLOCK)
        begin = max(0, block - 2) * BLOCK
        span = slice(begin, (block + 1) * BLOCK)
        count = (block + 1) * BLOCK - begin
        key_at = begin + lax.broadcasted_iota(jnp.int32, (BLOCK, count), 1)
        query_at = block * BLOCK + lax.broadcasted_iota(jnp.int32, (BLOCK, count), 0)
        allowed = (seg_col[at] == seg_row[:, span]) & (key_at <= query_at)
        bias = jnp.where(allowed, 0.0, MASKED_SCORE)
        key_span = keys[span]
        value_span = values[span]

        def one_pair(number, logs):
            columns = pl.ds(pl.multiple_of(number * TILE, TILE), TILE)
            query = turn_by(proj[rows, columns], cosine[at], sine[at], first) * HD ** (-0.5)
            query = query.astype(jnp.bfloat16)
            rotated[rows, columns] = query
            results = []
            for half in range(2):
                chosen = jnp.where(low if half == 0 else ~low, query, jnp.zeros_like(query))
                scores = nt(chosen, key_span) + bias
                largest = jnp.max(scores, axis=1, keepdims=True)
                shifted = jnp.exp(scores - largest)
                total = jnp.sum(shifted, axis=1, keepdims=True)
                results.append(nn(shifted.astype(jnp.bfloat16), value_span) * (1.0 / total))
                logs = jnp.where(lane == 2 * number + half, largest + jnp.log(total), logs)
            mixed[rows, columns] = jnp.where(low, results[0], results[1]).astype(jnp.bfloat16)
            return logs

        logs = lax.fori_loop(0, width // TILE, one_pair, jnp.zeros((BLOCK, TILE), jnp.float32))
        log_sums[:, at] = logs.T[: log_sums.shape[0]]


def attend_back_kernel(
    places,
    rotated,
    grad_mixed,
    log_sums,
    cosine,
    sine,
    seg_col,
    seg_row,
    grads,
    keys,
    values,
    key_sum,
    value_sum,
):
    length = rotated.shape[0]
    width = grad_mixed.shape[1]
    blocks = length // BLOCK
    _, low, first = lane_marks()
    key_sum[...] = jnp.zeros_like(key_sum)
    value_sum[...] = jnp.zeros_like(value_sum)
    for block in range(blocks):
        rows = rows_of(places, block)
        at = slice(block * BLOCK, (block + 1) * BLOCK)
        pair = rotated[rows, width:].astype(jnp.float32)
        swapped = pltpu.roll(pair, HD, 1)
        keys[at] = jnp.where(low, pair, swapped).astype(jnp.bfloat16)
        values[at] = jnp.where(low, swapped, pair).astype(jnp.bfloat16)
    for block in range(blocks):
        rows = rows_of(places, block)
        at = slice(block * BLOCK, (block + 1) * BLOCK)
        begin = max(0, block - 2) * BLOCK
        span = slice(begin, (block + 1) * BLOCK)
        count = (block + 1) * BLOCK - begin
        key_at = begin + lax.broadcasted_iota(jnp.int32, (count, BLOCK), 0)
        query_at = block * BLOCK + lax.broadcasted_iota(jnp.int32, (count, BLOCK), 1)
        allowed = (seg_col[span] == seg_row[:, at]) & (key_at <= query_at)
        bias = jnp.where(allowed, 0.0, MASKED_SCORE)
        key_span = keys[span]
        value_span = values[span]

        def one_pair(number, carry):
            columns = pl.ds(pl.multiple_of(number * TILE, TILE), TILE)
            query = rotated[rows, columns]
            grad = grad_mixed[rows, columns]
            results = []
            for half in range(2):
                side = low if half == 0 else ~low
                chosen = jnp.where(side, query, jnp.zeros_like(query))
                chosen_grad = jnp.where(side, grad, jnp.zeros_like(grad))
                logs = log_sums[pl.ds(2 * number + half, 1), at]
                probs = jnp.exp(nt(key_span, chosen) + bias - logs)
                grad_probs = nt(value_span, chosen_grad)
                inner = jnp.sum(probs * grad_probs, axis=0, keepdims=True)
                grad_scores = (probs * (grad_probs - inner)).astype(jnp.bfloat16)
                value_sum[span] += nn(probs.astype(jnp.bfloat16), chosen_grad)
                key_sum[span] += nn(grad_scores, chosen)
                results.append(tn(grad_scores, key_span))
            grad_query = jnp.where(low, results[0], results[1]) * HD ** (-0.5)
            grads[rows, columns] = turn_by(grad_query, cosine[at], -sine[at], first).astype(
                jnp.bfloat16
            )
            return carry

        lax.fori_loop(0, width // TILE, one_pair, 0)
    for block in range(blocks):
        rows = rows_of(places, block)
        at = slice(block * BLOCK, (block + 1) * BLOCK)
        grad_key = key_sum[at]
        grad_key = turn_by(grad_key + pltpu.roll(grad_key, HD, 1), cosine[at], -sine[at], first)
        grad_value = value_sum[at]
        grad_value = grad_value + pltpu.roll(grad_value, HD, 1)
        grads[rows, width:] = jnp.where(low, grad_key, grad_value).astype(jnp.bfloat16)


SMEM = pl.BlockSpec(memory_space=pltpu.SMEM)
VMEM = pl.BlockSpec(memory_space=pltpu.VMEM)


def attend(places, proj, cosine, sine, seg_col, seg_row):
    length, total = proj.shape
    width = total - TILE
    return pl.pallas_call(
        attend_kernel,
        out_shape=(
            jax.ShapeDtypeStruct((length, width), jnp.bfloat16),
            jax.ShapeDtypeStruct((length, total), jnp.bfloat16),
            jax.ShapeDtypeStruct((width // HD, length), jnp.float32),
        ),
        in_specs=[SMEM] + [VMEM] * 5,
        out_specs=(VMEM,) * 3,
        scratch_shapes=[pltpu.VMEM((length, TILE), jnp.bfloat16)] * 2,
        compiler_params=pltpu.CompilerParams(vmem_limit_bytes=48 << 20),
        cost_estimate=pl.CostEstimate(
            flops=17 << 30, bytes_accessed=8 << 20, transcendentals=0
        ),
    )(places, proj, cosine, sine, seg_col, seg_row)


def attend_back(places, rotated, grad_mixed, log_sums, cosine, sine, seg_col, seg_row):
    length, total = rotated.shape
    return pl.pallas_call(
        attend_back_kernel,
        out_shape=jax.ShapeDtypeStruct((length, total), jnp.bfloat16),
        in_specs=[SMEM] + [VMEM] * 7,
        out_specs=VMEM,
        scratch_shapes=[pltpu.VMEM((length, TILE), jnp.bfloat16)] * 2
        + [pltpu.VMEM((length, TILE), jnp.float32)] * 2,
        compiler_params=pltpu.CompilerParams(vmem_limit_bytes=48 << 20),
        cost_estimate=pl.CostEstimate(
            flops=26 << 30, bytes_accessed=8 << 20, transcendentals=0
        ),
    )(places, rotated, grad_mixed, log_sums, cosine, sine, seg_col, seg_row)


def to_core(values):
    return lax.ppermute(values, "row", SWAP)


def to_chip(values):
    return lax.ppermute(values, "col", SWAP)


def gather_blocks(own):
    across = to_chip(own)
    return own, to_core(own), across, to_core(across)


def scatter_blocks(products):
    own, beside, across, diagonal = products
    across_sum = (across + to_core(diagonal.astype(jnp.bfloat16))).astype(jnp.bfloat16)
    return own + to_core(beside.astype(jnp.bfloat16)) + to_chip(across_sum)


def pick(values, index, axis):
    return lax.dynamic_index_in_dim(values, index, axis, keepdims=False)


def halve_inner(values, line, inner, index, dp):
    while inner > 1:
        half = inner // 2
        bit = (index // half) % 2
        values = values.reshape((line, 2, half) + values.shape[2:])
        swaps = [(device, device ^ half) for device in range(dp)]
        arrived = lax.ppermute(pick(values, 1 - bit, 1), "dp", swaps)
        values = (pick(values, bit, 1) + arrived).astype(jnp.bfloat16)
        inner = half
    return values.reshape((line,) + values.shape[2:])


def along_line(values, line, inner, index):
    place = index // inner
    up = down = None
    for step in range(1, line):
        upward = pick(values, jnp.clip(line - step + place, 0, line - 1), 0)
        downward = pick(values, jnp.clip(place + step - line, 0, line - 1), 0)
        if step > 1:
            upward = upward + up
            downward = downward + down
        up_pairs, down_pairs = [], []
        for at in range(line - 1):
            if at < step:
                for low in range(inner):
                    up_pairs.append((at * inner + low, (at + 1) * inner + low))
                    mirror = line - 1 - at
                    down_pairs.append((mirror * inner + low, (mirror - 1) * inner + low))
        up = lax.ppermute(upward, "dp", up_pairs)
        down = lax.ppermute(downward, "dp", down_pairs)
    mine = pick(values, place, 0).astype(jnp.float32)
    return mine + up.astype(jnp.float32) + down.astype(jnp.float32)


def sum_over_dp(values, sizes, line_first):
    dp, line, inner = sizes
    index = lax.axis_index("dp")
    rows, columns = values.shape
    blocks = values.reshape(line, inner, rows // dp, columns)
    if not line_first:
        return along_line(halve_inner(blocks, line, inner, index, dp), line, inner, index)
    part = along_line(blocks, line, inner, index).astype(jnp.bfloat16)
    return halve_inner(part[None], 1, inner, index, dp)[0].astype(jnp.float32)


def sum_everywhere(values, dp):
    values = values + to_core(values)
    values = values + to_chip(values)
    step = 1
    while step < dp:
        values = values + lax.ppermute(values, "dp", [(i, i ^ step) for i in range(dp)])
        step *= 2
    return values


def norm_back(grad_normed, unit_rows, inverse, gain):
    scaled = grad_normed * gain
    inner = jnp.mean(scaled * unit_rows, axis=-1, keepdims=True)
    return inverse * (scaled - unit_rows * inner), jnp.sum(grad_normed * unit_rows, axis=0)


def local_for(dp):
    line = 4 if dp % 4 == 0 else 1
    sizes = (dp, line, dp // line)

    def local(
        tokens,
        segments,
        attn_gain,
        w_query,
        w_key,
        w_value,
        w_out,
        ffn_gain,
        w_gate,
        w_up,
        w_down,
        out_cotangent,
    ):
        query_width = w_query.shape[1]
        kv_width = w_key.shape[1]
        length = segments.shape[1]
        row, col = lax.axis_index("row"), lax.axis_index("col")
        places = jnp.stack(
            [((block // 2) ^ row) + 2 * ((block % 2) ^ col) for block in range(4)]
        ) * (length // 4)
        places = places.astype(jnp.int32)
        cosine, sine = rope_tables(positions(segments).reshape(length))
        seg_col = segments.reshape(length, 1)
        seg_row = segments.reshape(1, length)
        qkv_weight = jnp.concatenate([w_query, w_key, w_value], axis=1)

        inputs = tokens.astype(jnp.float32)
        inverse_one = lax.rsqrt(jnp.mean(inputs * inputs, axis=-1, keepdims=True) + EPSILON)
        unit_one = inputs * inverse_one
        normed_one = (unit_one * attn_gain).astype(jnp.bfloat16)
        blocks_one = gather_blocks(normed_one)
        proj = jnp.concatenate([nn(block, qkv_weight) for block in blocks_one], axis=0)
        attn_mixed, rotated, log_sums = attend(places, proj, cosine, sine, seg_col, seg_row)
        rows = length // 4
        mixed_blocks = [attn_mixed[i * rows : (i + 1) * rows] for i in range(4)]
        middle = inputs + scatter_blocks([nn(block, w_out) for block in mixed_blocks])

        cot_blocks = gather_blocks(out_cotangent)
        grad_rows = jnp.concatenate(cot_blocks, axis=0)
        inverse_two = lax.rsqrt(jnp.mean(middle * middle, axis=-1, keepdims=True) + EPSILON)
        unit_two = middle * inverse_two
        normed_two = (unit_two * ffn_gain).astype(jnp.bfloat16)
        gathered_two = jnp.concatenate(gather_blocks(normed_two), axis=0)
        gate_pre = nn(gathered_two, w_gate)
        up_pre = nn(gathered_two, w_up)
        sigmoid_gate = jax.nn.sigmoid(gate_pre)
        hidden = (gate_pre * sigmoid_gate * up_pre).astype(jnp.bfloat16)
        down_grad = sum_over_dp(tn(grad_rows, hidden).astype(jnp.bfloat16), sizes, False)
        grad_hidden = nt(grad_rows, w_down)
        slope = sigmoid_gate + gate_pre * sigmoid_gate * (1.0 - sigmoid_gate)
        grad_gate = (grad_hidden * up_pre * slope).astype(jnp.bfloat16)
        grad_up = (grad_hidden * gate_pre * sigmoid_gate).astype(jnp.bfloat16)
        gate_grad = sum_over_dp(tn(gathered_two, grad_gate).astype(jnp.bfloat16), sizes, True)
        up_grad = sum_over_dp(tn(gathered_two, grad_up).astype(jnp.bfloat16), sizes, False)

        back_two = nt(grad_gate, w_gate) + nt(grad_up, w_up)
        grad_normed_two = scatter_blocks([back_two[i * rows : (i + 1) * rows] for i in range(4)])
        grad_middle_norm, gain_two_grad = norm_back(
            grad_normed_two, unit_two, inverse_two, ffn_gain
        )
        grad_middle = out_cotangent.astype(jnp.float32) + grad_middle_norm
        grad_attn_blocks = gather_blocks(grad_middle.astype(jnp.bfloat16))
        grad_mixed = jnp.concatenate(
            [nt(block, w_out).astype(jnp.bfloat16) for block in grad_attn_blocks], axis=0
        )
        out_terms = jnp.concatenate(grad_attn_blocks, axis=0)
        out_grad = sum_over_dp(tn(out_terms, attn_mixed).astype(jnp.bfloat16), sizes, False)
        down = nn(hidden, w_down)
        output = middle + scatter_blocks([down[i * rows : (i + 1) * rows] for i in range(4)])

        grad_qkv = attend_back(
            places, rotated, grad_mixed, log_sums, cosine, sine, seg_col, seg_row
        )
        qkv_terms = tn(jnp.concatenate(blocks_one, axis=0), grad_qkv)
        gain_one_grad = jnp.sum(qkv_terms * qkv_weight.astype(jnp.float32), axis=1) / attn_gain
        qkv_grad = sum_over_dp(qkv_terms.astype(jnp.bfloat16), sizes, False)
        back_one = nt(grad_qkv, qkv_weight)
        grad_normed_one = scatter_blocks([back_one[i * rows : (i + 1) * rows] for i in range(4)])
        scaled = grad_normed_one * attn_gain
        inner = jnp.mean(scaled * unit_one, axis=-1, keepdims=True)
        input_grad = grad_middle + inverse_one * (scaled - unit_one * inner)
        gains = sum_everywhere(jnp.stack([gain_one_grad, gain_two_grad]), dp)
        key_end = query_width + kv_width
        return (
            output.astype(jnp.bfloat16),
            input_grad,
            gains[0],
            qkv_grad[:, :query_width],
            qkv_grad[:, query_width:key_end],
            qkv_grad[:, key_end:],
            out_grad.T,
            gains[1],
            gate_grad,
            up_grad,
            down_grad.T,
        )

    return local


def solution(mesh):
    rows = P(("dp", "row", "col"), None)
    columns = P(None, ("row", "col"))
    placed = (
        rows,
        P("dp", None),
        P(),
        columns,
        columns,
        columns,
        P(("row", "col"), None),
        P(),
        columns,
        columns,
        P(("row", "col"), None),
        rows,
    )
    summed = P("dp", ("row", "col"))
    turned = P(("row", "col"), "dp")
    return jax.shard_map(
        local_for(mesh.shape["dp"]),
        mesh=mesh,
        in_specs=placed,
        out_specs=(rows, rows, P(), summed, summed, summed, turned, P(), summed, summed, turned),
        check_vma=False,
    )
```

```python
import jax
import jax.numpy as jnp
from jax import lax
from jax.experimental import pallas as pl
from jax.experimental.pallas import tpu as pltpu
from jax.sharding import PartitionSpec as P

HD = 64
EPSILON = 1e-05
MASKED_SCORE = -1e30
BLOCK = 256
TILE = 128
SWAP = ((0, 1), (1, 0))


def positions(segment_ids):
    indices = jnp.arange(segment_ids.shape[-1], dtype=jnp.int32)
    previous = jnp.concatenate([segment_ids[..., :1] - 1, segment_ids[..., :-1]], axis=-1)
    starts = jnp.where(segment_ids != previous, indices, 0)
    return indices - lax.cummax(starts, axis=segment_ids.ndim - 1)


def rope_tables(position):
    exponent = jnp.arange(HD // 2, dtype=jnp.float32) * (-2.0 / HD)
    angles = position.astype(jnp.float32)[:, None] * (10000.0**exponent)[None, :]
    cosine, sine = jnp.cos(angles), jnp.sin(angles)
    return (
        jnp.concatenate([cosine] * 4, axis=1),
        jnp.concatenate([-sine, sine, -sine, sine], axis=1),
    )


def nt(left, right):
    return lax.dot_general(
        left, right, (((1,), (1,)), ((), ())), preferred_element_type=jnp.float32
    )


def nn(left, right):
    return lax.dot_general(
        left, right, (((1,), (0,)), ((), ())), preferred_element_type=jnp.float32
    )


def tn(left, right):
    return lax.dot_general(
        left, right, (((0,), (0,)), ((), ())), preferred_element_type=jnp.float32
    )


def lane_marks():
    lane = lax.broadcasted_iota(jnp.int32, (BLOCK, TILE), 1)
    return lane, lane < HD, lane % HD < HD // 2


def turn_by(values, cosine, sine, first):
    turned = jnp.where(
        first, pltpu.roll(values, TILE - HD // 2, 1), pltpu.roll(values, HD // 2, 1)
    )
    return values * cosine + turned * sine


def rows_of(places, block):
    return pl.ds(pl.multiple_of(places[block], BLOCK), BLOCK)


def segment_column(seg_row, at):
    return jnp.broadcast_to(seg_row[:, at], (TILE, BLOCK)).T


def attend_block(block, places, rotated, keys, values, seg_row, mixed, target, log_sums):
    width = mixed.shape[1]
    lane, low, _ = lane_marks()
    rows = rows_of(places, block)
    at = slice(block * BLOCK, (block + 1) * BLOCK)
    begin = max(0, block - 2) * BLOCK
    span = slice(begin, (block + 1) * BLOCK)
    count = (block + 1) * BLOCK - begin
    key_at = begin + lax.broadcasted_iota(jnp.int32, (BLOCK, count), 1)
    query_at = block * BLOCK + lax.broadcasted_iota(jnp.int32, (BLOCK, count), 0)
    seg_col = segment_column(seg_row, at)[:, :1]
    allowed = (seg_col == seg_row[:, span]) & (key_at <= query_at)
    bias = jnp.where(allowed, 0.0, MASKED_SCORE)
    key_span = keys[span]
    value_span = values[span]

    def one_pair(number, logs):
        columns = pl.ds(pl.multiple_of(number * TILE, TILE), TILE)
        query = rotated[rows, columns]
        results = []
        for half in range(2):
            chosen = jnp.where(low if half == 0 else ~low, query, jnp.zeros_like(query))
            scores = nt(chosen, key_span) + bias
            largest = jnp.max(scores, axis=1, keepdims=True)
            shifted = jnp.exp(scores - largest)
            total = jnp.sum(shifted, axis=1, keepdims=True)
            results.append(nn(shifted.astype(jnp.bfloat16), value_span) * (1.0 / total))
            logs = jnp.where(lane == 2 * number + half, largest + jnp.log(total), logs)
        mixed[target, columns] = jnp.where(low, results[0], results[1]).astype(jnp.bfloat16)
        return logs

    logs = lax.fori_loop(0, width // TILE, one_pair, jnp.zeros((BLOCK, TILE), jnp.float32))
    log_sums[:, at] = logs.T[: log_sums.shape[0]]


def key_value_rows(rotated, rows, keys, values, at, low):
    width = rotated.shape[1] - TILE
    pair = rotated[rows, width:].astype(jnp.float32)
    swapped = pltpu.roll(pair, HD, 1)
    keys[at] = jnp.where(low, pair, swapped).astype(jnp.bfloat16)
    values[at] = jnp.where(low, swapped, pair).astype(jnp.bfloat16)


def attend_side(side, places, rotated, keys, values, seg_row, mixed, log_sums):
    blocks = rotated.shape[0] // BLOCK
    for parity in range(2):

        @pl.when((places[blocks] ^ side) == parity)
        def _():
            for block in range(parity, blocks, 2):
                start = places[block] - side * 2 * BLOCK
                target = pl.ds(pl.multiple_of(start, BLOCK), BLOCK)
                attend_block(
                    block, places, rotated, keys, values, seg_row, mixed, target, log_sums
                )


def attend_far_kernel(
    places, near, across, diagonal, weight, w_out, cosine, sine, seg_row,
    mixed, rotated, log_sums, out_across, out_diagonal, keys, values,
):
    length, total = rotated.shape
    width = total - TILE
    blocks = length // BLOCK
    _, low, first = lane_marks()
    for block in range(blocks):
        rows = rows_of(places, block)
        at = slice(block * BLOCK, (block + 1) * BLOCK)

        def turn_all(proj):
            for start in range(0, width, TILE):
                query = turn_by(proj[:, start : start + TILE], cosine[at], sine[at], first)
                rotated[rows, start : start + TILE] = (query * HD ** (-0.5)).astype(jnp.bfloat16)
            pair = proj[:, width:]
            turned = jnp.where(low, turn_by(pair, cosine[at], sine[at], first), pair)
            rotated[rows, width:] = turned.astype(jnp.bfloat16)

        for piece, source in ((0, None), (1, None), (2, across), (3, diagonal)):

            @pl.when(places[block] == piece * BLOCK)
            def _(piece=piece, source=source):
                if source is None:
                    turn_all(near[piece * BLOCK : (piece + 1) * BLOCK])
                else:
                    turn_all(nn(source[...], weight[...]))

        key_value_rows(rotated, rows, keys, values, at, low)
    attend_side(1, places, rotated, keys, values, seg_row, mixed, log_sums)
    out_diagonal[...] = nn(mixed[BLOCK:], w_out[...]).astype(jnp.bfloat16)
    out_across[...] = nn(mixed[:BLOCK], w_out[...]).astype(jnp.bfloat16)


def attend_near_kernel(
    places, rotated, w_out, seg_row, mixed, log_sums, out_own, out_beside, keys, values
):
    blocks = rotated.shape[0] // BLOCK
    _, low, _ = lane_marks()
    for block in range(blocks):
        at = slice(block * BLOCK, (block + 1) * BLOCK)
        key_value_rows(rotated, rows_of(places, block), keys, values, at, low)
    attend_side(0, places, rotated, keys, values, seg_row, mixed, log_sums)
    out_beside[...] = nn(mixed[BLOCK:], w_out[...]).astype(jnp.bfloat16)
    out_own[...] = nn(mixed[:BLOCK], w_out[...]).astype(jnp.bfloat16)


def attend_back_kernel(
    places, rotated, near_logs, far_logs, cosine, sine, seg_row, w_out, weight,
    from_own, from_beside, from_across, from_diagonal,
    grads, back_own, back_beside, back_across, back_diagonal,
    keys, values, key_sum, value_sum, grad_mixed, seg_col,
):
    length = rotated.shape[0]
    width = grad_mixed.shape[1]
    blocks = length // BLOCK
    _, low, first = lane_marks()
    for piece, source in enumerate((from_own, from_beside, from_across, from_diagonal)):
        grad_mixed[piece * BLOCK : (piece + 1) * BLOCK] = nt(source[...], w_out[...]).astype(
            jnp.bfloat16
        )
    key_sum[...] = jnp.zeros_like(key_sum)
    value_sum[...] = jnp.zeros_like(value_sum)
    for block in range(blocks):
        at = slice(block * BLOCK, (block + 1) * BLOCK)
        key_value_rows(rotated, rows_of(places, block), keys, values, at, low)
        seg_col[at] = segment_column(seg_row, at)
    for block in range(blocks):
        rows = rows_of(places, block)
        at = slice(block * BLOCK, (block + 1) * BLOCK)
        is_near = places[blocks] == block % 2
        begin = max(0, block - 2) * BLOCK
        span = slice(begin, (block + 1) * BLOCK)
        count = (block + 1) * BLOCK - begin
        key_at = begin + lax.broadcasted_iota(jnp.int32, (count, BLOCK), 0)
        query_at = block * BLOCK + lax.broadcasted_iota(jnp.int32, (count, BLOCK), 1)
        allowed = (seg_col[span, :1] == seg_row[:, at]) & (key_at <= query_at)
        bias = jnp.where(allowed, 0.0, MASKED_SCORE)
        key_span = keys[span]
        value_span = values[span]

        def one_pair(number, carry):
            columns = pl.ds(pl.multiple_of(number * TILE, TILE), TILE)
            query = rotated[rows, columns]
            grad = grad_mixed[rows, columns]
            results = []
            for half in range(2):
                side = low if half == 0 else ~low
                chosen = jnp.where(side, query, jnp.zeros_like(query))
                chosen_grad = jnp.where(side, grad, jnp.zeros_like(grad))
                head = pl.ds(2 * number + half, 1)
                logs = jnp.where(is_near, near_logs[head, at], far_logs[head, at])
                probs = jnp.exp(nt(key_span, chosen) + bias - logs)
                grad_probs = nt(value_span, chosen_grad)
                inner = jnp.sum(probs * grad_probs, axis=0, keepdims=True)
                grad_scores = (probs * (grad_probs - inner)).astype(jnp.bfloat16)
                value_sum[span] += nn(probs.astype(jnp.bfloat16), chosen_grad)
                key_sum[span] += nn(grad_scores, chosen)
                results.append(tn(grad_scores, key_span))
            grad_query = jnp.where(low, results[0], results[1]) * HD ** (-0.5)
            grads[rows, columns] = turn_by(grad_query, cosine[at], -sine[at], first).astype(
                jnp.bfloat16
            )
            return carry

        lax.fori_loop(0, width // TILE, one_pair, 0)
    for block in range(blocks):
        rows = rows_of(places, block)
        at = slice(block * BLOCK, (block + 1) * BLOCK)
        grad_key = key_sum[at]
        grad_key = turn_by(grad_key + pltpu.roll(grad_key, HD, 1), cosine[at], -sine[at], first)
        grad_value = value_sum[at]
        grad_value = grad_value + pltpu.roll(grad_value, HD, 1)
        grads[rows, width:] = jnp.where(low, grad_key, grad_value).astype(jnp.bfloat16)
    for piece, target in enumerate((back_own, back_beside, back_across, back_diagonal)):
        grad_rows = grads[piece * BLOCK : (piece + 1) * BLOCK]
        target[...] = nt(grad_rows, weight[...]).astype(jnp.bfloat16)


SMEM = pl.BlockSpec(memory_space=pltpu.SMEM)
VMEM = pl.BlockSpec(memory_space=pltpu.VMEM)


ANY = pl.BlockSpec(memory_space=pl.ANY)
SCALE = 1000


def cost(flops, moved):
    return pl.CostEstimate(
        flops=int(flops) // SCALE, bytes_accessed=int(moved) // SCALE, transcendentals=0
    )


def attend_far(places, near, across, diagonal, weight, w_out, cosine, sine, seg_row):
    length, total = 2 * near.shape[0], near.shape[1]
    width = total - TILE
    depth = w_out.shape[1]
    block = jax.ShapeDtypeStruct((BLOCK, depth), jnp.bfloat16)
    return pl.pallas_call(
        attend_far_kernel,
        out_shape=(
            jax.ShapeDtypeStruct((length // 2, width), jnp.bfloat16),
            jax.ShapeDtypeStruct((length, total), jnp.bfloat16),
            jax.ShapeDtypeStruct((width // HD, length), jnp.float32),
            block,
            block,
        ),
        in_specs=[SMEM] + [VMEM] * 8,
        out_specs=(VMEM,) * 5,
        scratch_shapes=[pltpu.VMEM((length, TILE), jnp.bfloat16)] * 2,
        compiler_params=pltpu.CompilerParams(vmem_limit_bytes=48 << 20),
        cost_estimate=cost(14 << 30, 12 << 20),
        name="attend_far",
    )(places, near, across, diagonal, weight, w_out, cosine, sine, seg_row)


def attend_near(places, rotated, w_out, seg_row):
    length, total = rotated.shape
    width = total - TILE
    depth = w_out.shape[1]
    block = jax.ShapeDtypeStruct((BLOCK, depth), jnp.bfloat16)
    return pl.pallas_call(
        attend_near_kernel,
        out_shape=(
            jax.ShapeDtypeStruct((length // 2, width), jnp.bfloat16),
            jax.ShapeDtypeStruct((width // HD, length), jnp.float32),
            block,
            block,
        ),
        in_specs=[SMEM] + [VMEM] * 3,
        out_specs=(VMEM,) * 4,
        scratch_shapes=[pltpu.VMEM((length, TILE), jnp.bfloat16)] * 2,
        compiler_params=pltpu.CompilerParams(vmem_limit_bytes=48 << 20),
        cost_estimate=cost(10 << 30, 8 << 20),
        name="attend_near",
    )(places, rotated, w_out, seg_row)


def attend_back(
    places, rotated, near_logs, far_logs, cosine, sine, seg_row, w_out, weight, pieces
):
    length, total = rotated.shape
    return pl.pallas_call(
        attend_back_kernel,
        out_shape=(jax.ShapeDtypeStruct((length, total), jnp.bfloat16),)
        + (jax.ShapeDtypeStruct(pieces[0].shape, jnp.bfloat16),) * 4,
        in_specs=[SMEM] + [VMEM] * 12,
        out_specs=(VMEM,) * 5,
        scratch_shapes=[pltpu.VMEM((length, TILE), jnp.bfloat16)] * 2
        + [pltpu.VMEM((length, TILE), jnp.float32)] * 2
        + [
            pltpu.VMEM((length, total - TILE), jnp.bfloat16),
            pltpu.VMEM((length, TILE), jnp.int32),
        ],
        compiler_params=pltpu.CompilerParams(vmem_limit_bytes=52 << 20),
        cost_estimate=cost(32 << 30, 16 << 20),
        name="attend_back",
    )(
        places, rotated, near_logs, far_logs, cosine, sine, seg_row, w_out, weight, *pieces
    )


def terms_kernel(units, one, two, three, four, right, *outs):
    left = jnp.concatenate([one[...], two[...], three[...], four[...]], axis=0)
    total = tn(left, right[...]).astype(jnp.bfloat16)
    if len(outs) == 1:
        outs[0][0] = total
        return
    for number, out in enumerate(outs):

        @pl.when(pl.program_id(0) // 2 == number)
        def _(out=out):
            out[0] = total


def weight_terms(pieces, right, units, outs):
    count = pieces[0].shape[0]
    rows, width = right.shape
    blocks = units.shape[0]
    each = blocks // outs
    shape = jax.ShapeDtypeStruct((each, BLOCK, width), jnp.bfloat16)
    specs = [
        pl.BlockSpec(
            (1, BLOCK, width),
            lambda i, units, number=number: (jnp.clip(i - number * each, 0, each - 1), 0, 0),
        )
        for number in range(outs)
    ]
    return pl.pallas_call(
        terms_kernel,
        grid_spec=pltpu.PrefetchScalarGridSpec(
            num_scalar_prefetch=1,
            grid=(blocks,),
            in_specs=[pl.BlockSpec((count, BLOCK), lambda i, units: (0, units[i]))] * 4
            + [pl.BlockSpec((rows, width), lambda i, units: (0, 0))],
            out_specs=specs,
        ),
        out_shape=[shape] * outs,
        compiler_params=pltpu.CompilerParams(vmem_limit_bytes=60 << 20),
        cost_estimate=cost(
            2 * blocks * BLOCK * rows * width,
            2 * (blocks * BLOCK * (rows + 2 * width) + rows * width),
        ),
        name="weight_terms",
    )(units, *pieces, right)


def exchange(values, dp, distance):
    return lax.ppermute(values, "dp", [(device, device ^ distance) for device in range(dp)])


def numbered(bits, values, free):
    fixed = jnp.zeros((), jnp.int32)
    for bit, value in zip(bits, values):
        fixed = fixed + bit * value
    numbers = [fixed]
    for bit in free:
        numbers = [number + add for number in numbers for add in (0, bit)]
    return jnp.stack(numbers).astype(jnp.int32)


class DpSum:
    def __init__(self, pieces, right, order, dp):
        self.pieces, self.right, self.order, self.dp = pieces, right, order, dp
        unit = lax.axis_index("dp") // (dp // 8)
        self.mine = [(unit // bit) % 2 for bit in order]

    def terms(self, one, outs):
        _, two, three = self.mine
        units = [
            sum(bit * value for bit, value in zip(self.order, (one, second, third)))
            for second in (1 - two, two)
            for third in (1 - three, three)
        ]
        units = jnp.stack(units).astype(jnp.int32)
        return weight_terms(self.pieces, self.right, units, outs)

    def exchange(self, values, step):
        return exchange(values, self.dp, self.order[step] * (self.dp // 8))

    def first(self, outs=2):
        return self.terms(1 - self.mine[0], outs)

    def keep(self):
        return self.terms(self.mine[0], 1)[0]

    def second(self, keep, early):
        return add_up([keep[:2], early[:2]]).astype(jnp.bfloat16)

    def third(self, keep, late, middle):
        at = late.shape[0] - 2
        return add_up([keep[2], late[at], middle[0]]).astype(jnp.bfloat16)

    def finish(self, keep, late, middle, end, turned=False):
        at = late.shape[0] - 1
        total = add_up([keep[3], late[at], middle[1], end])
        index, left = lax.axis_index("dp"), self.dp // 8
        while left > 1:
            left //= 2
            bit = (index // left) % 2
            parts = total.reshape(2, total.shape[0] // 2, total.shape[1])
            there = exchange(pick(parts, 1 - bit, 0).astype(jnp.bfloat16), self.dp, left)
            total = pick(parts, bit, 0) + there.astype(jnp.float32)
        return total.T if turned else total


def sync(*values):
    return lax.optimization_barrier(values)


def column_tiles(width, most=256):
    return [(at, min(most, width - at)) for at in range(0, width, most)]


def feed_kernel(
    one, two, cot_one, cot_two, w_gate, w_up, w_down, *rest
):
    hidden, grad_gate, grad_up, rows, cots, gate, up, down, gates, ups, sems = rest[-11:]
    count = one.shape[0]
    moves = [
        pltpu.make_async_copy(source, target, sems.at[number])
        for number, (source, target) in enumerate(
            (
                (one, rows.at[:count]),
                (two, rows.at[count:]),
                (w_gate, gate),
                (w_up, up),
                (cot_one, cots.at[:count]),
                (cot_two, cots.at[count:]),
                (w_down, down),
            )
        )
    ]
    for move in moves:
        move.start()
    for move in moves[:3]:
        move.wait()
    tiles = column_tiles(gate.shape[1])
    for at, size in tiles:
        gates[:, at : at + size] = nn(rows[...], gate[:, at : at + size])
    moves[3].wait()
    for at, size in tiles:
        ups[:, at : at + size] = nn(rows[...], up[:, at : at + size])
    for move in moves[4:]:
        move.wait()
    for at, size in tiles:
        span = slice(at, at + size)
        grad_hidden = nt(cots[...], down[span])
        gate_pre = gates[:, span]
        up_pre = ups[:, span]
        sigmoid = jax.nn.sigmoid(gate_pre)
        silu = gate_pre * sigmoid
        hidden[:, span] = (silu * up_pre).astype(jnp.bfloat16)
        slope = sigmoid + silu * (1.0 - sigmoid)
        grad_gate[:, span] = (grad_hidden * up_pre * slope).astype(jnp.bfloat16)
        grad_up[:, span] = (grad_hidden * silu).astype(jnp.bfloat16)


def feed(side, pair, cots, w_gate, w_up, w_down, held=()):
    count, depth = pair[0].shape
    width = w_gate.shape[1]
    return pl.pallas_call(
        feed_kernel,
        grid=(1,),
        out_shape=(jax.ShapeDtypeStruct((4 * count, width), jnp.bfloat16),) * 3,
        in_specs=[ANY] * (7 + len(held)),
        out_specs=(pl.BlockSpec((2 * count, width), lambda i: (side, 0)),) * 3,
        scratch_shapes=[pltpu.VMEM((2 * count, depth), jnp.bfloat16)] * 2
        + [pltpu.VMEM((depth, width), jnp.bfloat16)] * 2
        + [
            pltpu.VMEM((width, depth), jnp.bfloat16),
            pltpu.VMEM((2 * count, width), jnp.float32),
            pltpu.VMEM((2 * count, width), jnp.float32),
            pltpu.SemaphoreType.DMA((7,)),
        ],
        input_output_aliases={7 + i: i for i in range(len(held))},
        compiler_params=pltpu.CompilerParams(vmem_limit_bytes=50 << 20),
        cost_estimate=cost(12 * count * depth * width, 28 << 20),
        name="feed",
    )(*pair, *cots, w_gate, w_up, w_down, *held)


def feed_back_kernel(grad_gate, grad_up, w_gate, w_up, one, two):
    total = nt(grad_gate[...], w_gate[...]) + nt(grad_up[...], w_up[...])
    total = total.astype(jnp.bfloat16)
    one[...] = total[: one.shape[0]]
    two[...] = total[one.shape[0] :]


def feed_back(side, grad_gate, grad_up, w_gate, w_up):
    count = grad_gate.shape[0] // 4
    depth, width = w_gate.shape
    size = 256
    rows = pl.BlockSpec((2 * count, width), lambda i: (side, 0))
    weights = pl.BlockSpec((size, width), lambda i: (i, 0))
    outs = pl.BlockSpec((count, size), lambda i: (0, i))
    return pl.pallas_call(
        feed_back_kernel,
        grid=(depth // size,),
        out_shape=(jax.ShapeDtypeStruct((count, depth), jnp.bfloat16),) * 2,
        in_specs=[rows, rows, weights, weights],
        out_specs=(outs, outs),
        compiler_params=pltpu.CompilerParams(vmem_limit_bytes=60 << 20),
        cost_estimate=cost(8 * count * depth * width, 18 << 20),
        name="feed_back",
    )(grad_gate, grad_up, w_gate, w_up)


def feed_down_kernel(hidden, w_down, *outs):
    total = nn(hidden[...], w_down[...]).astype(jnp.bfloat16)
    for number, out in enumerate(outs):
        out[...] = total[number * out.shape[0] : (number + 1) * out.shape[0]]


def feed_down(hidden, w_down):
    count = hidden.shape[0] // 4
    width, depth = w_down.shape
    size = 256
    return pl.pallas_call(
        feed_down_kernel,
        grid=(depth // size,),
        out_shape=(jax.ShapeDtypeStruct((count, depth), jnp.bfloat16),) * 4,
        in_specs=[
            pl.BlockSpec((4 * count, width), lambda i: (0, 0)),
            pl.BlockSpec((width, size), lambda i: (0, i)),
        ],
        out_specs=(pl.BlockSpec((count, size), lambda i: (0, i)),) * 4,
        compiler_params=pltpu.CompilerParams(vmem_limit_bytes=60 << 20),
        cost_estimate=cost(8 * count * depth * width, 20 << 20),
        name="feed_down",
    )(hidden, w_down)


def to_core(values):
    return lax.ppermute(values, "row", SWAP)


def to_chip(values):
    return lax.ppermute(values, "col", SWAP)


def gather_blocks(own):
    across = to_chip(own)
    return own, to_core(own), across, to_core(across)


def scatter_far(across, diagonal):
    return to_chip((across + to_core(diagonal)).astype(jnp.bfloat16))


def pick(values, index, axis):
    return lax.dynamic_index_in_dim(values, index, axis, keepdims=False)


def add_up(terms):
    total = terms[0].astype(jnp.float32)
    for term in terms[1:]:
        total = total + term.astype(jnp.float32)
    return total


def norm_back(grad_normed, unit_rows, inverse, gain):
    scaled = grad_normed * gain
    inner = jnp.mean(scaled * unit_rows, axis=-1, keepdims=True)
    return inverse * (scaled - unit_rows * inner), jnp.sum(grad_normed * unit_rows, axis=0)


def local_for(dp):
    def local(
        tokens,
        segments,
        attn_gain,
        w_query,
        w_key,
        w_value,
        w_out,
        ffn_gain,
        w_gate,
        w_up,
        w_down,
        out_cotangent,
    ):
        query_width = w_query.shape[1]
        kv_width = w_key.shape[1]
        length = segments.shape[1]
        row, col = lax.axis_index("row"), lax.axis_index("col")
        places = [
            (((block // 2) ^ row) + 2 * ((block % 2) ^ col)) * (length // 4) for block in range(4)
        ]
        places = jnp.stack(places + [col]).astype(jnp.int32)

        inputs = tokens.astype(jnp.float32)
        inverse_one = lax.rsqrt(jnp.mean(inputs * inputs, axis=-1, keepdims=True) + EPSILON)
        unit_one = inputs * inverse_one
        normed_one = (unit_one * attn_gain).astype(jnp.bfloat16)
        across_one = to_chip(normed_one)
        beside_one = to_core(normed_one)
        qkv_weight = jnp.concatenate([w_query, w_key, w_value], axis=1)
        cosine, sine = rope_tables(positions(segments).reshape(length))
        seg_row = segments.reshape(1, length)
        near = nn(jnp.concatenate([normed_one, beside_one], axis=0), qkv_weight)
        across_one, near, cot, cosine, sine = sync(
            across_one, near, out_cotangent, cosine, sine
        )
        across_cot = to_chip(cot)
        beside_cot = to_core(cot)
        diagonal_one = to_core(across_one)
        blocks_one = (normed_one, beside_one, across_one, diagonal_one)
        far_mixed, rotated, far_logs, out_across, out_diagonal = attend_far(
            places, near, across_one, diagonal_one, qkv_weight, w_out, cosine, sine, seg_row
        )
        out_across, out_diagonal, rotated, across_cot, beside_cot = sync(
            out_across, out_diagonal, rotated, across_cot, beside_cot
        )
        out_diagonal = to_core(out_diagonal)
        diagonal_cot = to_core(across_cot)
        out_across, out_diagonal, rotated, diagonal_cot = sync(
            out_across, out_diagonal, rotated, diagonal_cot
        )
        cots = (out_cotangent, beside_cot, across_cot, diagonal_cot)
        far_out = to_chip((out_across + out_diagonal).astype(jnp.bfloat16))
        near_mixed, near_logs, out_own, out_beside = attend_near(
            places, rotated, w_out, seg_row
        )
        far_out, out_own, out_beside = sync(far_out, out_own, out_beside)
        out_beside = to_core(out_beside)
        middle = add_up([inputs, out_own, out_beside, far_out])
        inverse_two = lax.rsqrt(jnp.mean(middle * middle, axis=-1, keepdims=True) + EPSILON)
        unit_two = middle * inverse_two
        normed_two = (unit_two * ffn_gain).astype(jnp.bfloat16)
        across_two = to_chip(normed_two)
        beside_two = to_core(normed_two)
        mixed = jnp.concatenate([near_mixed, far_mixed], axis=0)
        parts = feed(0, (normed_two, beside_two), cots[:2], w_gate, w_up, w_down)
        back_own, back_beside = feed_back(0, parts[1], parts[2], w_gate, w_up)
        parts, across_two, mixed, back_own, back_beside = sync(
            parts, across_two, mixed, back_own, back_beside
        )
        diagonal_two = to_core(across_two)
        back_beside = to_core(back_beside)
        blocks_two = (normed_two, beside_two, across_two, diagonal_two)
        hidden, grad_gate, grad_up = feed(
            1, blocks_two[2:], cots[2:], w_gate, w_up, w_down, parts
        )

        gate = DpSum(blocks_two, grad_gate, (1, 2, 4), dp)
        up = DpSum(blocks_two, grad_up, (1, 2, 4), dp)
        down = DpSum(cots, hidden, (2, 1, 4), dp)
        gate_first, down_first = gate.first(), down.first()
        gate_first, down_first, grad_gate, grad_up, hidden, back_beside = sync(
            gate_first, down_first, grad_gate, grad_up, hidden, back_beside
        )

        gate_early = gate.exchange(gate_first[0], 0)
        down_early = down.exchange(down_first[0], 0)
        far_across, far_diagonal = feed_back(1, grad_gate, grad_up, w_gate, w_up)
        far_diagonal = to_core(far_diagonal)
        gate_keep, down_keep = gate.keep(), down.keep()
        (
            gate_early, down_early, far_across, far_diagonal, gate_keep, down_keep, hidden, gate_late,
            down_late, grad_up,
        ) = sync(
            gate_early, down_early, far_across, far_diagonal, gate_keep, down_keep, hidden,
            gate_first[1], down_first[1], grad_up,
        )

        gate_late = gate.exchange(gate_late, 0)
        down_late = down.exchange(down_late, 0)
        back_far = to_chip((far_across + far_diagonal).astype(jnp.bfloat16))
        gate_middle = gate.second(gate_keep, gate_early)
        up.right = grad_up
        up_first = up.first()
        down_own, down_beside, down_across, down_diagonal = feed_down(hidden, w_down)
        (
            gate_late, down_late, back_far, gate_middle, up_first, down_own, down_beside, down_across,
            down_diagonal,
        ) = sync(
            gate_late, down_late, back_far, gate_middle, up_first, down_own, down_beside, down_across,
            down_diagonal,
        )

        up_early = up.exchange(up_first[0], 0)
        gate_middle = gate.exchange(gate_middle, 1)
        grad_normed_two = add_up([back_own, back_beside, back_far])
        grad_middle_norm, gain_two_grad = norm_back(
            grad_normed_two, unit_two, inverse_two, ffn_gain
        )
        grad_middle = out_cotangent.astype(jnp.float32) + grad_middle_norm
        from_own = grad_middle.astype(jnp.bfloat16)
        from_across = to_chip(from_own)
        from_beside = to_core(from_own)
        up_keep = up.keep()
        down_middle = down.second(down_keep, down_early)
        (
            up_early, gate_middle, from_across, from_beside, down_middle, up_keep, down_diagonal, up_late,
        ) = sync(
            up_early, gate_middle, from_across, from_beside, down_middle, up_keep, down_diagonal,
            up_first[1],
        )

        from_diagonal = to_core(from_across)
        down_diagonal = to_core(down_diagonal)
        up_middle = up.second(up_keep, up_early)
        gate_end = gate.third(gate_keep, gate_late, gate_middle)
        from_diagonal, up_middle, gate_end, up_late, down_diagonal = sync(
            from_diagonal, up_middle, gate_end, up_late, down_diagonal
        )

        grad_attn = (from_own, from_beside, from_across, from_diagonal)
        up_late = up.exchange(up_late, 0)
        up_middle = up.exchange(up_middle, 1)
        gate_end = gate.exchange(gate_end, 2)
        down_far = to_chip((down_across + down_diagonal).astype(jnp.bfloat16))
        out = DpSum(grad_attn, mixed, (1, 2, 4), dp)
        out_first = out.exchange(out.first(1)[0], 0)
        out_keep = out.keep()
        grad_qkv, *backs = attend_back(
            places, rotated, near_logs, far_logs, cosine, sine, seg_row, w_out, qkv_weight, grad_attn
        )
        (
            up_late, up_middle, gate_end, out_first, grad_qkv, backs, down_middle, down_far, out_keep,
        ) = sync(
            up_late, up_middle, gate_end, out_first, grad_qkv, backs, down_middle, down_far, out_keep
        )

        qkv = DpSum(blocks_one, grad_qkv, (1, 2, 4), dp)
        down_middle = down.exchange(down_middle, 1)
        up_end = up.exchange(up.third(up_keep, up_late, up_middle), 2)
        out_middle = out.exchange(out.second(out_keep, out_first), 1)
        one_diagonal = to_core(backs[3])
        one_beside = to_core(backs[1])
        gain_one_grad = sum(
            jnp.sum(part.astype(jnp.float32) * block.astype(jnp.float32), axis=0)
            for part, block in zip(backs, blocks_one)
        )
        gains = jnp.stack([gain_one_grad / attn_gain, gain_two_grad])
        gate_grad = gate.finish(gate_keep, gate_late, gate_middle, gate_end)
        qkv_first, qkv_keep = qkv.first(1)[0], qkv.keep()
        (
            down_middle, up_end, out_middle, one_diagonal, one_beside, gate_grad, qkv_first, qkv_keep,
            gains,
        ) = sync(
            down_middle, up_end, out_middle, one_diagonal, one_beside, gate_grad, qkv_first, qkv_keep,
            gains,
        )

        qkv_first = qkv.exchange(qkv_first, 0)
        down_end = down.exchange(down.third(down_keep, down_late, down_middle), 2)
        one_far = to_chip((backs[2] + one_diagonal).astype(jnp.bfloat16))
        gains = gains + to_core(gains)
        down_beside = to_core(down_beside)
        up_grad = up.finish(up_keep, up_late, up_middle, up_end)
        qkv_first, down_end, one_far, up_grad, gains, down_beside = sync(
            qkv_first, down_end, one_far, up_grad, gains, down_beside
        )

        qkv_middle = qkv.exchange(qkv.second(qkv_keep, qkv_first), 1)
        out_end = out.exchange(out.third(out_keep, out_first, out_middle), 2)
        gains = gains + to_chip(gains)
        output = add_up([middle, down_own, down_beside, down_far]).astype(jnp.bfloat16)
        down_grad = down.finish(down_keep, down_late, down_middle, down_end, True)
        grad_normed_one = add_up([backs[0], one_beside, one_far])
        scaled = grad_normed_one * attn_gain
        mean = jnp.mean(scaled * unit_one, axis=-1, keepdims=True)
        input_grad = grad_middle + inverse_one * (scaled - unit_one * mean)
        qkv_middle, out_end, output, down_grad, input_grad, gains = sync(
            qkv_middle, out_end, output, down_grad, input_grad, gains
        )

        qkv_end = qkv.exchange(qkv.third(qkv_keep, qkv_first, qkv_middle), 2)
        step = 1
        while step < dp:
            gains = gains + exchange(gains, dp, step)
            step *= 2
        out_grad = out.finish(out_keep, out_first, out_middle, out_end, True)
        qkv_end, out_grad, gains = sync(qkv_end, out_grad, gains)
        qkv_grad = qkv.finish(qkv_keep, qkv_first, qkv_middle, qkv_end)
        key_end = query_width + kv_width
        return (
            output,
            input_grad,
            gains[0],
            qkv_grad[:, :query_width],
            qkv_grad[:, query_width:key_end],
            qkv_grad[:, key_end:],
            out_grad,
            gains[1],
            gate_grad,
            up_grad,
            down_grad,
        )

    return local


def solution(mesh):
    rows = P(("dp", "row", "col"), None)
    columns = P(None, ("row", "col"))
    placed = (
        rows,
        P("dp", None),
        P(),
        columns,
        columns,
        columns,
        P(("row", "col"), None),
        P(),
        columns,
        columns,
        P(("row", "col"), None),
        rows,
    )
    summed = P("dp", ("row", "col"))
    turned = P(("row", "col"), "dp")
    return jax.shard_map(
        local_for(mesh.shape["dp"]),
        mesh=mesh,
        in_specs=placed,
        out_specs=(rows, rows, P(), summed, summed, summed, turned, P(), summed, summed, turned),
        check_vma=False,
    )
```

```python
import jax
import jax.numpy as jnp
from jax import lax
from jax.experimental import pallas as pl
from jax.experimental.pallas import tpu as pltpu
from jax.sharding import PartitionSpec as P

HD = 64
EPSILON = 1e-05
MASKED_SCORE = -1e30
BLOCK = 256
TILE = 128
SWAP = ((0, 1), (1, 0))


def positions(segment_ids):
    indices = jnp.arange(segment_ids.shape[-1], dtype=jnp.int32)
    previous = jnp.concatenate([segment_ids[..., :1] - 1, segment_ids[..., :-1]], axis=-1)
    starts = jnp.where(segment_ids != previous, indices, 0)
    return indices - lax.cummax(starts, axis=segment_ids.ndim - 1)


def rope_tables(position):
    exponent = jnp.arange(HD // 2, dtype=jnp.float32) * (-2.0 / HD)
    angles = position.astype(jnp.float32)[:, None] * (10000.0**exponent)[None, :]
    cosine, sine = jnp.cos(angles), jnp.sin(angles)
    return (
        jnp.concatenate([cosine] * 4, axis=1),
        jnp.concatenate([-sine, sine, -sine, sine], axis=1),
    )


def nt(left, right):
    return lax.dot_general(
        left, right, (((1,), (1,)), ((), ())), preferred_element_type=jnp.float32
    )


def nn(left, right):
    return lax.dot_general(
        left, right, (((1,), (0,)), ((), ())), preferred_element_type=jnp.float32
    )


def tn(left, right):
    return lax.dot_general(
        left, right, (((0,), (0,)), ((), ())), preferred_element_type=jnp.float32
    )


def lane_marks():
    lane = lax.broadcasted_iota(jnp.int32, (BLOCK, TILE), 1)
    return lane, lane < HD, lane % HD < HD // 2


def turn_by(values, cosine, sine, first):
    turned = jnp.where(
        first, pltpu.roll(values, TILE - HD // 2, 1), pltpu.roll(values, HD // 2, 1)
    )
    return values * cosine + turned * sine


def rows_of(places, block):
    return pl.ds(pl.multiple_of(places[block], BLOCK), BLOCK)


def segment_column(seg_row, at):
    return jnp.broadcast_to(seg_row[:, at], (TILE, BLOCK)).T


def attend_block(block, places, rotated, keys, values, seg_row, mixed, target, log_sums):
    width = mixed.shape[1]
    lane, low, _ = lane_marks()
    rows = rows_of(places, block)
    at = slice(block * BLOCK, (block + 1) * BLOCK)
    begin = max(0, block - 2) * BLOCK
    span = slice(begin, (block + 1) * BLOCK)
    count = (block + 1) * BLOCK - begin
    key_at = begin + lax.broadcasted_iota(jnp.int32, (BLOCK, count), 1)
    query_at = block * BLOCK + lax.broadcasted_iota(jnp.int32, (BLOCK, count), 0)
    seg_col = segment_column(seg_row, at)[:, :1]
    allowed = (seg_col == seg_row[:, span]) & (key_at <= query_at)
    bias = jnp.where(allowed, 0.0, MASKED_SCORE)
    key_span = keys[span]
    value_span = values[span]

    def one_pair(number, logs):
        columns = pl.ds(pl.multiple_of(number * TILE, TILE), TILE)
        query = rotated[rows, columns]
        results = []
        for half in range(2):
            chosen = jnp.where(low if half == 0 else ~low, query, jnp.zeros_like(query))
            scores = nt(chosen, key_span) + bias
            largest = jnp.max(scores, axis=1, keepdims=True)
            shifted = jnp.exp(scores - largest)
            total = jnp.sum(shifted, axis=1, keepdims=True)
            results.append(nn(shifted.astype(jnp.bfloat16), value_span) * (1.0 / total))
            logs = jnp.where(lane == 2 * number + half, largest + jnp.log(total), logs)
        mixed[target, columns] = jnp.where(low, results[0], results[1]).astype(jnp.bfloat16)
        return logs

    logs = lax.fori_loop(0, width // TILE, one_pair, jnp.zeros((BLOCK, TILE), jnp.float32))
    log_sums[:, at] = logs.T[: log_sums.shape[0]]


def key_value_rows(rotated, rows, keys, values, at, low):
    width = rotated.shape[1] - TILE
    pair = rotated[rows, width:].astype(jnp.float32)
    swapped = pltpu.roll(pair, HD, 1)
    keys[at] = jnp.where(low, pair, swapped).astype(jnp.bfloat16)
    values[at] = jnp.where(low, swapped, pair).astype(jnp.bfloat16)


def attend_side(side, places, rotated, keys, values, seg_row, mixed, log_sums):
    blocks = rotated.shape[0] // BLOCK
    for parity in range(2):

        @pl.when((places[blocks] ^ side) == parity)
        def _():
            for block in range(parity, blocks, 2):
                start = places[block] - side * 2 * BLOCK
                target = pl.ds(pl.multiple_of(start, BLOCK), BLOCK)
                attend_block(
                    block, places, rotated, keys, values, seg_row, mixed, target, log_sums
                )


def attend_far_kernel(
    places, near, across, diagonal, weight, w_out, cosine, sine, seg_row,
    mixed, rotated, log_sums, out_across, out_diagonal, keys, values,
):
    length, total = rotated.shape
    width = total - TILE
    blocks = length // BLOCK
    _, low, first = lane_marks()
    for block in range(blocks):
        rows = rows_of(places, block)
        at = slice(block * BLOCK, (block + 1) * BLOCK)

        def turn_all(proj):
            for start in range(0, width, TILE):
                query = turn_by(proj[:, start : start + TILE], cosine[at], sine[at], first)
                rotated[rows, start : start + TILE] = (query * HD ** (-0.5)).astype(jnp.bfloat16)
            pair = proj[:, width:]
            turned = jnp.where(low, turn_by(pair, cosine[at], sine[at], first), pair)
            rotated[rows, width:] = turned.astype(jnp.bfloat16)

        for piece, source in ((0, None), (1, None), (2, across), (3, diagonal)):

            @pl.when(places[block] == piece * BLOCK)
            def _(piece=piece, source=source):
                if source is None:
                    turn_all(near[piece * BLOCK : (piece + 1) * BLOCK])
                else:
                    turn_all(nn(source[...], weight[...]))

        key_value_rows(rotated, rows, keys, values, at, low)
    attend_side(1, places, rotated, keys, values, seg_row, mixed, log_sums)
    out_diagonal[...] = nn(mixed[BLOCK:], w_out[...]).astype(jnp.bfloat16)
    out_across[...] = nn(mixed[:BLOCK], w_out[...]).astype(jnp.bfloat16)


def attend_near_kernel(
    places, rotated, w_out, seg_row, mixed, log_sums, out_own, out_beside, keys, values
):
    blocks = rotated.shape[0] // BLOCK
    _, low, _ = lane_marks()
    for block in range(blocks):
        at = slice(block * BLOCK, (block + 1) * BLOCK)
        key_value_rows(rotated, rows_of(places, block), keys, values, at, low)
    attend_side(0, places, rotated, keys, values, seg_row, mixed, log_sums)
    out_beside[...] = nn(mixed[BLOCK:], w_out[...]).astype(jnp.bfloat16)
    out_own[...] = nn(mixed[:BLOCK], w_out[...]).astype(jnp.bfloat16)


def attend_back_kernel(
    places, rotated, near_logs, far_logs, cosine, sine, seg_row, w_out, weight,
    from_own, from_beside, from_across, from_diagonal,
    grads, back_own, back_across, back_others,
    keys, values, key_sum, value_sum, grad_mixed, seg_col,
):
    length = rotated.shape[0]
    width = grad_mixed.shape[1]
    blocks = length // BLOCK
    _, low, first = lane_marks()
    for piece, source in enumerate((from_own, from_beside, from_across, from_diagonal)):
        grad_mixed[piece * BLOCK : (piece + 1) * BLOCK] = nt(source[...], w_out[...]).astype(
            jnp.bfloat16
        )
    key_sum[...] = jnp.zeros_like(key_sum)
    value_sum[...] = jnp.zeros_like(value_sum)
    for block in range(blocks):
        at = slice(block * BLOCK, (block + 1) * BLOCK)
        key_value_rows(rotated, rows_of(places, block), keys, values, at, low)
        seg_col[at] = segment_column(seg_row, at)
    for block in range(blocks):
        rows = rows_of(places, block)
        at = slice(block * BLOCK, (block + 1) * BLOCK)
        is_near = places[blocks] == block % 2
        begin = max(0, block - 2) * BLOCK
        span = slice(begin, (block + 1) * BLOCK)
        count = (block + 1) * BLOCK - begin
        key_at = begin + lax.broadcasted_iota(jnp.int32, (count, BLOCK), 0)
        query_at = block * BLOCK + lax.broadcasted_iota(jnp.int32, (count, BLOCK), 1)
        allowed = (seg_col[span, :1] == seg_row[:, at]) & (key_at <= query_at)
        bias = jnp.where(allowed, 0.0, MASKED_SCORE)
        key_span = keys[span]
        value_span = values[span]

        def one_pair(number, carry):
            columns = pl.ds(pl.multiple_of(number * TILE, TILE), TILE)
            query = rotated[rows, columns]
            grad = grad_mixed[rows, columns]
            results = []
            for half in range(2):
                side = low if half == 0 else ~low
                chosen = jnp.where(side, query, jnp.zeros_like(query))
                chosen_grad = jnp.where(side, grad, jnp.zeros_like(grad))
                head = pl.ds(2 * number + half, 1)
                logs = jnp.where(is_near, near_logs[head, at], far_logs[head, at])
                probs = jnp.exp(nt(key_span, chosen) + bias - logs)
                grad_probs = nt(value_span, chosen_grad)
                inner = jnp.sum(probs * grad_probs, axis=0, keepdims=True)
                grad_scores = (probs * (grad_probs - inner)).astype(jnp.bfloat16)
                value_sum[span] += nn(probs.astype(jnp.bfloat16), chosen_grad)
                key_sum[span] += nn(grad_scores, chosen)
                results.append(tn(grad_scores, key_span))
            grad_query = jnp.where(low, results[0], results[1]) * HD ** (-0.5)
            grads[rows, columns] = turn_by(grad_query, cosine[at], -sine[at], first).astype(
                jnp.bfloat16
            )
            return carry

        lax.fori_loop(0, width // TILE, one_pair, 0)
    for block in range(blocks):
        rows = rows_of(places, block)
        at = slice(block * BLOCK, (block + 1) * BLOCK)
        grad_key = key_sum[at]
        grad_key = turn_by(grad_key + pltpu.roll(grad_key, HD, 1), cosine[at], -sine[at], first)
        grad_value = value_sum[at]
        grad_value = grad_value + pltpu.roll(grad_value, HD, 1)
        grads[rows, width:] = jnp.where(low, grad_key, grad_value).astype(jnp.bfloat16)
    targets = (back_own, back_others.at[:BLOCK], back_across, back_others.at[BLOCK:])
    for piece, target in enumerate(targets):
        grad_rows = grads[piece * BLOCK : (piece + 1) * BLOCK]
        target[...] = nt(grad_rows, weight[...]).astype(jnp.bfloat16)


SMEM = pl.BlockSpec(memory_space=pltpu.SMEM)
VMEM = pl.BlockSpec(memory_space=pltpu.VMEM)


ANY = pl.BlockSpec(memory_space=pl.ANY)
def params(limit):
    return pltpu.CompilerParams(vmem_limit_bytes=limit << 20)


def attend_far(places, near, across, diagonal, weight, w_out, cosine, sine, seg_row):
    length, total = 2 * near.shape[0], near.shape[1]
    width = total - TILE
    depth = w_out.shape[1]
    block = jax.ShapeDtypeStruct((BLOCK, depth), jnp.bfloat16)
    return pl.pallas_call(
        attend_far_kernel,
        out_shape=(
            jax.ShapeDtypeStruct((length // 2, width), jnp.bfloat16),
            jax.ShapeDtypeStruct((length, total), jnp.bfloat16),
            jax.ShapeDtypeStruct((width // HD, length), jnp.float32),
            block,
            block,
        ),
        in_specs=[SMEM] + [VMEM] * 8,
        out_specs=(VMEM,) * 5,
        scratch_shapes=[pltpu.VMEM((length, TILE), jnp.bfloat16)] * 2,
        compiler_params=params(48),
        name="attend_far",
    )(places, near, across, diagonal, weight, w_out, cosine, sine, seg_row)


def attend_near(places, rotated, w_out, seg_row):
    length, total = rotated.shape
    width = total - TILE
    depth = w_out.shape[1]
    block = jax.ShapeDtypeStruct((BLOCK, depth), jnp.bfloat16)
    return pl.pallas_call(
        attend_near_kernel,
        out_shape=(
            jax.ShapeDtypeStruct((length // 2, width), jnp.bfloat16),
            jax.ShapeDtypeStruct((width // HD, length), jnp.float32),
            block,
            block,
        ),
        in_specs=[SMEM] + [VMEM] * 3,
        out_specs=(VMEM,) * 4,
        scratch_shapes=[pltpu.VMEM((length, TILE), jnp.bfloat16)] * 2,
        compiler_params=params(48),
        name="attend_near",
    )(places, rotated, w_out, seg_row)


def attend_back(
    places, rotated, near_logs, far_logs, cosine, sine, seg_row, w_out, weight, pieces
):
    length, total = rotated.shape
    return pl.pallas_call(
        attend_back_kernel,
        out_shape=(jax.ShapeDtypeStruct((length, total), jnp.bfloat16),)
        + (jax.ShapeDtypeStruct(pieces[0].shape, jnp.bfloat16),) * 2
        + (jax.ShapeDtypeStruct((2 * BLOCK, pieces[0].shape[1]), jnp.bfloat16),),
        in_specs=[SMEM] + [VMEM] * 12,
        out_specs=(VMEM,) * 4,
        scratch_shapes=[pltpu.VMEM((length, TILE), jnp.bfloat16)] * 2
        + [pltpu.VMEM((length, TILE), jnp.float32)] * 2
        + [
            pltpu.VMEM((length, total - TILE), jnp.bfloat16),
            pltpu.VMEM((length, TILE), jnp.int32),
        ],
        compiler_params=params(52),
        name="attend_back",
    )(
        places, rotated, near_logs, far_logs, cosine, sine, seg_row, w_out, weight, *pieces
    )


def terms_kernel(starts, units, one, two, three, four, right, *outs):
    left = jnp.concatenate([one[...], two[...], three[...], four[...]], axis=0)
    total = tn(left, right[...]).astype(jnp.bfloat16)
    step = pl.program_id(0)
    for out, start, end in zip(outs, starts, starts[1:]):

        @pl.when((step >= start) & (step < end))
        def _(out=out):
            out[0] = total


def weight_terms(pieces, right, units, sizes):
    count = pieces[0].shape[0]
    rows, width = right.shape
    starts = [sum(sizes[:number]) for number in range(len(sizes) + 1)]
    return pl.pallas_call(
        lambda *refs: terms_kernel(starts, *refs),
        grid_spec=pltpu.PrefetchScalarGridSpec(
            num_scalar_prefetch=1,
            grid=(starts[-1],),
            in_specs=[pl.BlockSpec((count, BLOCK), lambda i, units: (0, units[i]))] * 4
            + [pl.BlockSpec((rows, width), lambda i, units: (0, 0))],
            out_specs=[
                pl.BlockSpec(
                    (1, BLOCK, width),
                    lambda i, units, start=start, size=size: (
                        jnp.clip(i - start, 0, size - 1),
                        0,
                        0,
                    ),
                )
                for start, size in zip(starts, sizes)
            ],
        ),
        out_shape=[jax.ShapeDtypeStruct((size, BLOCK, width), jnp.bfloat16) for size in sizes],
        compiler_params=params(60),
        name="weight_terms",
    )(units, *pieces, right)


def exchange(values, dp, distance):
    return lax.ppermute(values, "dp", [(device, device ^ distance) for device in range(dp)])


def numbered(bits, values, free):
    fixed = jnp.zeros((), jnp.int32)
    for bit, value in zip(bits, values):
        fixed = fixed + bit * value
    numbers = [fixed]
    for bit in free:
        numbers = [number + add for number in numbers for add in (0, bit)]
    return jnp.stack(numbers).astype(jnp.int32)


class DpSum:
    def __init__(self, pieces, right, order, dp):
        self.pieces, self.right, self.order, self.dp = pieces, right, order, dp
        unit = lax.axis_index("dp") // (dp // 8)
        self.mine = [(unit // bit) % 2 for bit in order]

    def units(self, one):
        _, two, three = self.mine
        return [
            sum(bit * value for bit, value in zip(self.order, (one, second, third)))
            for second in (1 - two, two)
            for third in (1 - three, three)
        ]

    def terms(self, units, *sizes):
        units = jnp.stack(units).astype(jnp.int32)
        return weight_terms(self.pieces, self.right, units, sizes)

    def early(self):
        return self.terms(self.units(1 - self.mine[0])[:2], 2)[0]

    def late(self):
        return self.terms(self.units(1 - self.mine[0])[2:], 2)[0]

    def whole(self):
        return self.terms(self.units(1 - self.mine[0]), 4)[0]

    def keep(self):
        return self.terms(self.units(self.mine[0]), 4)[0]

    def halves(self):
        return self.terms(self.units(1 - self.mine[0]), 2, 2)

    def whole_and_keep(self):
        return self.terms(self.units(1 - self.mine[0]) + self.units(self.mine[0]), 4, 4)

    def send(self, values, step):
        return exchange(values, self.dp, self.order[step] * (self.dp // 8))

    def second(self, keep, early):
        return add_up([keep[:2], early[:2]]).astype(jnp.bfloat16)

    def third(self, keep, late, middle):
        at = late.shape[0] - 2
        return add_up([keep[2], late[at], middle[0]]).astype(jnp.bfloat16)

    def finish(self, keep, late, middle, end, turned=False):
        total = add_up([keep[3], late[-1], middle[-1], end])
        index, left = lax.axis_index("dp"), self.dp // 8
        while left > 1:
            left //= 2
            bit = (index // left) % 2
            parts = total.reshape(2, total.shape[0] // 2, total.shape[1])
            there = exchange(pick(parts, 1 - bit, 0).astype(jnp.bfloat16), self.dp, left)
            total = pick(parts, bit, 0) + there.astype(jnp.float32)
        return total.T if turned else total


def third_of_two_kernel(*refs):
    out = refs[-1]
    for number in range(2):
        one, two, three = (ref[0].astype(jnp.float32) for ref in refs[3 * number : 3 * number + 3])
        out[number] = (one + two + three).astype(jnp.bfloat16)


def third_of_two(one, two):
    _, rows, columns = one[0].shape
    size = rows // 4
    specs = [
        pl.BlockSpec((1, size, columns), lambda i, at=at: (at, i, 0)) for at in (2, 0, 0)
    ]
    return pl.pallas_call(
        third_of_two_kernel,
        grid=(rows // size,),
        in_specs=specs * 2,
        out_specs=pl.BlockSpec((2, size, columns), lambda i: (0, i, 0)),
        out_shape=jax.ShapeDtypeStruct((2, rows, columns), jnp.bfloat16),
        compiler_params=params(60),
        name="third_of_two",
    )(*one, *two)


def sync(*values):
    return lax.optimization_barrier(values)


def column_tiles(width, most=256):
    return [(at, min(most, width - at)) for at in range(0, width, most)]


def feed_kernel(backs, *refs):
    one, two, cot_one, cot_two, w_gate, w_up, w_down = refs[:7]
    outs, scratch = refs[-11 - backs : -8], refs[-8:]
    hidden, grad_gate, grad_up = outs[:3]
    rows, cots, gate, up, down, gates, ups, sems = scratch
    count = one.shape[0]
    moves = [
        pltpu.make_async_copy(source, target, sems.at[number])
        for number, (source, target) in enumerate(
            (
                (one, rows.at[:count]),
                (two, rows.at[count:]),
                (w_gate, gate),
                (w_up, up),
                (cot_one, cots.at[:count]),
                (cot_two, cots.at[count:]),
                (w_down, down),
            )
        )
    ]
    for move in moves:
        move.start()
    for move in moves[:3]:
        move.wait()
    tiles = column_tiles(gate.shape[1])
    for at, size in tiles:
        gates[:, at : at + size] = nn(rows[...], gate[:, at : at + size])
    moves[3].wait()
    for at, size in tiles:
        ups[:, at : at + size] = nn(rows[...], up[:, at : at + size])
    for move in moves[4:]:
        move.wait()
    for at, size in tiles:
        span = slice(at, at + size)
        grad_hidden = nt(cots[...], down[span])
        gate_pre = gates[:, span]
        up_pre = ups[:, span]
        sigmoid = jax.nn.sigmoid(gate_pre)
        silu = gate_pre * sigmoid
        hidden[:, span] = (silu * up_pre).astype(jnp.bfloat16)
        slope = sigmoid + silu * (1.0 - sigmoid)
        grad_gate[:, span] = (grad_hidden * up_pre * slope).astype(jnp.bfloat16)
        grad_up[:, span] = (grad_hidden * silu).astype(jnp.bfloat16)
    if backs:
        for at, size in column_tiles(gate.shape[0]):
            span = slice(at, at + size)
            total = nt(grad_gate[...], gate[span]) + nt(grad_up[...], up[span])
            outs[3][:, span] = total[:count].astype(jnp.bfloat16)
            outs[4][:, span] = total[count:].astype(jnp.bfloat16)


def feed(side, pair, cots, w_gate, w_up, w_down, held=(), backs=0):
    count, depth = pair[0].shape
    width = w_gate.shape[1]
    block = pl.BlockSpec((count, depth), lambda i: (0, 0))
    return pl.pallas_call(
        lambda *refs: feed_kernel(backs, *refs),
        grid=(1,),
        out_shape=(jax.ShapeDtypeStruct((4 * count, width), jnp.bfloat16),) * 3
        + (jax.ShapeDtypeStruct((count, depth), jnp.bfloat16),) * backs,
        in_specs=[ANY] * (7 + len(held)),
        out_specs=(pl.BlockSpec((2 * count, width), lambda i: (side, 0)),) * 3 + (block,) * backs,
        scratch_shapes=[pltpu.VMEM((2 * count, depth), jnp.bfloat16)] * 2
        + [pltpu.VMEM((depth, width), jnp.bfloat16)] * 2
        + [
            pltpu.VMEM((width, depth), jnp.bfloat16),
            pltpu.VMEM((2 * count, width), jnp.float32),
            pltpu.VMEM((2 * count, width), jnp.float32),
            pltpu.SemaphoreType.DMA((7,)),
        ],
        input_output_aliases={7 + i: i for i in range(len(held))},
        compiler_params=params(56),
        name="feed",
    )(*pair, *cots, w_gate, w_up, w_down, *held)


def feed_back_kernel(grad_gate, grad_up, w_gate, w_up, one, two):
    total = nt(grad_gate[...], w_gate[...]) + nt(grad_up[...], w_up[...])
    total = total.astype(jnp.bfloat16)
    one[...] = total[: one.shape[0]]
    two[...] = total[one.shape[0] :]


def feed_back(side, grad_gate, grad_up, w_gate, w_up):
    count = grad_gate.shape[0] // 4
    depth, width = w_gate.shape
    size = 256
    rows = pl.BlockSpec((2 * count, width), lambda i: (side, 0))
    weights = pl.BlockSpec((size, width), lambda i: (i, 0))
    outs = pl.BlockSpec((count, size), lambda i: (0, i))
    return pl.pallas_call(
        feed_back_kernel,
        grid=(depth // size,),
        out_shape=(jax.ShapeDtypeStruct((count, depth), jnp.bfloat16),) * 2,
        in_specs=[rows, rows, weights, weights],
        out_specs=(outs, outs),
        compiler_params=params(60),
        name="feed_back",
    )(grad_gate, grad_up, w_gate, w_up)


def feed_down_kernel(hidden, w_down, own, across, others):
    total = nn(hidden[...], w_down[...]).astype(jnp.bfloat16)
    count = own.shape[0]
    own[...] = total[:count]
    others[:count] = total[count : 2 * count]
    across[...] = total[2 * count : 3 * count]
    others[count:] = total[3 * count :]


def feed_down(hidden, w_down):
    count = hidden.shape[0] // 4
    width, depth = w_down.shape
    size = 256
    block = pl.BlockSpec((count, size), lambda i: (0, i))
    return pl.pallas_call(
        feed_down_kernel,
        grid=(depth // size,),
        out_shape=(jax.ShapeDtypeStruct((count, depth), jnp.bfloat16),) * 2
        + (jax.ShapeDtypeStruct((2 * count, depth), jnp.bfloat16),),
        in_specs=[
            pl.BlockSpec((4 * count, width), lambda i: (0, 0)),
            pl.BlockSpec((width, size), lambda i: (0, i)),
        ],
        out_specs=(block, block, pl.BlockSpec((2 * count, size), lambda i: (0, i))),
        compiler_params=params(60),
        name="feed_down",
    )(hidden, w_down)


def to_core(values):
    return lax.ppermute(values, "row", SWAP)


def to_chip(values):
    return lax.ppermute(values, "col", SWAP)


def gather_blocks(own):
    across = to_chip(own)
    return own, to_core(own), across, to_core(across)


def scatter_far(across, diagonal):
    return to_chip((across + to_core(diagonal)).astype(jnp.bfloat16))


def pick(values, index, axis):
    return lax.dynamic_index_in_dim(values, index, axis, keepdims=False)


def add_up(terms):
    total = terms[0].astype(jnp.float32)
    for term in terms[1:]:
        total = total + term.astype(jnp.float32)
    return total


def norm_back(grad_normed, unit_rows, inverse, gain):
    scaled = grad_normed * gain
    inner = jnp.mean(scaled * unit_rows, axis=-1, keepdims=True)
    return inverse * (scaled - unit_rows * inner), jnp.sum(grad_normed * unit_rows, axis=0)


def local_for(dp):
    def local(
        tokens,
        segments,
        attn_gain,
        w_query,
        w_key,
        w_value,
        w_out,
        ffn_gain,
        w_gate,
        w_up,
        w_down,
        out_cotangent,
    ):
        query_width = w_query.shape[1]
        kv_width = w_key.shape[1]
        length = segments.shape[1]
        row, col = lax.axis_index("row"), lax.axis_index("col")
        places = [
            (((block // 2) ^ row) + 2 * ((block % 2) ^ col)) * (length // 4) for block in range(4)
        ]
        places = jnp.stack(places + [col]).astype(jnp.int32)

        inputs = tokens.astype(jnp.float32)
        inverse_one = lax.rsqrt(jnp.mean(inputs * inputs, axis=-1, keepdims=True) + EPSILON)
        unit_one = inputs * inverse_one
        normed_one = (unit_one * attn_gain).astype(jnp.bfloat16)
        across_one = to_chip(normed_one)
        beside_one = to_core(normed_one)
        qkv_weight = jnp.concatenate([w_query, w_key, w_value], axis=1)
        cosine, sine = rope_tables(positions(segments).reshape(length))
        seg_row = segments.reshape(1, length)
        near = nn(jnp.concatenate([normed_one, beside_one], axis=0), qkv_weight)
        across_one, near, cot, cosine, sine = sync(
            across_one, near, out_cotangent, cosine, sine
        )
        across_cot = to_chip(cot)
        beside_cot = to_core(cot)
        diagonal_one = to_core(across_one)
        blocks_one = (normed_one, beside_one, across_one, diagonal_one)
        far_mixed, rotated, far_logs, out_across, out_diagonal = attend_far(
            places, near, across_one, diagonal_one, qkv_weight, w_out, cosine, sine, seg_row
        )
        out_across, out_diagonal, rotated, across_cot, beside_cot = sync(
            out_across, out_diagonal, rotated, across_cot, beside_cot
        )
        out_diagonal = to_core(out_diagonal)
        diagonal_cot = to_core(across_cot)
        out_across, out_diagonal, rotated, diagonal_cot = sync(
            out_across, out_diagonal, rotated, diagonal_cot
        )
        cots = (out_cotangent, beside_cot, across_cot, diagonal_cot)
        far_out = to_chip((out_across + out_diagonal).astype(jnp.bfloat16))
        near_mixed, near_logs, out_own, out_beside = attend_near(
            places, rotated, w_out, seg_row
        )
        far_out, out_own, out_beside = sync(far_out, out_own, out_beside)
        out_beside = to_core(out_beside)
        middle = add_up([inputs, out_own, out_beside, far_out])
        inverse_two = lax.rsqrt(jnp.mean(middle * middle, axis=-1, keepdims=True) + EPSILON)
        unit_two = middle * inverse_two
        normed_two = (unit_two * ffn_gain).astype(jnp.bfloat16)
        across_two = to_chip(normed_two)
        beside_two = to_core(normed_two)
        mixed = jnp.concatenate([near_mixed, far_mixed], axis=0)
        *parts, back_own, back_beside = feed(
            0, (normed_two, beside_two), cots[:2], w_gate, w_up, w_down, backs=2
        )
        parts, across_two, mixed, back_own, back_beside = sync(
            parts, across_two, mixed, back_own, back_beside
        )
        diagonal_two = to_core(across_two)
        back_beside = to_core(back_beside)
        blocks_two = (normed_two, beside_two, across_two, diagonal_two)
        hidden, grad_gate, grad_up = feed(
            1, blocks_two[2:], cots[2:], w_gate, w_up, w_down, parts
        )

        gate = DpSum(blocks_two, grad_gate, (1, 2, 4), dp)
        down = DpSum(cots, hidden, (2, 1, 4), dp)
        gate_early, down_early = gate.early(), down.early()
        gate_early, down_early, grad_gate, grad_up, hidden, back_beside = sync(
            gate_early, down_early, grad_gate, grad_up, hidden, back_beside
        )

        gate.right, down.right = grad_gate, hidden
        up = DpSum(blocks_two, grad_up, (1, 2, 4), dp)
        gate_early = gate.send(gate_early, 0)
        down_early = down.send(down_early, 0)
        far_across, far_diagonal = feed_back(1, grad_gate, grad_up, w_gate, w_up)
        far_diagonal = to_core(far_diagonal)
        gate_late, down_late = gate.late(), down.late()
        (
            gate_early, down_early, far_across, far_diagonal, gate_late, down_late, gate.right,
            down.right, up.right,
        ) = sync(
            gate_early, down_early, far_across, far_diagonal, gate_late, down_late, grad_gate,
            hidden, grad_up,
        )

        gate_late = gate.send(gate_late, 0)
        down_late = down.send(down_late, 0)
        back_far = to_chip((far_across + far_diagonal).astype(jnp.bfloat16))
        gate_keep, down_keep = gate.keep(), down.keep()
        gate_middle = gate.second(gate_keep, gate_early)
        down_middle = down.second(down_keep, down_early)
        gate_late, down_late, back_far, gate_middle, down_middle, up.right, hidden = sync(
            gate_late, down_late, back_far, gate_middle, down_middle, up.right, down.right
        )

        gate_middle = gate.send(gate_middle, 1)
        down_middle = down.send(down_middle, 1)
        grad_normed_two = add_up([back_own, back_beside, back_far])
        grad_middle_norm, gain_two_grad = norm_back(
            grad_normed_two, unit_two, inverse_two, ffn_gain
        )
        grad_middle = out_cotangent.astype(jnp.float32) + grad_middle_norm
        from_own = grad_middle.astype(jnp.bfloat16)
        from_across = to_chip(from_own)
        from_beside = to_core(from_own)
        up_whole, up_keep = up.whole_and_keep()
        down_own, down_across, down_others = feed_down(hidden, w_down)
        (
            gate_middle, down_middle, from_across, from_beside, up_whole, up_keep, down_own,
            down_across, down_others,
        ) = sync(
            gate_middle, down_middle, from_across, from_beside, up_whole, up_keep, down_own,
            down_across, down_others,
        )

        up_whole = up.send(up_whole, 0)
        from_diagonal = to_core(from_across)
        ends = third_of_two(
            (gate_keep, gate_late, gate_middle), (down_keep, down_late, down_middle)
        )
        ends, from_diagonal = sync(ends, from_diagonal)
        ends = gate.send(ends, 2)
        down_others = to_core(down_others)
        grad_attn = (from_own, from_beside, from_across, from_diagonal)
        out = DpSum(grad_attn, mixed, (2, 1, 4), dp)
        out_whole = out.send(out.whole(), 0)
        grad_qkv, back_own, back_across, back_others = attend_back(
            places, rotated, near_logs, far_logs, cosine, sine, seg_row, w_out, qkv_weight, grad_attn
        )
        qkv = DpSum(blocks_one, grad_qkv, (1, 2, 4), dp)
        qkv_early, qkv_late = qkv.halves()
        gain_one_grad = sum(
            jnp.sum(part.astype(jnp.float32) * block.astype(jnp.float32), axis=0)
            for part, block in zip(
                (back_own, back_others[:BLOCK], back_across, back_others[BLOCK:]), blocks_one
            )
        )
        gains = jnp.stack([gain_one_grad / attn_gain, gain_two_grad])
        (
            up_whole, ends, out_whole, qkv_early, qkv_late, qkv.right, back_own, back_across,
            back_others, down_others, gains, out.right,
        ) = sync(
            up_whole, ends, out_whole, qkv_early, qkv_late, grad_qkv, back_own, back_across,
            back_others, down_others, gains, mixed,
        )

        qkv_early = qkv.send(qkv_early, 0)
        up_middle = up.second(up_keep, up_whole)
        up_first = up.send(up_middle[:1], 1)
        others = to_core(back_others)
        gains_there = to_core(gains)
        out_keep, qkv_keep = out.keep(), qkv.keep()
        (
            qkv_early, up_first, up_middle, others, gains, gains_there, out_keep, qkv_keep, qkv_late,
        ) = sync(
            qkv_early, up_first, up_middle, others, gains, gains_there, out_keep, qkv_keep, qkv_late,
        )

        up_end = up.send(up.third(up_keep, up_whole, up_first), 2)
        qkv_middle = qkv.send(qkv.second(qkv_keep, qkv_early), 1)
        both = jnp.concatenate([qkv_late, out.second(out_keep, out_whole)], axis=2)
        both = qkv.send(both, 0)
        one_far = to_chip((back_across + others[BLOCK:]).astype(jnp.bfloat16))
        gains = gains + gains_there
        gains_there = to_chip(gains)
        gate_grad = gate.finish(gate_keep, gate_late, gate_middle, ends[0])
        down_grad = down.finish(down_keep, down_late, down_middle, ends[1], True)
        up_end, qkv_middle, both, one_far, gains, gains_there, gate_grad, down_grad, up_middle = sync(
            up_end, qkv_middle, both, one_far, gains, gains_there, gate_grad, down_grad, up_middle
        )
        width = qkv_weight.shape[1]
        qkv_late, out_middle = both[:, :, :width], both[:, :, width:]

        up_second = up.send(up_middle[1:], 1)
        ends = jnp.concatenate(
            [
                qkv.third(qkv_keep, qkv_late, qkv_middle),
                out.third(out_keep, out_whole, out_middle),
            ],
            axis=1,
        )
        ends = qkv.send(ends, 2)
        down_far = to_chip((down_across + down_others[BLOCK:]).astype(jnp.bfloat16))
        gains = gains + gains_there
        gains_there = exchange(gains, dp, 1)
        grad_normed_one = add_up([back_own, others[:BLOCK], one_far])
        scaled = grad_normed_one * attn_gain
        mean = jnp.mean(scaled * unit_one, axis=-1, keepdims=True)
        input_grad = grad_middle + inverse_one * (scaled - unit_one * mean)
        ends, up_second, down_far, gains, gains_there, input_grad = sync(
            ends, up_second, down_far, gains, gains_there, input_grad
        )
        gains = gains + gains_there
        step = 2
        while step < dp:
            gains = gains + exchange(gains, dp, step)
            step *= 2
        up_grad = up.finish(up_keep, up_whole, up_second, up_end)
        qkv_grad = qkv.finish(qkv_keep, qkv_late, qkv_middle, ends[:, :width])
        out_grad = out.finish(out_keep, out_whole, out_middle, ends[:, width:], True)
        output = add_up([middle, down_own, down_others[:BLOCK], down_far]).astype(jnp.bfloat16)
        key_end = query_width + kv_width
        return (
            output,
            input_grad,
            gains[0],
            qkv_grad[:, :query_width],
            qkv_grad[:, query_width:key_end],
            qkv_grad[:, key_end:],
            out_grad,
            gains[1],
            gate_grad,
            up_grad,
            down_grad,
        )

    return local


def solution(mesh):
    rows = P(("dp", "row", "col"), None)
    columns = P(None, ("row", "col"))
    placed = (
        rows,
        P("dp", None),
        P(),
        columns,
        columns,
        columns,
        P(("row", "col"), None),
        P(),
        columns,
        columns,
        P(("row", "col"), None),
        rows,
    )
    summed = P("dp", ("row", "col"))
    turned = P(("row", "col"), "dp")
    return jax.shard_map(
        local_for(mesh.shape["dp"]),
        mesh=mesh,
        in_specs=placed,
        out_specs=(rows, rows, P(), summed, summed, summed, turned, P(), summed, summed, turned),
        check_vma=False,
    )
```

```python
import jax
import jax.numpy as jnp
from jax import lax
from jax.experimental import pallas as pl
from jax.experimental.pallas import tpu as pltpu
from jax.sharding import PartitionSpec as P

HD = 64
EPSILON = 1e-05
MASKED_SCORE = -1e30
BLOCK = 256
TILE = 128
SWAP = ((0, 1), (1, 0))


def positions(segment_ids):
    indices = jnp.arange(segment_ids.shape[-1], dtype=jnp.int32)
    previous = jnp.concatenate([segment_ids[..., :1] - 1, segment_ids[..., :-1]], axis=-1)
    starts = jnp.where(segment_ids != previous, indices, 0)
    return indices - lax.cummax(starts, axis=segment_ids.ndim - 1)


def rope_tables(position):
    exponent = jnp.arange(HD // 2, dtype=jnp.float32) * (-2.0 / HD)
    angles = position.astype(jnp.float32)[:, None] * (10000.0**exponent)[None, :]
    cosine, sine = jnp.cos(angles), jnp.sin(angles)
    return (
        jnp.concatenate([cosine] * 4, axis=1),
        jnp.concatenate([-sine, sine, -sine, sine], axis=1),
    )


def nt(left, right):
    return lax.dot_general(
        left, right, (((1,), (1,)), ((), ())), preferred_element_type=jnp.float32
    )


def nn(left, right):
    return lax.dot_general(
        left, right, (((1,), (0,)), ((), ())), preferred_element_type=jnp.float32
    )


def tn(left, right):
    return lax.dot_general(
        left, right, (((0,), (0,)), ((), ())), preferred_element_type=jnp.float32
    )


def lane_marks():
    lane = lax.broadcasted_iota(jnp.int32, (BLOCK, TILE), 1)
    return lane, lane < HD, lane % HD < HD // 2


def turn_by(values, cosine, sine, first):
    turned = jnp.where(
        first, pltpu.roll(values, TILE - HD // 2, 1), pltpu.roll(values, HD // 2, 1)
    )
    return values * cosine + turned * sine


def rows_of(places, block):
    return pl.ds(pl.multiple_of(places[block], BLOCK), BLOCK)


def segment_column(seg_row, at):
    return jnp.broadcast_to(seg_row[:, at], (TILE, BLOCK)).T


def attend_block(block, places, rotated, keys, values, seg_row, mixed, target, log_sums):
    width = mixed.shape[1]
    lane, low, _ = lane_marks()
    rows = rows_of(places, block)
    at = slice(block * BLOCK, (block + 1) * BLOCK)
    begin = max(0, block - 2) * BLOCK
    span = slice(begin, (block + 1) * BLOCK)
    count = (block + 1) * BLOCK - begin
    key_at = begin + lax.broadcasted_iota(jnp.int32, (BLOCK, count), 1)
    query_at = block * BLOCK + lax.broadcasted_iota(jnp.int32, (BLOCK, count), 0)
    seg_col = segment_column(seg_row, at)[:, :1]
    allowed = (seg_col == seg_row[:, span]) & (key_at <= query_at)
    bias = jnp.where(allowed, 0.0, MASKED_SCORE)
    key_span = keys[span]
    value_span = values[span]

    def one_pair(number, logs):
        columns = pl.ds(pl.multiple_of(number * TILE, TILE), TILE)
        query = rotated[rows, columns]
        results = []
        for half in range(2):
            chosen = jnp.where(low if half == 0 else ~low, query, jnp.zeros_like(query))
            scores = nt(chosen, key_span) + bias
            largest = jnp.max(scores, axis=1, keepdims=True)
            shifted = jnp.exp(scores - largest)
            total = jnp.sum(shifted, axis=1, keepdims=True)
            results.append(nn(shifted.astype(jnp.bfloat16), value_span) * (1.0 / total))
            logs = jnp.where(lane == 2 * number + half, largest + jnp.log(total), logs)
        mixed[target, columns] = jnp.where(low, results[0], results[1]).astype(jnp.bfloat16)
        return logs

    logs = lax.fori_loop(0, width // TILE, one_pair, jnp.zeros((BLOCK, TILE), jnp.float32))
    log_sums[:, at] = logs.T[: log_sums.shape[0]]


def key_value_rows(rotated, rows, keys, values, at, low):
    width = rotated.shape[1] - TILE
    pair = rotated[rows, width:].astype(jnp.float32)
    swapped = pltpu.roll(pair, HD, 1)
    keys[at] = jnp.where(low, pair, swapped).astype(jnp.bfloat16)
    values[at] = jnp.where(low, swapped, pair).astype(jnp.bfloat16)


def attend_side(side, places, rotated, keys, values, seg_row, mixed, log_sums):
    blocks = rotated.shape[0] // BLOCK
    for parity in range(2):

        @pl.when((places[blocks] ^ side) == parity)
        def _():
            for block in range(parity, blocks, 2):
                start = places[block] - side * 2 * BLOCK
                target = pl.ds(pl.multiple_of(start, BLOCK), BLOCK)
                attend_block(
                    block, places, rotated, keys, values, seg_row, mixed, target, log_sums
                )


def attend_far_kernel(
    places, near, across, diagonal, weight, w_out, cosine, sine, seg_row,
    mixed, rotated, log_sums, out_across, out_diagonal, keys, values,
):
    length, total = rotated.shape
    width = total - TILE
    blocks = length // BLOCK
    _, low, first = lane_marks()
    for block in range(blocks):
        rows = rows_of(places, block)
        at = slice(block * BLOCK, (block + 1) * BLOCK)

        def turn_all(proj):
            for start in range(0, width, TILE):
                query = turn_by(proj[:, start : start + TILE], cosine[at], sine[at], first)
                rotated[rows, start : start + TILE] = (query * HD ** (-0.5)).astype(jnp.bfloat16)
            pair = proj[:, width:]
            turned = jnp.where(low, turn_by(pair, cosine[at], sine[at], first), pair)
            rotated[rows, width:] = turned.astype(jnp.bfloat16)

        for piece, source in ((0, None), (1, None), (2, across), (3, diagonal)):

            @pl.when(places[block] == piece * BLOCK)
            def _(piece=piece, source=source):
                if source is None:
                    turn_all(near[piece * BLOCK : (piece + 1) * BLOCK])
                else:
                    turn_all(nn(source[...], weight[...]))

        key_value_rows(rotated, rows, keys, values, at, low)
    attend_side(1, places, rotated, keys, values, seg_row, mixed, log_sums)
    out_diagonal[...] = nn(mixed[BLOCK:], w_out[...]).astype(jnp.bfloat16)
    out_across[...] = nn(mixed[:BLOCK], w_out[...]).astype(jnp.bfloat16)


def attend_near_kernel(
    places, rotated, w_out, seg_row, mixed, log_sums, out_own, out_beside, keys, values
):
    blocks = rotated.shape[0] // BLOCK
    _, low, _ = lane_marks()
    for block in range(blocks):
        at = slice(block * BLOCK, (block + 1) * BLOCK)
        key_value_rows(rotated, rows_of(places, block), keys, values, at, low)
    attend_side(0, places, rotated, keys, values, seg_row, mixed, log_sums)
    out_beside[...] = nn(mixed[BLOCK:], w_out[...]).astype(jnp.bfloat16)
    out_own[...] = nn(mixed[:BLOCK], w_out[...]).astype(jnp.bfloat16)


def attend_back_kernel(
    places, rotated, near_logs, far_logs, cosine, sine, seg_row, w_out, weight,
    from_own, from_beside, from_across, from_diagonal,
    grads, back_own, back_across, back_others,
    keys, values, key_sum, value_sum, grad_mixed, seg_col,
):
    length = rotated.shape[0]
    width = grad_mixed.shape[1]
    blocks = length // BLOCK
    _, low, first = lane_marks()
    for piece, source in enumerate((from_own, from_beside, from_across, from_diagonal)):
        grad_mixed[piece * BLOCK : (piece + 1) * BLOCK] = nt(source[...], w_out[...]).astype(
            jnp.bfloat16
        )
    key_sum[...] = jnp.zeros_like(key_sum)
    value_sum[...] = jnp.zeros_like(value_sum)
    for block in range(blocks):
        at = slice(block * BLOCK, (block + 1) * BLOCK)
        key_value_rows(rotated, rows_of(places, block), keys, values, at, low)
        seg_col[at] = segment_column(seg_row, at)
    for block in range(blocks):
        rows = rows_of(places, block)
        at = slice(block * BLOCK, (block + 1) * BLOCK)
        is_near = places[blocks] == block % 2
        begin = max(0, block - 2) * BLOCK
        span = slice(begin, (block + 1) * BLOCK)
        count = (block + 1) * BLOCK - begin
        key_at = begin + lax.broadcasted_iota(jnp.int32, (count, BLOCK), 0)
        query_at = block * BLOCK + lax.broadcasted_iota(jnp.int32, (count, BLOCK), 1)
        allowed = (seg_col[span, :1] == seg_row[:, at]) & (key_at <= query_at)
        bias = jnp.where(allowed, 0.0, MASKED_SCORE)
        key_span = keys[span]
        value_span = values[span]

        def one_pair(number, carry):
            columns = pl.ds(pl.multiple_of(number * TILE, TILE), TILE)
            query = rotated[rows, columns]
            grad = grad_mixed[rows, columns]
            results = []
            for half in range(2):
                side = low if half == 0 else ~low
                chosen = jnp.where(side, query, jnp.zeros_like(query))
                chosen_grad = jnp.where(side, grad, jnp.zeros_like(grad))
                head = pl.ds(2 * number + half, 1)
                logs = jnp.where(is_near, near_logs[head, at], far_logs[head, at])
                probs = jnp.exp(nt(key_span, chosen) + bias - logs)
                grad_probs = nt(value_span, chosen_grad)
                inner = jnp.sum(probs * grad_probs, axis=0, keepdims=True)
                grad_scores = (probs * (grad_probs - inner)).astype(jnp.bfloat16)
                value_sum[span] += nn(probs.astype(jnp.bfloat16), chosen_grad)
                key_sum[span] += nn(grad_scores, chosen)
                results.append(tn(grad_scores, key_span))
            grad_query = jnp.where(low, results[0], results[1]) * HD ** (-0.5)
            grads[rows, columns] = turn_by(grad_query, cosine[at], -sine[at], first).astype(
                jnp.bfloat16
            )
            return carry

        lax.fori_loop(0, width // TILE, one_pair, 0)
    for block in range(blocks):
        rows = rows_of(places, block)
        at = slice(block * BLOCK, (block + 1) * BLOCK)
        grad_key = key_sum[at]
        grad_key = turn_by(grad_key + pltpu.roll(grad_key, HD, 1), cosine[at], -sine[at], first)
        grad_value = value_sum[at]
        grad_value = grad_value + pltpu.roll(grad_value, HD, 1)
        grads[rows, width:] = jnp.where(low, grad_key, grad_value).astype(jnp.bfloat16)
    targets = (back_own, back_others.at[:BLOCK], back_across, back_others.at[BLOCK:])
    for piece, target in enumerate(targets):
        grad_rows = grads[piece * BLOCK : (piece + 1) * BLOCK]
        target[...] = nt(grad_rows, weight[...]).astype(jnp.bfloat16)


SMEM = pl.BlockSpec(memory_space=pltpu.SMEM)
VMEM = pl.BlockSpec(memory_space=pltpu.VMEM)


ANY = pl.BlockSpec(memory_space=pl.ANY)
LITTLE = pl.CostEstimate(flops=1 << 20, bytes_accessed=1 << 12, transcendentals=0)


def params(limit):
    return pltpu.CompilerParams(vmem_limit_bytes=limit << 20)


def attend_far(places, near, across, diagonal, weight, w_out, cosine, sine, seg_row):
    length, total = 2 * near.shape[0], near.shape[1]
    width = total - TILE
    depth = w_out.shape[1]
    block = jax.ShapeDtypeStruct((BLOCK, depth), jnp.bfloat16)
    return pl.pallas_call(
        attend_far_kernel,
        out_shape=(
            jax.ShapeDtypeStruct((length // 2, width), jnp.bfloat16),
            jax.ShapeDtypeStruct((length, total), jnp.bfloat16),
            jax.ShapeDtypeStruct((width // HD, length), jnp.float32),
            block,
            block,
        ),
        in_specs=[SMEM] + [VMEM] * 8,
        out_specs=(VMEM,) * 5,
        scratch_shapes=[pltpu.VMEM((length, TILE), jnp.bfloat16)] * 2,
        compiler_params=params(48),
        cost_estimate=LITTLE,
        name="attend_far",
    )(places, near, across, diagonal, weight, w_out, cosine, sine, seg_row)


def attend_near(places, rotated, w_out, seg_row):
    length, total = rotated.shape
    width = total - TILE
    depth = w_out.shape[1]
    block = jax.ShapeDtypeStruct((BLOCK, depth), jnp.bfloat16)
    return pl.pallas_call(
        attend_near_kernel,
        out_shape=(
            jax.ShapeDtypeStruct((length // 2, width), jnp.bfloat16),
            jax.ShapeDtypeStruct((width // HD, length), jnp.float32),
            block,
            block,
        ),
        in_specs=[SMEM] + [VMEM] * 3,
        out_specs=(VMEM,) * 4,
        scratch_shapes=[pltpu.VMEM((length, TILE), jnp.bfloat16)] * 2,
        compiler_params=params(48),
        cost_estimate=LITTLE,
        name="attend_near",
    )(places, rotated, w_out, seg_row)


def attend_back(
    places, rotated, near_logs, far_logs, cosine, sine, seg_row, w_out, weight, pieces
):
    length, total = rotated.shape
    return pl.pallas_call(
        attend_back_kernel,
        out_shape=(jax.ShapeDtypeStruct((length, total), jnp.bfloat16),)
        + (jax.ShapeDtypeStruct(pieces[0].shape, jnp.bfloat16),) * 2
        + (jax.ShapeDtypeStruct((2 * BLOCK, pieces[0].shape[1]), jnp.bfloat16),),
        in_specs=[SMEM] + [VMEM] * 12,
        out_specs=(VMEM,) * 4,
        scratch_shapes=[pltpu.VMEM((length, TILE), jnp.bfloat16)] * 2
        + [pltpu.VMEM((length, TILE), jnp.float32)] * 2
        + [
            pltpu.VMEM((length, total - TILE), jnp.bfloat16),
            pltpu.VMEM((length, TILE), jnp.int32),
        ],
        compiler_params=params(52),
        cost_estimate=LITTLE,
        name="attend_back",
    )(
        places, rotated, near_logs, far_logs, cosine, sine, seg_row, w_out, weight, *pieces
    )


def terms_kernel(starts, units, one, two, three, four, right, *outs):
    left = jnp.concatenate([one[...], two[...], three[...], four[...]], axis=0)
    total = tn(left, right[...]).astype(jnp.bfloat16)
    step = pl.program_id(0)
    for out, start, end in zip(outs, starts, starts[1:]):

        @pl.when((step >= start) & (step < end))
        def _(out=out):
            out[0] = total


def weight_terms(pieces, right, units, first, sizes):
    count = pieces[0].shape[0]
    rows, width = right.shape
    starts = [sum(sizes[:number]) for number in range(len(sizes) + 1)]
    return pl.pallas_call(
        lambda *refs: terms_kernel(starts, *refs),
        grid_spec=pltpu.PrefetchScalarGridSpec(
            num_scalar_prefetch=1,
            grid=(starts[-1],),
            in_specs=[pl.BlockSpec((count, BLOCK), lambda i, units: (0, units[first + i]))] * 4
            + [pl.BlockSpec((rows, width), lambda i, units: (0, 0))],
            out_specs=[
                pl.BlockSpec(
                    (1, BLOCK, width),
                    lambda i, units, start=start, size=size: (
                        jnp.clip(i - start, 0, size - 1),
                        0,
                        0,
                    ),
                )
                for start, size in zip(starts, sizes)
            ],
        ),
        out_shape=[jax.ShapeDtypeStruct((size, BLOCK, width), jnp.bfloat16) for size in sizes],
        compiler_params=params(60),
        cost_estimate=LITTLE,
        name="weight_terms",
    )(units, *pieces, right)


def pair_kernel(each, units, *refs):
    left, right, outs = refs[:8], refs[8:10], refs[10:]
    for number, out in enumerate(outs):

        @pl.when(pl.program_id(0) // each == number)
        def _(number=number, out=out):
            pieces = [ref[...] for ref in left[4 * number : 4 * number + 4]]
            total = tn(jnp.concatenate(pieces, axis=0), right[number][...])
            out[0] = total.astype(jnp.bfloat16)


def weight_pair(sums, first, size):
    count = sums[0].pieces[0].shape[0]
    rows, width = sums[0].right.shape

    def step(i, number):
        return jnp.clip(i - number * size, 0, size - 1)

    specs = []
    for number, each in enumerate(sums):
        specs += [
            pl.BlockSpec(
                (count, BLOCK),
                lambda i, units, number=number, start=each.base + first: (
                    0,
                    units[start + step(i, number)],
                ),
            )
        ] * 4
    return pl.pallas_call(
        lambda *refs: pair_kernel(size, *refs),
        grid_spec=pltpu.PrefetchScalarGridSpec(
            num_scalar_prefetch=1,
            grid=(2 * size,),
            in_specs=specs + [pl.BlockSpec((rows, width), lambda i, units: (0, 0))] * 2,
            out_specs=[
                pl.BlockSpec(
                    (1, BLOCK, width), lambda i, units, number=number: (step(i, number), 0, 0)
                )
                for number in range(2)
            ],
        ),
        out_shape=[jax.ShapeDtypeStruct((size, BLOCK, width), jnp.bfloat16)] * 2,
        compiler_params=params(60),
        cost_estimate=LITTLE,
        name="weight_pair",
    )(sums[0].units, *sums[0].pieces, *sums[1].pieces, sums[0].right, sums[1].right)


def exchange(values, dp, distance):
    return lax.ppermute(values, "dp", [(device, device ^ distance) for device in range(dp)])


def numbered(bits, values, free):
    fixed = jnp.zeros((), jnp.int32)
    for bit, value in zip(bits, values):
        fixed = fixed + bit * value
    numbers = [fixed]
    for bit in free:
        numbers = [number + add for number in numbers for add in (0, bit)]
    return jnp.stack(numbers).astype(jnp.int32)


ORDERS = ((1, 2, 4), (2, 1, 4))


def unit_table(dp):
    unit = lax.axis_index("dp") // (dp // 8)
    numbers = []
    for order in ORDERS:
        one, two, three = ((unit // bit) % 2 for bit in order)
        numbers += [
            sum(bit * value for bit, value in zip(order, values))
            for values in (
                (first, second, third)
                for first in (1 - one, one)
                for second in (1 - two, two)
                for third in (1 - three, three)
            )
        ]
    return jnp.stack(numbers).astype(jnp.int32)


class DpSum:
    def __init__(self, pieces, right, order, dp, units):
        self.pieces, self.right, self.order, self.dp, self.units = pieces, right, order, dp, units
        self.base = 8 * ORDERS.index(order)

    def terms(self, first, *sizes):
        return weight_terms(self.pieces, self.right, self.units, self.base + first, sizes)

    def whole(self):
        return self.terms(0, 4)[0]

    def halves(self):
        return self.terms(0, 2, 2)

    def keep(self):
        return self.terms(4, 4)[0]

    def whole_and_keep(self):
        return self.terms(0, 4, 4)

    def send(self, values, step):
        return exchange(values, self.dp, self.order[step] * (self.dp // 8))

    def second(self, keep, early):
        return add_up([keep[:2], early[:2]]).astype(jnp.bfloat16)

    def second_unit(self, number, keep, early):
        return add_up([keep[number : number + 1], early[number : number + 1]]).astype(jnp.bfloat16)

    def third(self, keep, late, middle):
        at = late.shape[0] - 2
        return add_up([keep[2], late[at], middle[0]]).astype(jnp.bfloat16)

    def finish(self, keep, late, middle, *ends, turned=False):
        if self.dp == 8:
            return finish_sum(keep, late, middle, ends, turned)
        total = finish_sum(keep, late, middle, ends, False)
        index, left = lax.axis_index("dp"), self.dp // 8
        while left > 1:
            left //= 2
            bit = (index // left) % 2
            parts = total.reshape(2, total.shape[0] // 2, total.shape[1])
            there = exchange(pick(parts, 1 - bit, 0).astype(jnp.bfloat16), self.dp, left)
            total = pick(parts, bit, 0) + there.astype(jnp.float32)
        return total.T if turned else total


def finish_kernel(turned, ends, keep, late, middle, *refs):
    out = refs[-1]
    end = refs[0][...].astype(jnp.float32)
    if ends == 2:
        end = jnp.where(pl.program_id(0) == 0, end, refs[1][...].astype(jnp.float32))
    total = keep[0].astype(jnp.float32) + late[0].astype(jnp.float32)
    total = total + middle[0].astype(jnp.float32) + end
    out[...] = total.T if turned else total


def finish_sum(keep, late, middle, ends, turned):
    _, rows, columns = keep.shape
    size = rows // 2
    specs = [
        pl.BlockSpec((1, size, columns), lambda i, at=array.shape[0] - 1: (at, i, 0))
        for array in (keep, late, middle)
    ]
    end = pl.BlockSpec((size, columns), lambda i: (0 if len(ends) == 2 else i, 0))
    shape = (columns, rows) if turned else (rows, columns)
    out = (
        pl.BlockSpec((columns, size), lambda i: (0, i))
        if turned
        else pl.BlockSpec((size, columns), lambda i: (i, 0))
    )
    return pl.pallas_call(
        lambda *refs: finish_kernel(turned, len(ends), *refs),
        grid=(2,),
        in_specs=specs + [end] * len(ends),
        out_specs=out,
        out_shape=jax.ShapeDtypeStruct(shape, jnp.float32),
        compiler_params=params(40),
        cost_estimate=LITTLE,
        name="finish_sum",
    )(keep, late, middle, *ends)


def row_call(kernel, rows, wholes, outs, totals=0):
    count, depth = rows[0].shape
    size = 64
    block = pl.BlockSpec((size, depth), lambda i: (i, 0))
    whole = pl.BlockSpec((1, depth), lambda i: (0, 0))
    return pl.pallas_call(
        kernel,
        grid=(count // size,),
        in_specs=[block] * len(rows) + [whole] * len(wholes),
        out_specs=(block,) * len(outs) + (whole,) * totals,
        out_shape=tuple(jax.ShapeDtypeStruct((count, depth), kind) for kind in outs)
        + (jax.ShapeDtypeStruct((1, depth), jnp.float32),) * totals,
        compiler_params=params(40),
        cost_estimate=LITTLE,
        name=kernel.__name__,
    )(*rows, *(array.reshape(1, depth) for array in wholes))


def scale_back(values, grads, gain):
    inverse = lax.rsqrt(jnp.mean(values * values, axis=-1, keepdims=True) + EPSILON)
    unit = values * inverse
    scaled = grads * gain
    return unit, inverse * (scaled - unit * jnp.mean(scaled * unit, axis=-1, keepdims=True))


def middle_back(middle, cot, one, two, three, gain, grad_middle, rounded, gain_grad):
    grads = one[...].astype(jnp.float32) + two[...].astype(jnp.float32) + three[...].astype(jnp.float32)
    unit, back = scale_back(middle[...], grads, gain[...])
    total = cot[...].astype(jnp.float32) + back
    grad_middle[...] = total
    rounded[...] = total.astype(jnp.bfloat16)

    @pl.when(pl.program_id(0) == 0)
    def _():
        gain_grad[...] = jnp.zeros_like(gain_grad)

    gain_grad[...] += jnp.sum(grads * unit, axis=0, keepdims=True)


def input_back(tokens, grad_middle, one, two, three, gain, input_grad):
    grads = one[...].astype(jnp.float32) + two[...].astype(jnp.float32) + three[...].astype(jnp.float32)
    _, back = scale_back(tokens[...].astype(jnp.float32), grads, gain[...])
    input_grad[...] = grad_middle[...] + back


def add_output(middle, one, two, three, output):
    total = middle[...] + one[...].astype(jnp.float32) + two[...].astype(jnp.float32)
    output[...] = (total + three[...].astype(jnp.float32)).astype(jnp.bfloat16)


def sync(*values):
    return lax.optimization_barrier(values)


def column_tiles(width, most=256):
    return [(at, min(most, width - at)) for at in range(0, width, most)]


def feed_near_kernel(one, two, cot_one, cot_two, w_gate, w_up, w_down, *rest):
    hidden, grad_gate, grad_up, back_one, back_two = rest[:5]
    rows, cots, gate, up, down, gates, ups, sems = rest[5:]
    sources = (one, two, w_gate, w_up, cot_one, cot_two, w_down)
    feed_steps(sources, rest[5:], hidden, grad_gate, grad_up)
    count = back_one.shape[0]
    for at, size in column_tiles(gate.shape[0]):
        span = slice(at, at + size)
        total = nt(grad_gate[...], gate[span]) + nt(grad_up[...], up[span])
        back_one[:, span] = total[:count].astype(jnp.bfloat16)
        back_two[:, span] = total[count:].astype(jnp.bfloat16)


def feed_far_kernel(units, one, two, cot_one, cot_two, w_gate, w_up, w_down, *rest):
    near_one, near_two, near_cot_one, near_cot_two, held_hidden, held_gate, _ = rest[:7]
    hidden, grad_gate, grad_up, gate_early, down_early = rest[7:12]
    near_rows, near_cots, near_hidden, near_gate, near_sems = rest[12:17]
    scratch = rest[17:]
    rows, cots = scratch[:2]
    count = one.shape[0]
    moves = [
        pltpu.make_async_copy(held_hidden.at[: 2 * count], near_hidden, near_sems.at[0]),
        pltpu.make_async_copy(held_gate.at[: 2 * count], near_gate, near_sems.at[1]),
    ]
    lefts = (
        (near_one, near_rows, 0, 0),
        (near_two, near_rows, count, 0),
        (near_cot_one, near_cots, 0, 8),
        (near_cot_two, near_cots, count, 8),
    )
    for number, (source, target, start, first) in enumerate(lefts):
        for unit in range(2):
            columns = pl.ds(pl.multiple_of(units[first + unit] * BLOCK, BLOCK), BLOCK)
            moves.append(
                pltpu.make_async_copy(
                    source.at[:, columns],
                    target.at[unit, start : start + count],
                    near_sems.at[2 + 2 * number + unit],
                )
            )
    sources = (one, two, w_gate, w_up, cot_one, cot_two, w_down)
    feed_steps(sources, scratch, hidden, grad_gate, grad_up, moves)
    for first, left, far_left, near_right, far_right, out in (
        (0, near_rows, rows, near_gate, grad_gate, gate_early),
        (8, near_cots, cots, near_hidden, hidden, down_early),
    ):
        for unit in range(2):
            columns = pl.ds(pl.multiple_of(units[first + unit] * BLOCK, BLOCK), BLOCK)
            total = tn(left[unit], near_right[...]) + tn(far_left[:, columns], far_right[...])
            out[unit] = total.astype(jnp.bfloat16)


def feed_steps(sources, scratch, hidden, grad_gate, grad_up, more=()):
    rows, cots, gate, up, down, gates, ups, sems = scratch
    count = sources[0].shape[0]
    targets = (
        rows.at[:count], rows.at[count:], gate, up, cots.at[:count], cots.at[count:], down,
    )
    moves = [
        pltpu.make_async_copy(source, target, sems.at[number])
        for number, (source, target) in enumerate(zip(sources, targets))
    ]
    for move in (*moves, *more):
        move.start()
    for move in moves[:3]:
        move.wait()
    tiles = column_tiles(gate.shape[1])
    for at, size in tiles:
        gates[:, at : at + size] = nn(rows[...], gate[:, at : at + size])
    moves[3].wait()
    for at, size in tiles:
        ups[:, at : at + size] = nn(rows[...], up[:, at : at + size])
    for move in moves[4:]:
        move.wait()
    for at, size in tiles:
        span = slice(at, at + size)
        grad_hidden = nt(cots[...], down[span])
        gate_pre = gates[:, span]
        up_pre = ups[:, span]
        sigmoid = jax.nn.sigmoid(gate_pre)
        silu = gate_pre * sigmoid
        hidden[:, span] = (silu * up_pre).astype(jnp.bfloat16)
        slope = sigmoid + silu * (1.0 - sigmoid)
        grad_gate[:, span] = (grad_hidden * up_pre * slope).astype(jnp.bfloat16)
        grad_up[:, span] = (grad_hidden * silu).astype(jnp.bfloat16)
    for move in more:
        move.wait()


def feed_scratch(count, depth, width):
    return (
        [pltpu.VMEM((2 * count, depth), jnp.bfloat16)] * 2
        + [pltpu.VMEM((depth, width), jnp.bfloat16)] * 2
        + [
            pltpu.VMEM((width, depth), jnp.bfloat16),
            pltpu.VMEM((2 * count, width), jnp.float32),
            pltpu.VMEM((2 * count, width), jnp.float32),
            pltpu.SemaphoreType.DMA((7,)),
        ]
    )


def feed_near(pair, cots, w_gate, w_up, w_down):
    count, depth = pair[0].shape
    width = w_gate.shape[1]
    return pl.pallas_call(
        feed_near_kernel,
        grid=(1,),
        out_shape=(jax.ShapeDtypeStruct((4 * count, width), jnp.bfloat16),) * 3
        + (jax.ShapeDtypeStruct((count, depth), jnp.bfloat16),) * 2,
        in_specs=[ANY] * 7,
        out_specs=(pl.BlockSpec((2 * count, width), lambda i: (0, 0)),) * 3
        + (pl.BlockSpec((count, depth), lambda i: (0, 0)),) * 2,
        scratch_shapes=feed_scratch(count, depth, width),
        compiler_params=params(56),
        cost_estimate=LITTLE,
        name="feed_near",
    )(*pair, *cots, w_gate, w_up, w_down)


def feed_far(units, blocks, cots, w_gate, w_up, w_down, held):
    count, depth = blocks[0].shape
    width = w_gate.shape[1]
    early = jax.ShapeDtypeStruct((2, BLOCK, width), jnp.bfloat16)
    return pl.pallas_call(
        feed_far_kernel,
        grid_spec=pltpu.PrefetchScalarGridSpec(
            num_scalar_prefetch=1,
            grid=(1,),
            in_specs=[ANY] * 14,
            out_specs=(pl.BlockSpec((2 * count, width), lambda i, units: (1, 0)),) * 3
            + (pl.BlockSpec((2, BLOCK, width), lambda i, units: (0, 0, 0)),) * 2,
            scratch_shapes=[pltpu.VMEM((2, 2 * count, BLOCK), jnp.bfloat16)] * 2
            + [pltpu.VMEM((2 * count, width), jnp.bfloat16)] * 2
            + [pltpu.SemaphoreType.DMA((10,))]
            + feed_scratch(count, depth, width),
        ),
        out_shape=(jax.ShapeDtypeStruct((4 * count, width), jnp.bfloat16),) * 3 + (early,) * 2,
        input_output_aliases={12: 0, 13: 1, 14: 2},
        compiler_params=params(60),
        cost_estimate=LITTLE,
        name="feed_far",
    )(units, *blocks[2:], *cots[2:], w_gate, w_up, w_down, *blocks[:2], *cots[:2], *held)


def feed_back_kernel(grad_gate, grad_up, w_gate, w_up, one, two):
    total = nt(grad_gate[...], w_gate[...]) + nt(grad_up[...], w_up[...])
    total = total.astype(jnp.bfloat16)
    one[...] = total[: one.shape[0]]
    two[...] = total[one.shape[0] :]


def feed_back(side, grad_gate, grad_up, w_gate, w_up):
    count = grad_gate.shape[0] // 4
    depth, width = w_gate.shape
    size = 256
    rows = pl.BlockSpec((2 * count, width), lambda i: (side, 0))
    weights = pl.BlockSpec((size, width), lambda i: (i, 0))
    outs = pl.BlockSpec((count, size), lambda i: (0, i))
    return pl.pallas_call(
        feed_back_kernel,
        grid=(depth // size,),
        out_shape=(jax.ShapeDtypeStruct((count, depth), jnp.bfloat16),) * 2,
        in_specs=[rows, rows, weights, weights],
        out_specs=(outs, outs),
        compiler_params=params(60),
        cost_estimate=LITTLE,
        name="feed_back",
    )(grad_gate, grad_up, w_gate, w_up)


def feed_down_kernel(hidden, w_down, own, across, others):
    total = nn(hidden[...], w_down[...]).astype(jnp.bfloat16)
    count = own.shape[0]
    own[...] = total[:count]
    others[:count] = total[count : 2 * count]
    across[...] = total[2 * count : 3 * count]
    others[count:] = total[3 * count :]


def feed_down(hidden, w_down):
    count = hidden.shape[0] // 4
    width, depth = w_down.shape
    size = 512
    block = pl.BlockSpec((count, size), lambda i: (0, i))
    return pl.pallas_call(
        feed_down_kernel,
        grid=(depth // size,),
        out_shape=(jax.ShapeDtypeStruct((count, depth), jnp.bfloat16),) * 2
        + (jax.ShapeDtypeStruct((2 * count, depth), jnp.bfloat16),),
        in_specs=[
            pl.BlockSpec((4 * count, width), lambda i: (0, 0)),
            pl.BlockSpec((width, size), lambda i: (0, i)),
        ],
        out_specs=(block, block, pl.BlockSpec((2 * count, size), lambda i: (0, i))),
        compiler_params=params(60),
        cost_estimate=LITTLE,
        name="feed_down",
    )(hidden, w_down)


def to_core(values):
    return lax.ppermute(values, "row", SWAP)


def to_chip(values):
    return lax.ppermute(values, "col", SWAP)


def gather_blocks(own):
    across = to_chip(own)
    return own, to_core(own), across, to_core(across)


def scatter_far(across, diagonal):
    return to_chip((across + to_core(diagonal)).astype(jnp.bfloat16))


def pick(values, index, axis):
    return lax.dynamic_index_in_dim(values, index, axis, keepdims=False)


def add_up(terms):
    total = terms[0].astype(jnp.float32)
    for term in terms[1:]:
        total = total + term.astype(jnp.float32)
    return total


def local_for(dp):
    def local(
        tokens,
        segments,
        attn_gain,
        w_query,
        w_key,
        w_value,
        w_out,
        ffn_gain,
        w_gate,
        w_up,
        w_down,
        out_cotangent,
    ):
        query_width = w_query.shape[1]
        kv_width = w_key.shape[1]
        length = segments.shape[1]
        row, col = lax.axis_index("row"), lax.axis_index("col")
        places = [
            (((block // 2) ^ row) + 2 * ((block % 2) ^ col)) * (length // 4) for block in range(4)
        ]
        places = jnp.stack(places + [col]).astype(jnp.int32)

        inputs = tokens.astype(jnp.float32)
        inverse_one = lax.rsqrt(jnp.mean(inputs * inputs, axis=-1, keepdims=True) + EPSILON)
        unit_one = inputs * inverse_one
        normed_one = (unit_one * attn_gain).astype(jnp.bfloat16)
        across_one = to_chip(normed_one)
        beside_one = to_core(normed_one)
        qkv_weight = jnp.concatenate([w_query, w_key, w_value], axis=1)
        cosine, sine = rope_tables(positions(segments).reshape(length))
        seg_row = segments.reshape(1, length)
        near = nn(jnp.concatenate([normed_one, beside_one], axis=0), qkv_weight)
        across_one, near, cot, cosine, sine, units = sync(
            across_one, near, out_cotangent, cosine, sine, unit_table(dp)
        )
        across_cot = to_chip(cot)
        beside_cot = to_core(cot)
        diagonal_one = to_core(across_one)
        blocks_one = (normed_one, beside_one, across_one, diagonal_one)
        far_mixed, rotated, far_logs, out_across, out_diagonal = attend_far(
            places, near, across_one, diagonal_one, qkv_weight, w_out, cosine, sine, seg_row
        )
        out_across, out_diagonal, rotated, across_cot, beside_cot = sync(
            out_across, out_diagonal, rotated, across_cot, beside_cot
        )
        out_diagonal = to_core(out_diagonal)
        out_across, out_diagonal, rotated, across_cot = sync(
            out_across, out_diagonal, rotated, across_cot
        )
        diagonal_cot = to_core(across_cot)
        far_out = to_chip((out_across + out_diagonal).astype(jnp.bfloat16))
        near_mixed, near_logs, out_own, out_beside = attend_near(
            places, rotated, w_out, seg_row
        )
        far_out, out_own, out_beside, diagonal_cot = sync(
            far_out, out_own, out_beside, diagonal_cot
        )
        cots = (out_cotangent, beside_cot, across_cot, diagonal_cot)
        out_beside = to_core(out_beside)
        middle = add_up([inputs, out_own, out_beside, far_out])
        inverse_two = lax.rsqrt(jnp.mean(middle * middle, axis=-1, keepdims=True) + EPSILON)
        unit_two = middle * inverse_two
        normed_two = (unit_two * ffn_gain).astype(jnp.bfloat16)
        across_two = to_chip(normed_two)
        beside_two = to_core(normed_two)
        mixed = jnp.concatenate([near_mixed, far_mixed], axis=0)
        *parts, back_own, back_beside = feed_near(
            (normed_two, beside_two), cots[:2], w_gate, w_up, w_down
        )
        parts, across_two, mixed, back_own, back_beside = sync(
            parts, across_two, mixed, back_own, back_beside
        )
        diagonal_two = to_core(across_two)
        back_beside = to_core(back_beside)
        blocks_two = (normed_two, beside_two, across_two, diagonal_two)
        gate = DpSum(blocks_two, None, (1, 2, 4), dp, units)
        down = DpSum(cots, None, (2, 1, 4), dp, units)
        hidden, grad_gate, grad_up, gate_early, down_early = feed_far(
            units, blocks_two, cots, w_gate, w_up, w_down, parts
        )
        gate_early, down_early, grad_gate, grad_up, hidden, back_beside = sync(
            gate_early, down_early, grad_gate, grad_up, hidden, back_beside
        )

        gate.right, down.right = grad_gate, hidden
        up = DpSum(blocks_two, grad_up, (1, 2, 4), dp, units)
        gate_early = gate.send(gate_early, 0)
        down_early = down.send(down_early, 0)
        far_across, far_diagonal = feed_back(1, grad_gate, grad_up, w_gate, w_up)
        far_diagonal = to_core(far_diagonal)
        gate_late, down_late = weight_pair((gate, down), 2, 2)
        back_far = (far_across + far_diagonal).astype(jnp.bfloat16)
        gate_early, down_early, back_far, gate_late, down_late, gate.right, down.right, up.right = sync(
            gate_early, down_early, back_far, gate_late, down_late, grad_gate, hidden, grad_up
        )

        gate_late = gate.send(gate_late, 0)
        down_late = down.send(down_late, 0)
        back_far = to_chip(back_far)
        gate_keep, down_keep = weight_pair((gate, down), 4, 4)
        gate_middle = gate.second(gate_keep, gate_early)
        down_middle = down.second(down_keep, down_early)
        down_own, down_across, down_others = feed_down(down.right, w_down)
        (
            gate_late, down_late, back_far, gate_middle, down_middle, up.right, down_own, down_across,
            down_others,
        ) = sync(
            gate_late, down_late, back_far, gate_middle, down_middle, up.right, down_own, down_across,
            down_others,
        )

        gate_middle = gate.send(gate_middle, 1)
        down_middle = down.send(down_middle, 1)
        grad_middle, from_own, gain_two_grad = row_call(
            middle_back,
            (middle, out_cotangent, back_own, back_beside, back_far),
            (ffn_gain,),
            (jnp.float32, jnp.bfloat16),
            1,
        )
        from_across = to_chip(from_own)
        from_beside = to_core(from_own)
        up_whole, up_keep = up.whole_and_keep()
        down_others = to_core(down_others)
        down_far = (down_across + down_others[BLOCK:]).astype(jnp.bfloat16)
        (
            gate_middle, down_middle, from_across, from_beside, up_whole, up_keep, down_others, down_far,
        ) = sync(
            gate_middle, down_middle, from_across, from_beside, up_whole, up_keep, down_others, down_far
        )

        up_whole = up.send(up_whole, 0)
        gate_end = gate.third(gate_keep, gate_late, gate_middle)
        gate_end, from_across, down_keep = sync(gate_end, from_across, down_keep)
        gate_end = gate.send(gate_end, 2)
        from_diagonal = to_core(from_across)
        down_end = down.third(down_keep, down_late, down_middle)
        half = BLOCK // 2
        down_end, from_diagonal = sync((down_end[:half], down_end[half:]), from_diagonal)
        down_ends = down.send(down_end[0], 2)
        down_far = to_chip(down_far)
        grad_attn = (from_own, from_beside, from_across, from_diagonal)
        out = DpSum(grad_attn, mixed, (2, 1, 4), dp, units)
        out_whole = out.send(out.whole(), 0)
        grad_qkv, back_own, back_across, back_others = attend_back(
            places, rotated, near_logs, far_logs, cosine, sine, seg_row, w_out, qkv_weight, grad_attn
        )
        qkv = DpSum(blocks_one, grad_qkv, (1, 2, 4), dp, units)
        qkv_early, qkv_late = qkv.halves()
        gain_one_grad = sum(
            jnp.sum(part.astype(jnp.float32) * block.astype(jnp.float32), axis=0)
            for part, block in zip(
                (back_own, back_others[:BLOCK], back_across, back_others[BLOCK:]), blocks_one
            )
        )
        gains = jnp.stack([gain_one_grad / attn_gain, gain_two_grad[0]])
        (
            up_whole, gate_end, down_ends, out_whole, qkv_early, qkv_late, qkv.right, back_own,
            back_across, back_others, down_far, gains, out.right, down_end,
        ) = sync(
            up_whole, gate_end, down_ends, out_whole, qkv_early, qkv_late, grad_qkv, back_own,
            back_across, back_others, down_far, gains, mixed, down_end[1],
        )

        qkv_early = qkv.send(qkv_early, 0)
        down_end = down.send(down_end, 2)
        up_first = up.second_unit(0, up_keep, up_whole)
        up_first, up_keep, back_others, gains, out.right, qkv.right = sync(
            up_first, up_keep, back_others, gains, out.right, qkv.right
        )
        up_first = up.send(up_first, 1)
        others = to_core(back_others)
        gains_there = to_core(gains)
        up_second = up.second_unit(1, up_keep, up_whole)
        out_keep, qkv_keep = out.keep(), qkv.keep()
        both = jnp.concatenate([qkv_late, out.second(out_keep, out_whole)], axis=2)
        one_far = (back_across + others[BLOCK:]).astype(jnp.bfloat16)
        (
            qkv_early, up_first, others, gains, up_second, out_keep, qkv_keep, both, one_far, down_end,
        ) = sync(
            qkv_early, up_first, others, gains + gains_there, up_second, out_keep, qkv_keep, both,
            one_far, down_end,
        )

        both = qkv.send(both, 0)
        one_far = to_chip(one_far)
        gains_there = to_chip(gains)
        up_end = up.third(up_keep, up_whole, up_first)
        qkv_middle = qkv.second(qkv_keep, qkv_early)
        up_end, qkv_middle, gate_end, down_end, down_far = sync(
            up_end, qkv_middle, gate_end, down_end, down_far
        )
        up_end = up.send(up_end, 2)
        qkv_middle = qkv.send(qkv_middle, 1)
        gate_grad = gate.finish(gate_keep, gate_late, gate_middle, gate_end)
        down_grad = down.finish(
            down_keep, down_late, down_middle, down_ends, down_end, turned=True
        )
        (output,) = row_call(
            add_output, (middle, down_own, down_others, down_far), (), (jnp.bfloat16,)
        )
        (
            up_end, qkv_middle, both, one_far, gains, gate_grad, down_grad, up_second, output,
        ) = sync(
            up_end, qkv_middle, both, one_far, gains + gains_there, gate_grad, down_grad, up_second,
            output,
        )
        width = qkv_weight.shape[1]
        qkv_late, out_middle = both[:, :, :width], both[:, :, width:]

        up_second = up.send(up_second, 1)
        ends = jnp.concatenate(
            [
                qkv.third(qkv_keep, qkv_late, qkv_middle),
                out.third(out_keep, out_whole, out_middle),
            ],
            axis=1,
        )
        ends, gains, one_far = sync(ends, gains, one_far)
        ends = qkv.send(ends, 2)
        gains_there = exchange(gains, dp, 1)
        (input_grad,) = row_call(
            input_back,
            (tokens, grad_middle, back_own, others, one_far),
            (attn_gain,),
            (jnp.float32,),
        )
        up_grad = up.finish(up_keep, up_whole, up_second, up_end)
        ends, gains, input_grad, up_grad = sync(ends, gains + gains_there, input_grad, up_grad)
        step = 2
        while step < dp:
            gains = gains + exchange(gains, dp, step)
            step *= 2
        qkv_grad = qkv.finish(qkv_keep, qkv_late, qkv_middle, ends[:, :width])
        out_grad = out.finish(out_keep, out_whole, out_middle, ends[:, width:], turned=True)
        key_end = query_width + kv_width
        return (
            output,
            input_grad,
            gains[0],
            qkv_grad[:, :query_width],
            qkv_grad[:, query_width:key_end],
            qkv_grad[:, key_end:],
            out_grad,
            gains[1],
            gate_grad,
            up_grad,
            down_grad,
        )

    return local


def solution(mesh):
    rows = P(("dp", "row", "col"), None)
    columns = P(None, ("row", "col"))
    placed = (
        rows,
        P("dp", None),
        P(),
        columns,
        columns,
        columns,
        P(("row", "col"), None),
        P(),
        columns,
        columns,
        P(("row", "col"), None),
        rows,
    )
    summed = P("dp", ("row", "col"))
    turned = P(("row", "col"), "dp")
    return jax.shard_map(
        local_for(mesh.shape["dp"]),
        mesh=mesh,
        in_specs=placed,
        out_specs=(rows, rows, P(), summed, summed, summed, turned, P(), summed, summed, turned),
        check_vma=False,
    )
```

```python
import jax
import jax.numpy as jnp
from jax import lax
from jax.experimental import pallas as pl
from jax.experimental.pallas import tpu as pltpu
from jax.sharding import PartitionSpec as P

HD = 64
EPSILON = 1e-05
MASKED_SCORE = -1e30
BLOCK = 256
TILE = 128
SWAP = ((0, 1), (1, 0))


def positions(segment_ids):
    indices = jnp.arange(segment_ids.shape[-1], dtype=jnp.int32)
    previous = jnp.concatenate([segment_ids[..., :1] - 1, segment_ids[..., :-1]], axis=-1)
    starts = jnp.where(segment_ids != previous, indices, 0)
    return indices - lax.cummax(starts, axis=segment_ids.ndim - 1)


def rope_tables(position):
    exponent = jnp.arange(HD // 2, dtype=jnp.float32) * (-2.0 / HD)
    angles = position.astype(jnp.float32)[:, None] * (10000.0**exponent)[None, :]
    cosine, sine = jnp.cos(angles), jnp.sin(angles)
    return (
        jnp.concatenate([cosine] * 4, axis=1),
        jnp.concatenate([-sine, sine, -sine, sine], axis=1),
    )


def nt(left, right):
    return lax.dot_general(
        left, right, (((1,), (1,)), ((), ())), preferred_element_type=jnp.float32
    )


def nn(left, right):
    return lax.dot_general(
        left, right, (((1,), (0,)), ((), ())), preferred_element_type=jnp.float32
    )


def tn(left, right):
    return lax.dot_general(
        left, right, (((0,), (0,)), ((), ())), preferred_element_type=jnp.float32
    )


def lane_marks():
    lane = lax.broadcasted_iota(jnp.int32, (BLOCK, TILE), 1)
    return lane, lane < HD, lane % HD < HD // 2


def turn_by(values, cosine, sine, first):
    turned = jnp.where(
        first, pltpu.roll(values, TILE - HD // 2, 1), pltpu.roll(values, HD // 2, 1)
    )
    return values * cosine + turned * sine


def rows_of(places, block):
    return pl.ds(pl.multiple_of(places[block], BLOCK), BLOCK)


def segment_column(seg_row, at):
    return jnp.broadcast_to(seg_row[:, at], (TILE, BLOCK)).T


def attend_block(block, places, rotated, keys, values, seg_row, mixed, target, log_sums):
    width = mixed.shape[1]
    lane, low, _ = lane_marks()
    rows = rows_of(places, block)
    at = slice(block * BLOCK, (block + 1) * BLOCK)
    begin = max(0, block - 2) * BLOCK
    span = slice(begin, (block + 1) * BLOCK)
    count = (block + 1) * BLOCK - begin
    key_at = begin + lax.broadcasted_iota(jnp.int32, (BLOCK, count), 1)
    query_at = block * BLOCK + lax.broadcasted_iota(jnp.int32, (BLOCK, count), 0)
    seg_col = segment_column(seg_row, at)[:, :1]
    allowed = (seg_col == seg_row[:, span]) & (key_at <= query_at)
    bias = jnp.where(allowed, 0.0, MASKED_SCORE)
    key_span = keys[span]
    value_span = values[span]

    def one_pair(number, logs):
        columns = pl.ds(pl.multiple_of(number * TILE, TILE), TILE)
        query = rotated[rows, columns]
        results = []
        for half in range(2):
            chosen = jnp.where(low if half == 0 else ~low, query, jnp.zeros_like(query))
            scores = nt(chosen, key_span) + bias
            largest = jnp.max(scores, axis=1, keepdims=True)
            shifted = jnp.exp(scores - largest)
            total = jnp.sum(shifted, axis=1, keepdims=True)
            results.append(nn(shifted.astype(jnp.bfloat16), value_span) * (1.0 / total))
            logs = jnp.where(lane == 2 * number + half, largest + jnp.log(total), logs)
        mixed[target, columns] = jnp.where(low, results[0], results[1]).astype(jnp.bfloat16)
        return logs

    logs = lax.fori_loop(0, width // TILE, one_pair, jnp.zeros((BLOCK, TILE), jnp.float32))
    log_sums[:, at] = logs.T[: log_sums.shape[0]]


def key_value_rows(rotated, rows, keys, values, at, low):
    width = rotated.shape[1] - TILE
    pair = rotated[rows, width:].astype(jnp.float32)
    swapped = pltpu.roll(pair, HD, 1)
    keys[at] = jnp.where(low, pair, swapped).astype(jnp.bfloat16)
    values[at] = jnp.where(low, swapped, pair).astype(jnp.bfloat16)


def attend_side(side, places, rotated, keys, values, seg_row, mixed, log_sums):
    blocks = rotated.shape[0] // BLOCK
    for parity in range(2):

        @pl.when((places[blocks] ^ side) == parity)
        def _():
            for block in range(parity, blocks, 2):
                start = places[block] - side * 2 * BLOCK
                target = pl.ds(pl.multiple_of(start, BLOCK), BLOCK)
                attend_block(
                    block, places, rotated, keys, values, seg_row, mixed, target, log_sums
                )


def attend_far_kernel(
    places, near, across, diagonal, weight, w_out, cosine, sine, seg_row,
    mixed, rotated, log_sums, out_across, out_diagonal, keys, values,
):
    length, total = rotated.shape
    width = total - TILE
    blocks = length // BLOCK
    _, low, first = lane_marks()
    for block in range(blocks):
        rows = rows_of(places, block)
        at = slice(block * BLOCK, (block + 1) * BLOCK)

        def turn_all(proj):
            for start in range(0, width, TILE):
                query = turn_by(proj[:, start : start + TILE], cosine[at], sine[at], first)
                rotated[rows, start : start + TILE] = (query * HD ** (-0.5)).astype(jnp.bfloat16)
            pair = proj[:, width:]
            turned = jnp.where(low, turn_by(pair, cosine[at], sine[at], first), pair)
            rotated[rows, width:] = turned.astype(jnp.bfloat16)

        for piece, source in ((0, None), (1, None), (2, across), (3, diagonal)):

            @pl.when(places[block] == piece * BLOCK)
            def _(piece=piece, source=source):
                if source is None:
                    turn_all(near[piece * BLOCK : (piece + 1) * BLOCK])
                else:
                    turn_all(nn(source[...], weight[...]))

        key_value_rows(rotated, rows, keys, values, at, low)
    attend_side(1, places, rotated, keys, values, seg_row, mixed, log_sums)
    out_diagonal[...] = nn(mixed[BLOCK:], w_out[...]).astype(jnp.bfloat16)
    out_across[...] = nn(mixed[:BLOCK], w_out[...]).astype(jnp.bfloat16)


def attend_near_kernel(
    places, rotated, w_out, seg_row, mixed, log_sums, out_own, out_beside, keys, values
):
    blocks = rotated.shape[0] // BLOCK
    _, low, _ = lane_marks()
    for block in range(blocks):
        at = slice(block * BLOCK, (block + 1) * BLOCK)
        key_value_rows(rotated, rows_of(places, block), keys, values, at, low)
    attend_side(0, places, rotated, keys, values, seg_row, mixed, log_sums)
    out_beside[...] = nn(mixed[BLOCK:], w_out[...]).astype(jnp.bfloat16)
    out_own[...] = nn(mixed[:BLOCK], w_out[...]).astype(jnp.bfloat16)


def attend_back_kernel(
    places, rotated, near_logs, far_logs, cosine, sine, seg_row, w_out, weight,
    from_own, from_beside, from_across, from_diagonal,
    grads, back_own, back_across, back_others,
    keys, values, key_sum, value_sum, grad_mixed, seg_col,
):
    length = rotated.shape[0]
    width = grad_mixed.shape[1]
    blocks = length // BLOCK
    _, low, first = lane_marks()
    for piece, source in enumerate((from_own, from_beside, from_across, from_diagonal)):
        grad_mixed[piece * BLOCK : (piece + 1) * BLOCK] = nt(source[...], w_out[...]).astype(
            jnp.bfloat16
        )
    key_sum[...] = jnp.zeros_like(key_sum)
    value_sum[...] = jnp.zeros_like(value_sum)
    for block in range(blocks):
        at = slice(block * BLOCK, (block + 1) * BLOCK)
        key_value_rows(rotated, rows_of(places, block), keys, values, at, low)
        seg_col[at] = segment_column(seg_row, at)
    def block_back(block, begin):
        rows = rows_of(places, block)
        at = slice(block * BLOCK, (block + 1) * BLOCK)
        is_near = places[blocks] == block % 2
        span = slice(begin, (block + 1) * BLOCK)
        count = (block + 1) * BLOCK - begin
        key_at = begin + lax.broadcasted_iota(jnp.int32, (count, BLOCK), 0)
        query_at = block * BLOCK + lax.broadcasted_iota(jnp.int32, (count, BLOCK), 1)
        allowed = (seg_col[span, :1] == seg_row[:, at]) & (key_at <= query_at)
        bias = jnp.where(allowed, 0.0, MASKED_SCORE)
        key_span = keys[span]
        value_span = values[span]

        def one_pair(number, carry):
            columns = pl.ds(pl.multiple_of(number * TILE, TILE), TILE)
            query = rotated[rows, columns]
            grad = grad_mixed[rows, columns]
            results = []
            for half in range(2):
                side = low if half == 0 else ~low
                chosen = jnp.where(side, query, jnp.zeros_like(query))
                chosen_grad = jnp.where(side, grad, jnp.zeros_like(grad))
                head = pl.ds(2 * number + half, 1)
                logs = jnp.where(is_near, near_logs[head, at], far_logs[head, at])
                probs = jnp.exp(nt(key_span, chosen) + bias - logs)
                grad_probs = nt(value_span, chosen_grad)
                inner = jnp.sum(probs * grad_probs, axis=0, keepdims=True)
                grad_scores = (probs * (grad_probs - inner)).astype(jnp.bfloat16)
                value_sum[span] += nn(probs.astype(jnp.bfloat16), chosen_grad)
                key_sum[span] += nn(grad_scores, chosen)
                results.append(tn(grad_scores, key_span))
            grad_query = jnp.where(low, results[0], results[1]) * HD ** (-0.5)
            grads[rows, columns] = turn_by(grad_query, cosine[at], -sine[at], first).astype(
                jnp.bfloat16
            )
            return carry

        lax.fori_loop(0, width // TILE, one_pair, 0)
    for block in range(blocks):
        if block < 2:
            block_back(block, 0)
            continue
        for back in (1, 2):

            @pl.when(places[blocks - 1 + block] == back - 1)
            def _(block=block, back=back):
                block_back(block, (block - back) * BLOCK)

    for block in range(blocks):
        rows = rows_of(places, block)
        at = slice(block * BLOCK, (block + 1) * BLOCK)
        grad_key = key_sum[at]
        grad_key = turn_by(grad_key + pltpu.roll(grad_key, HD, 1), cosine[at], -sine[at], first)
        grad_value = value_sum[at]
        grad_value = grad_value + pltpu.roll(grad_value, HD, 1)
        grads[rows, width:] = jnp.where(low, grad_key, grad_value).astype(jnp.bfloat16)
    targets = (back_own, back_others.at[:BLOCK], back_across, back_others.at[BLOCK:])
    for piece, target in enumerate(targets):
        grad_rows = grads[piece * BLOCK : (piece + 1) * BLOCK]
        target[...] = nt(grad_rows, weight[...]).astype(jnp.bfloat16)


SMEM = pl.BlockSpec(memory_space=pltpu.SMEM)
VMEM = pl.BlockSpec(memory_space=pltpu.VMEM)


ANY = pl.BlockSpec(memory_space=pl.ANY)
LITTLE = pl.CostEstimate(flops=1 << 20, bytes_accessed=1 << 12, transcendentals=0)


def params(limit):
    return pltpu.CompilerParams(vmem_limit_bytes=limit << 20)


def attend_far(places, near, across, diagonal, weight, w_out, cosine, sine, seg_row):
    length, total = 2 * near.shape[0], near.shape[1]
    width = total - TILE
    depth = w_out.shape[1]
    block = jax.ShapeDtypeStruct((BLOCK, depth), jnp.bfloat16)
    return pl.pallas_call(
        attend_far_kernel,
        out_shape=(
            jax.ShapeDtypeStruct((length // 2, width), jnp.bfloat16),
            jax.ShapeDtypeStruct((length, total), jnp.bfloat16),
            jax.ShapeDtypeStruct((width // HD, length), jnp.float32),
            block,
            block,
        ),
        in_specs=[SMEM] + [VMEM] * 8,
        out_specs=(VMEM,) * 5,
        scratch_shapes=[pltpu.VMEM((length, TILE), jnp.bfloat16)] * 2,
        compiler_params=params(48),
        cost_estimate=LITTLE,
        name="attend_far",
    )(places, near, across, diagonal, weight, w_out, cosine, sine, seg_row)


def attend_near(places, rotated, w_out, seg_row):
    length, total = rotated.shape
    width = total - TILE
    depth = w_out.shape[1]
    block = jax.ShapeDtypeStruct((BLOCK, depth), jnp.bfloat16)
    return pl.pallas_call(
        attend_near_kernel,
        out_shape=(
            jax.ShapeDtypeStruct((length // 2, width), jnp.bfloat16),
            jax.ShapeDtypeStruct((width // HD, length), jnp.float32),
            block,
            block,
        ),
        in_specs=[SMEM] + [VMEM] * 3,
        out_specs=(VMEM,) * 4,
        scratch_shapes=[pltpu.VMEM((length, TILE), jnp.bfloat16)] * 2,
        compiler_params=params(48),
        cost_estimate=LITTLE,
        name="attend_near",
    )(places, rotated, w_out, seg_row)


def attend_back(
    places, rotated, near_logs, far_logs, cosine, sine, seg_row, w_out, weight, pieces
):
    length, total = rotated.shape
    return pl.pallas_call(
        attend_back_kernel,
        out_shape=(jax.ShapeDtypeStruct((length, total), jnp.bfloat16),)
        + (jax.ShapeDtypeStruct(pieces[0].shape, jnp.bfloat16),) * 2
        + (jax.ShapeDtypeStruct((2 * BLOCK, pieces[0].shape[1]), jnp.bfloat16),),
        in_specs=[SMEM] + [VMEM] * 12,
        out_specs=(VMEM,) * 4,
        scratch_shapes=[pltpu.VMEM((length, TILE), jnp.bfloat16)] * 2
        + [pltpu.VMEM((length, TILE), jnp.float32)] * 2
        + [
            pltpu.VMEM((length, total - TILE), jnp.bfloat16),
            pltpu.VMEM((length, TILE), jnp.int32),
        ],
        compiler_params=params(52),
        cost_estimate=LITTLE,
        name="attend_back",
    )(
        places, rotated, near_logs, far_logs, cosine, sine, seg_row, w_out, weight, *pieces
    )


def terms_kernel(starts, units, one, two, three, four, right, *outs):
    left = jnp.concatenate([one[...], two[...], three[...], four[...]], axis=0)
    total = tn(left, right[...]).astype(jnp.bfloat16)
    step = pl.program_id(0)
    for out, start, end in zip(outs, starts, starts[1:]):

        @pl.when((step >= start) & (step < end))
        def _(out=out):
            out[0] = total


def weight_terms(pieces, right, units, first, sizes):
    count = pieces[0].shape[0]
    rows, width = right.shape
    starts = [sum(sizes[:number]) for number in range(len(sizes) + 1)]
    return pl.pallas_call(
        lambda *refs: terms_kernel(starts, *refs),
        grid_spec=pltpu.PrefetchScalarGridSpec(
            num_scalar_prefetch=1,
            grid=(starts[-1],),
            in_specs=[pl.BlockSpec((count, BLOCK), lambda i, units: (0, units[first + i]))] * 4
            + [pl.BlockSpec((rows, width), lambda i, units: (0, 0))],
            out_specs=[
                pl.BlockSpec(
                    (1, BLOCK, width),
                    lambda i, units, start=start, size=size: (
                        jnp.clip(i - start, 0, size - 1),
                        0,
                        0,
                    ),
                )
                for start, size in zip(starts, sizes)
            ],
        ),
        out_shape=[jax.ShapeDtypeStruct((size, BLOCK, width), jnp.bfloat16) for size in sizes],
        compiler_params=params(60),
        cost_estimate=LITTLE,
        name="weight_terms",
    )(units, *pieces, right)


def pair_kernel(each, units, *refs):
    left, right, outs = refs[:8], refs[8:10], refs[10:]
    for number, out in enumerate(outs):

        @pl.when(pl.program_id(0) // each == number)
        def _(number=number, out=out):
            pieces = [ref[...] for ref in left[4 * number : 4 * number + 4]]
            total = tn(jnp.concatenate(pieces, axis=0), right[number][...])
            out[0] = total.astype(jnp.bfloat16)


def weight_pair(sums, first, size):
    count = sums[0].pieces[0].shape[0]
    rows, width = sums[0].right.shape

    def step(i, number):
        return jnp.clip(i - number * size, 0, size - 1)

    specs = []
    for number, each in enumerate(sums):
        specs += [
            pl.BlockSpec(
                (count, BLOCK),
                lambda i, units, number=number, start=each.base + first: (
                    0,
                    units[start + step(i, number)],
                ),
            )
        ] * 4
    return pl.pallas_call(
        lambda *refs: pair_kernel(size, *refs),
        grid_spec=pltpu.PrefetchScalarGridSpec(
            num_scalar_prefetch=1,
            grid=(2 * size,),
            in_specs=specs + [pl.BlockSpec((rows, width), lambda i, units: (0, 0))] * 2,
            out_specs=[
                pl.BlockSpec(
                    (1, BLOCK, width), lambda i, units, number=number: (step(i, number), 0, 0)
                )
                for number in range(2)
            ],
        ),
        out_shape=[jax.ShapeDtypeStruct((size, BLOCK, width), jnp.bfloat16)] * 2,
        compiler_params=params(60),
        cost_estimate=LITTLE,
        name="weight_pair",
    )(sums[0].units, *sums[0].pieces, *sums[1].pieces, sums[0].right, sums[1].right)


def exchange(values, dp, distance):
    return lax.ppermute(values, "dp", [(device, device ^ distance) for device in range(dp)])


def numbered(bits, values, free):
    fixed = jnp.zeros((), jnp.int32)
    for bit, value in zip(bits, values):
        fixed = fixed + bit * value
    numbers = [fixed]
    for bit in free:
        numbers = [number + add for number in numbers for add in (0, bit)]
    return jnp.stack(numbers).astype(jnp.int32)


ORDERS = ((1, 2, 4), (2, 1, 4))


def unit_table(dp):
    unit = lax.axis_index("dp") // (dp // 8)
    numbers = []
    for order in ORDERS:
        one, two, three = ((unit // bit) % 2 for bit in order)
        numbers += [
            sum(bit * value for bit, value in zip(order, values))
            for values in (
                (first, second, third)
                for first in (1 - one, one)
                for second in (1 - two, two)
                for third in (1 - three, three)
            )
        ]
    return jnp.stack(numbers).astype(jnp.int32)


class DpSum:
    def __init__(self, pieces, right, order, dp, units):
        self.pieces, self.right, self.order, self.dp, self.units = pieces, right, order, dp, units
        self.base = 8 * ORDERS.index(order)

    def terms(self, first, *sizes):
        return weight_terms(self.pieces, self.right, self.units, self.base + first, sizes)

    def whole(self):
        return self.terms(0, 4)[0]

    def halves(self):
        return self.terms(0, 2, 2)

    def keep(self):
        return self.terms(4, 4)[0]

    def whole_and_keep(self):
        return self.terms(0, 4, 4)

    def send(self, values, step):
        return exchange(values, self.dp, self.order[step] * (self.dp // 8))

    def second(self, keep, early):
        return add_up([keep[:2], early[:2]]).astype(jnp.bfloat16)

    def second_unit(self, number, keep, early):
        return add_up([keep[number : number + 1], early[number : number + 1]]).astype(jnp.bfloat16)

    def third(self, keep, late, middle):
        at = late.shape[0] - 2
        return add_up([keep[2], late[at], middle[0]]).astype(jnp.bfloat16)

    def finish(self, keep, late, middle, *ends, turned=False):
        if self.dp == 8:
            return finish_sum(keep, late, middle, ends, turned)
        total = finish_sum(keep, late, middle, ends, False)
        index, left = lax.axis_index("dp"), self.dp // 8
        while left > 1:
            left //= 2
            bit = (index // left) % 2
            parts = total.reshape(2, total.shape[0] // 2, total.shape[1])
            there = exchange(pick(parts, 1 - bit, 0).astype(jnp.bfloat16), self.dp, left)
            total = pick(parts, bit, 0) + there.astype(jnp.float32)
        return total.T if turned else total


def finish_kernel(turned, ends, keep, late, middle, *refs):
    out = refs[-1]
    end = refs[0][...].astype(jnp.float32)
    if ends == 2:
        end = jnp.where(pl.program_id(0) == 0, end, refs[1][...].astype(jnp.float32))
    total = keep[0].astype(jnp.float32) + late[0].astype(jnp.float32)
    total = total + middle[0].astype(jnp.float32) + end
    out[...] = total.T if turned else total


def finish_sum(keep, late, middle, ends, turned):
    _, rows, columns = keep.shape
    size = rows // 2
    specs = [
        pl.BlockSpec((1, size, columns), lambda i, at=array.shape[0] - 1: (at, i, 0))
        for array in (keep, late, middle)
    ]
    end = pl.BlockSpec((size, columns), lambda i: (0 if len(ends) == 2 else i, 0))
    shape = (columns, rows) if turned else (rows, columns)
    out = (
        pl.BlockSpec((columns, size), lambda i: (0, i))
        if turned
        else pl.BlockSpec((size, columns), lambda i: (i, 0))
    )
    return pl.pallas_call(
        lambda *refs: finish_kernel(turned, len(ends), *refs),
        grid=(2,),
        in_specs=specs + [end] * len(ends),
        out_specs=out,
        out_shape=jax.ShapeDtypeStruct(shape, jnp.float32),
        compiler_params=params(40),
        cost_estimate=LITTLE,
        name="finish_sum",
    )(keep, late, middle, *ends)


def row_call(kernel, rows, wholes, outs, totals=0):
    count, depth = rows[0].shape
    size = 64
    block = pl.BlockSpec((size, depth), lambda i: (i, 0))
    whole = pl.BlockSpec((1, depth), lambda i: (0, 0))
    return pl.pallas_call(
        kernel,
        grid=(count // size,),
        in_specs=[block] * len(rows) + [whole] * len(wholes),
        out_specs=(block,) * len(outs) + (whole,) * totals,
        out_shape=tuple(jax.ShapeDtypeStruct((count, depth), kind) for kind in outs)
        + (jax.ShapeDtypeStruct((1, depth), jnp.float32),) * totals,
        compiler_params=params(40),
        cost_estimate=LITTLE,
        name=kernel.__name__,
    )(*rows, *(array.reshape(1, depth) for array in wholes))


def normalize_two(one, two, gain, *outs):
    for rows, out in zip((one, two), outs):
        values = rows[...].astype(jnp.float32)
        inverse = lax.rsqrt(jnp.mean(values * values, axis=-1, keepdims=True) + EPSILON)
        out[...] = (values * inverse * gain[...]).astype(jnp.bfloat16)


def scale_back(values, grads, gain):
    inverse = lax.rsqrt(jnp.mean(values * values, axis=-1, keepdims=True) + EPSILON)
    unit = values * inverse
    scaled = grads * gain
    return unit, inverse * (scaled - unit * jnp.mean(scaled * unit, axis=-1, keepdims=True))


def middle_back(middle, cot, one, two, three, gain, grad_middle, rounded, gain_grad):
    grads = one[...].astype(jnp.float32) + two[...].astype(jnp.float32) + three[...].astype(jnp.float32)
    unit, back = scale_back(middle[...], grads, gain[...])
    total = cot[...].astype(jnp.float32) + back
    grad_middle[...] = total
    rounded[...] = total.astype(jnp.bfloat16)

    @pl.when(pl.program_id(0) == 0)
    def _():
        gain_grad[...] = jnp.zeros_like(gain_grad)

    gain_grad[...] += jnp.sum(grads * unit, axis=0, keepdims=True)


def input_back(tokens, grad_middle, one, two, three, gain, input_grad):
    grads = one[...].astype(jnp.float32) + two[...].astype(jnp.float32) + three[...].astype(jnp.float32)
    _, back = scale_back(tokens[...].astype(jnp.float32), grads, gain[...])
    input_grad[...] = grad_middle[...] + back


def add_output(middle, one, two, three, output):
    total = middle[...] + one[...].astype(jnp.float32) + two[...].astype(jnp.float32)
    output[...] = (total + three[...].astype(jnp.float32)).astype(jnp.bfloat16)


def sync(*values):
    return lax.optimization_barrier(values)


def column_tiles(width, most=256):
    return [(at, min(most, width - at)) for at in range(0, width, most)]


def feed_near_kernel(one, two, cot_one, cot_two, w_gate, w_up, w_down, *rest):
    hidden, grad_gate, grad_up, back_one, back_two = rest[:5]
    rows, cots, gate, up, down, gates, ups, sems = rest[5:]
    sources = (one, two, w_gate, w_up, cot_one, cot_two, w_down)
    feed_steps(sources, rest[5:], hidden, grad_gate, grad_up)
    count = back_one.shape[0]
    for at, size in column_tiles(gate.shape[0]):
        span = slice(at, at + size)
        total = nt(grad_gate[...], gate[span]) + nt(grad_up[...], up[span])
        back_one[:, span] = total[:count].astype(jnp.bfloat16)
        back_two[:, span] = total[count:].astype(jnp.bfloat16)


def feed_far_kernel(units, one, two, cot_one, cot_two, w_gate, w_up, w_down, *rest):
    near_one, near_two, near_cot_one, near_cot_two, held_hidden, held_gate, _ = rest[:7]
    results, (gate_early, down_early) = rest[7:10], rest[10:12]
    near_rows, near_cots, near_hidden, near_gate, near_sems = rest[12:17]
    hidden, grad_gate, grad_up, out_sems = made = rest[17:21]
    scratch = rest[21:]
    rows, cots = scratch[:2]
    count = one.shape[0]
    moves = [
        pltpu.make_async_copy(held_hidden.at[: 2 * count], near_hidden, near_sems.at[0]),
        pltpu.make_async_copy(held_gate.at[: 2 * count], near_gate, near_sems.at[1]),
    ]
    lefts = (
        (near_one, near_rows, 0, 0),
        (near_two, near_rows, count, 0),
        (near_cot_one, near_cots, 0, 8),
        (near_cot_two, near_cots, count, 8),
    )
    for number, (source, target, start, first) in enumerate(lefts):
        for unit in range(2):
            columns = pl.ds(pl.multiple_of(units[first + unit] * BLOCK, BLOCK), BLOCK)
            moves.append(
                pltpu.make_async_copy(
                    source.at[:, columns],
                    target.at[unit, start : start + count],
                    near_sems.at[2 + 2 * number + unit],
                )
            )
    sources = (one, two, w_gate, w_up, cot_one, cot_two, w_down)
    feed_steps(sources, scratch, hidden, grad_gate, grad_up, moves)
    stores = [
        pltpu.make_async_copy(source, target.at[2 * count :], out_sems.at[number])
        for number, (source, target) in enumerate(zip(made[:3], results))
    ]
    for store in stores:
        store.start()
    for first, left, far_left, near_right, far_right, out in (
        (0, near_rows, rows, near_gate, grad_gate, gate_early),
        (8, near_cots, cots, near_hidden, hidden, down_early),
    ):
        for unit in range(2):
            columns = pl.ds(pl.multiple_of(units[first + unit] * BLOCK, BLOCK), BLOCK)
            total = tn(left[unit], near_right[...]) + tn(far_left[:, columns], far_right[...])
            out[unit] = total.astype(jnp.bfloat16)
    for store in stores:
        store.wait()


def feed_steps(sources, scratch, hidden, grad_gate, grad_up, more=()):
    rows, cots, gate, up, down, gates, ups, sems = scratch
    count = sources[0].shape[0]
    targets = (
        rows.at[:count], rows.at[count:], gate, up, cots.at[:count], cots.at[count:], down,
    )
    moves = [
        pltpu.make_async_copy(source, target, sems.at[number])
        for number, (source, target) in enumerate(zip(sources, targets))
    ]
    for move in (*moves, *more):
        move.start()
    for move in moves[:3]:
        move.wait()
    tiles = column_tiles(gate.shape[1])
    for at, size in tiles:
        gates[:, at : at + size] = nn(rows[...], gate[:, at : at + size])
    moves[3].wait()
    for at, size in tiles:
        ups[:, at : at + size] = nn(rows[...], up[:, at : at + size])
    for move in moves[4:]:
        move.wait()
    for at, size in tiles:
        span = slice(at, at + size)
        grad_hidden = nt(cots[...], down[span])
        gate_pre = gates[:, span]
        up_pre = ups[:, span]
        sigmoid = jax.nn.sigmoid(gate_pre)
        silu = gate_pre * sigmoid
        hidden[:, span] = (silu * up_pre).astype(jnp.bfloat16)
        slope = sigmoid + silu * (1.0 - sigmoid)
        grad_gate[:, span] = (grad_hidden * up_pre * slope).astype(jnp.bfloat16)
        grad_up[:, span] = (grad_hidden * silu).astype(jnp.bfloat16)
    for move in more:
        move.wait()


def feed_scratch(count, depth, width):
    return (
        [pltpu.VMEM((2 * count, depth), jnp.bfloat16)] * 2
        + [pltpu.VMEM((depth, width), jnp.bfloat16)] * 2
        + [
            pltpu.VMEM((width, depth), jnp.bfloat16),
            pltpu.VMEM((2 * count, width), jnp.float32),
            pltpu.VMEM((2 * count, width), jnp.float32),
            pltpu.SemaphoreType.DMA((7,)),
        ]
    )


def feed_near(pair, cots, w_gate, w_up, w_down):
    count, depth = pair[0].shape
    width = w_gate.shape[1]
    return pl.pallas_call(
        feed_near_kernel,
        grid=(1,),
        out_shape=(jax.ShapeDtypeStruct((4 * count, width), jnp.bfloat16),) * 3
        + (jax.ShapeDtypeStruct((count, depth), jnp.bfloat16),) * 2,
        in_specs=[ANY] * 7,
        out_specs=(pl.BlockSpec((2 * count, width), lambda i: (0, 0)),) * 3
        + (pl.BlockSpec((count, depth), lambda i: (0, 0)),) * 2,
        scratch_shapes=feed_scratch(count, depth, width),
        compiler_params=params(56),
        cost_estimate=LITTLE,
        name="feed_near",
    )(*pair, *cots, w_gate, w_up, w_down)


def feed_far(units, blocks, cots, w_gate, w_up, w_down, held):
    count, depth = blocks[0].shape
    width = w_gate.shape[1]
    early = jax.ShapeDtypeStruct((2, BLOCK, width), jnp.bfloat16)
    return pl.pallas_call(
        feed_far_kernel,
        grid_spec=pltpu.PrefetchScalarGridSpec(
            num_scalar_prefetch=1,
            grid=(1,),
            in_specs=[ANY] * 14,
            out_specs=(ANY,) * 3 + (pl.BlockSpec((2, BLOCK, width), lambda i, units: (0, 0, 0)),) * 2,
            scratch_shapes=[pltpu.VMEM((2, 2 * count, BLOCK), jnp.bfloat16)] * 2
            + [pltpu.VMEM((2 * count, width), jnp.bfloat16)] * 2
            + [pltpu.SemaphoreType.DMA((10,))]
            + [pltpu.VMEM((2 * count, width), jnp.bfloat16)] * 3
            + [pltpu.SemaphoreType.DMA((3,))]
            + feed_scratch(count, depth, width),
        ),
        out_shape=(jax.ShapeDtypeStruct((4 * count, width), jnp.bfloat16),) * 3 + (early,) * 2,
        input_output_aliases={12: 0, 13: 1, 14: 2},
        compiler_params=params(60),
        cost_estimate=LITTLE,
        name="feed_far",
    )(units, *blocks[2:], *cots[2:], w_gate, w_up, w_down, *blocks[:2], *cots[:2], *held)


def feed_back_kernel(grad_gate, grad_up, w_gate, w_up, one, two):
    total = nt(grad_gate[...], w_gate[...]) + nt(grad_up[...], w_up[...])
    total = total.astype(jnp.bfloat16)
    one[...] = total[: one.shape[0]]
    two[...] = total[one.shape[0] :]


def feed_back(side, grad_gate, grad_up, w_gate, w_up):
    count = grad_gate.shape[0] // 4
    depth, width = w_gate.shape
    size = 256
    rows = pl.BlockSpec((2 * count, width), lambda i: (side, 0))
    weights = pl.BlockSpec((size, width), lambda i: (i, 0))
    outs = pl.BlockSpec((count, size), lambda i: (0, i))
    return pl.pallas_call(
        feed_back_kernel,
        grid=(depth // size,),
        out_shape=(jax.ShapeDtypeStruct((count, depth), jnp.bfloat16),) * 2,
        in_specs=[rows, rows, weights, weights],
        out_specs=(outs, outs),
        compiler_params=params(60),
        cost_estimate=LITTLE,
        name="feed_back",
    )(grad_gate, grad_up, w_gate, w_up)


def feed_down_kernel(hidden, w_down, own, across, others):
    total = nn(hidden[...], w_down[...]).astype(jnp.bfloat16)
    count = own.shape[0]
    own[...] = total[:count]
    others[:count] = total[count : 2 * count]
    across[...] = total[2 * count : 3 * count]
    others[count:] = total[3 * count :]


def feed_down(hidden, w_down):
    count = hidden.shape[0] // 4
    width, depth = w_down.shape
    size = 512
    block = pl.BlockSpec((count, size), lambda i: (0, i))
    return pl.pallas_call(
        feed_down_kernel,
        grid=(depth // size,),
        out_shape=(jax.ShapeDtypeStruct((count, depth), jnp.bfloat16),) * 2
        + (jax.ShapeDtypeStruct((2 * count, depth), jnp.bfloat16),),
        in_specs=[
            pl.BlockSpec((4 * count, width), lambda i: (0, 0)),
            pl.BlockSpec((width, size), lambda i: (0, i)),
        ],
        out_specs=(block, block, pl.BlockSpec((2 * count, size), lambda i: (0, i))),
        compiler_params=params(60),
        cost_estimate=LITTLE,
        name="feed_down",
    )(hidden, w_down)


def to_core(values):
    return lax.ppermute(values, "row", SWAP)


def to_chip(values):
    return lax.ppermute(values, "col", SWAP)


def gather_blocks(own):
    across = to_chip(own)
    return own, to_core(own), across, to_core(across)


def scatter_far(across, diagonal):
    return to_chip((across + to_core(diagonal)).astype(jnp.bfloat16))


def pick(values, index, axis):
    return lax.dynamic_index_in_dim(values, index, axis, keepdims=False)


def add_up(terms):
    total = terms[0].astype(jnp.float32)
    for term in terms[1:]:
        total = total + term.astype(jnp.float32)
    return total


def local_for(dp):
    def local(
        tokens,
        segments,
        attn_gain,
        w_query,
        w_key,
        w_value,
        w_out,
        ffn_gain,
        w_gate,
        w_up,
        w_down,
        out_cotangent,
    ):
        query_width = w_query.shape[1]
        kv_width = w_key.shape[1]
        length = segments.shape[1]
        row, col = lax.axis_index("row"), lax.axis_index("col")
        places = [
            (((block // 2) ^ row) + 2 * ((block % 2) ^ col)) * (length // 4) for block in range(4)
        ]
        reaches = [
            segments[0, (block - 1) * BLOCK - 1] == segments[0, block * BLOCK]
            for block in range(2, length // BLOCK)
        ]
        places = jnp.stack([number.astype(jnp.int32) for number in places + [col] + reaches])

        across_raw = to_chip(tokens)
        inputs = tokens.astype(jnp.float32)
        inverse_one = lax.rsqrt(jnp.mean(inputs * inputs, axis=-1, keepdims=True) + EPSILON)
        unit_one = inputs * inverse_one
        normed_one = (unit_one * attn_gain).astype(jnp.bfloat16)
        beside_one = to_core(normed_one)
        qkv_weight = jnp.concatenate([w_query, w_key, w_value], axis=1)
        cosine, sine = rope_tables(positions(segments).reshape(length))
        seg_row = segments.reshape(1, length)
        near = nn(jnp.concatenate([normed_one, beside_one], axis=0), qkv_weight)
        across_raw, near, cot, cosine, sine, units = sync(
            across_raw, near, out_cotangent, cosine, sine, unit_table(dp)
        )
        across_cot = to_chip(cot)
        beside_cot = to_core(cot)
        diagonal_raw = to_core(across_raw)
        across_one, diagonal_one = row_call(
            normalize_two, (across_raw, diagonal_raw), (attn_gain,), (jnp.bfloat16, jnp.bfloat16)
        )
        blocks_one = (normed_one, beside_one, across_one, diagonal_one)
        far_mixed, rotated, far_logs, out_across, out_diagonal = attend_far(
            places, near, across_one, diagonal_one, qkv_weight, w_out, cosine, sine, seg_row
        )
        out_across, out_diagonal, rotated, across_cot, beside_cot = sync(
            out_across, out_diagonal, rotated, across_cot, beside_cot
        )
        out_diagonal = to_core(out_diagonal)
        out_across, out_diagonal, rotated, across_cot = sync(
            out_across, out_diagonal, rotated, across_cot
        )
        diagonal_cot = to_core(across_cot)
        far_out = to_chip((out_across + out_diagonal).astype(jnp.bfloat16))
        near_mixed, near_logs, out_own, out_beside = attend_near(
            places, rotated, w_out, seg_row
        )
        far_out, out_own, out_beside, diagonal_cot = sync(
            far_out, out_own, out_beside, diagonal_cot
        )
        cots = (out_cotangent, beside_cot, across_cot, diagonal_cot)
        out_beside = to_core(out_beside)
        middle = add_up([inputs, out_own, out_beside, far_out])
        inverse_two = lax.rsqrt(jnp.mean(middle * middle, axis=-1, keepdims=True) + EPSILON)
        unit_two = middle * inverse_two
        normed_two = (unit_two * ffn_gain).astype(jnp.bfloat16)
        across_two = to_chip(normed_two)
        beside_two = to_core(normed_two)
        mixed = jnp.concatenate([near_mixed, far_mixed], axis=0)
        *parts, back_own, back_beside = feed_near(
            (normed_two, beside_two), cots[:2], w_gate, w_up, w_down
        )
        parts, across_two, mixed, back_own, back_beside = sync(
            parts, across_two, mixed, back_own, back_beside
        )
        diagonal_two = to_core(across_two)
        back_beside = to_core(back_beside)
        blocks_two = (normed_two, beside_two, across_two, diagonal_two)
        gate = DpSum(blocks_two, None, (1, 2, 4), dp, units)
        down = DpSum(cots, None, (2, 1, 4), dp, units)
        hidden, grad_gate, grad_up, gate_early, down_early = feed_far(
            units, blocks_two, cots, w_gate, w_up, w_down, parts
        )
        gate_early, down_early, grad_gate, grad_up, hidden, back_beside = sync(
            gate_early, down_early, grad_gate, grad_up, hidden, back_beside
        )

        gate.right, down.right = grad_gate, hidden
        up = DpSum(blocks_two, grad_up, (1, 2, 4), dp, units)
        gate_early = gate.send(gate_early, 0)
        down_early = down.send(down_early, 0)
        far_across, far_diagonal = feed_back(1, grad_gate, grad_up, w_gate, w_up)
        far_diagonal = to_core(far_diagonal)
        gate_late, down_late = weight_pair((gate, down), 2, 2)
        back_far = (far_across + far_diagonal).astype(jnp.bfloat16)
        gate_early, down_early, back_far, gate_late, down_late, gate.right, down.right, up.right = sync(
            gate_early, down_early, back_far, gate_late, down_late, grad_gate, hidden, grad_up
        )

        gate_late = gate.send(gate_late, 0)
        down_late = down.send(down_late, 0)
        back_far = to_chip(back_far)
        gate_keep, down_keep = weight_pair((gate, down), 4, 4)
        gate_middle = gate.second(gate_keep, gate_early)
        down_middle = down.second(down_keep, down_early)
        down_own, down_across, down_others = feed_down(down.right, w_down)
        (
            gate_late, down_late, back_far, gate_middle, down_middle, up.right, down_own, down_across,
            down_others,
        ) = sync(
            gate_late, down_late, back_far, gate_middle, down_middle, up.right, down_own, down_across,
            down_others,
        )

        gate_middle = gate.send(gate_middle, 1)
        down_middle = down.send(down_middle, 1)
        grad_middle, from_own, gain_two_grad = row_call(
            middle_back,
            (middle, out_cotangent, back_own, back_beside, back_far),
            (ffn_gain,),
            (jnp.float32, jnp.bfloat16),
            1,
        )
        from_across = to_chip(from_own)
        from_beside = to_core(from_own)
        up_whole, up_keep = up.whole_and_keep()
        down_others = to_core(down_others)
        down_far = (down_across + down_others[BLOCK:]).astype(jnp.bfloat16)
        (
            gate_middle, down_middle, from_across, from_beside, up_whole, up_keep, down_others, down_far,
        ) = sync(
            gate_middle, down_middle, from_across, from_beside, up_whole, up_keep, down_others, down_far
        )

        up_whole = up.send(up_whole, 0)
        gate_end = gate.third(gate_keep, gate_late, gate_middle)
        gate_end, from_across, down_keep = sync(gate_end, from_across, down_keep)
        gate_end = gate.send(gate_end, 2)
        from_diagonal = to_core(from_across)
        down_end = down.third(down_keep, down_late, down_middle)
        half = BLOCK // 2
        down_end, from_diagonal = sync((down_end[:half], down_end[half:]), from_diagonal)
        down_ends = down.send(down_end[0], 2)
        down_far = to_chip(down_far)
        grad_attn = (from_own, from_beside, from_across, from_diagonal)
        out = DpSum(grad_attn, mixed, (2, 1, 4), dp, units)
        out_whole = out.send(out.whole(), 0)
        grad_qkv, back_own, back_across, back_others = attend_back(
            places, rotated, near_logs, far_logs, cosine, sine, seg_row, w_out, qkv_weight, grad_attn
        )
        qkv = DpSum(blocks_one, grad_qkv, (1, 2, 4), dp, units)
        qkv_early, qkv_late = qkv.halves()
        gain_one_grad = sum(
            jnp.sum(part.astype(jnp.float32) * block.astype(jnp.float32), axis=0)
            for part, block in zip(
                (back_own, back_others[:BLOCK], back_across, back_others[BLOCK:]), blocks_one
            )
        )
        gains = jnp.stack([gain_one_grad / attn_gain, gain_two_grad[0]])
        (
            up_whole, gate_end, down_ends, out_whole, qkv_early, qkv_late, qkv.right, back_own,
            back_across, back_others, down_far, gains, out.right, down_end,
        ) = sync(
            up_whole, gate_end, down_ends, out_whole, qkv_early, qkv_late, grad_qkv, back_own,
            back_across, back_others, down_far, gains, mixed, down_end[1],
        )

        qkv_early = qkv.send(qkv_early, 0)
        down_end = down.send(down_end, 2)
        up_first = up.second_unit(0, up_keep, up_whole)
        up_first, up_keep, back_others, gains, out.right, qkv.right = sync(
            up_first, up_keep, back_others, gains, out.right, qkv.right
        )
        up_first = up.send(up_first, 1)
        others = to_core(back_others)
        gains_there = to_core(gains)
        up_second = up.second_unit(1, up_keep, up_whole)
        out_keep, qkv_keep = out.keep(), qkv.keep()
        both = jnp.concatenate([qkv_late, out.second(out_keep, out_whole)], axis=2)
        others, back_across, down_end = sync(others, back_across, down_end)
        qkv_middle = qkv.second(qkv_keep, qkv_early)
        one_far = (back_across + others[BLOCK:]).astype(jnp.bfloat16)
        (
            qkv_middle, up_first, others, gains, up_second, out_keep, qkv_keep, both, one_far, down_end,
        ) = sync(
            qkv_middle, up_first, others, gains + gains_there, up_second, out_keep, qkv_keep, both,
            one_far, down_end,
        )

        up_end = up.third(up_keep, up_whole, up_first)
        up_end, qkv_middle, both, one_far, gains, gate_end, down_end, down_far = sync(
            up_end, qkv_middle, both, one_far, gains, gate_end, down_end, down_far
        )
        up_end = up.send(up_end, 2)
        qkv_middle = qkv.send(qkv_middle, 1)
        both = qkv.send(both, 0)
        one_far = to_chip(one_far)
        gains_there = to_chip(gains)
        gate_grad = gate.finish(gate_keep, gate_late, gate_middle, gate_end)
        down_grad = down.finish(
            down_keep, down_late, down_middle, down_ends, down_end, turned=True
        )
        (output,) = row_call(
            add_output, (middle, down_own, down_others, down_far), (), (jnp.bfloat16,)
        )
        (
            up_end, qkv_middle, both, one_far, gains, gate_grad, down_grad, up_second, output,
        ) = sync(
            up_end, qkv_middle, both, one_far, gains + gains_there, gate_grad, down_grad, up_second,
            output,
        )
        width = qkv_weight.shape[1]
        qkv_late, out_middle = both[:, :, :width], both[:, :, width:]

        up_second = up.send(up_second, 1)
        ends = jnp.concatenate(
            [
                qkv.third(qkv_keep, qkv_late, qkv_middle),
                out.third(out_keep, out_whole, out_middle),
            ],
            axis=1,
        )
        ends, gains, one_far = sync(ends, gains, one_far)
        ends = qkv.send(ends, 2)
        gains_there = exchange(gains, dp, 1)
        (input_grad,) = row_call(
            input_back,
            (tokens, grad_middle, back_own, others, one_far),
            (attn_gain,),
            (jnp.float32,),
        )
        up_grad = up.finish(up_keep, up_whole, up_second, up_end)
        ends, gains, input_grad, up_grad = sync(ends, gains + gains_there, input_grad, up_grad)
        step = 2
        while step < dp:
            gains = gains + exchange(gains, dp, step)
            step *= 2
        qkv_grad = qkv.finish(qkv_keep, qkv_late, qkv_middle, ends[:, :width])
        out_grad = out.finish(out_keep, out_whole, out_middle, ends[:, width:], turned=True)
        key_end = query_width + kv_width
        return (
            output,
            input_grad,
            gains[0],
            qkv_grad[:, :query_width],
            qkv_grad[:, query_width:key_end],
            qkv_grad[:, key_end:],
            out_grad,
            gains[1],
            gate_grad,
            up_grad,
            down_grad,
        )

    return local


def solution(mesh):
    rows = P(("dp", "row", "col"), None)
    columns = P(None, ("row", "col"))
    placed = (
        rows,
        P("dp", None),
        P(),
        columns,
        columns,
        columns,
        P(("row", "col"), None),
        P(),
        columns,
        columns,
        P(("row", "col"), None),
        rows,
    )
    summed = P("dp", ("row", "col"))
    turned = P(("row", "col"), "dp")
    return jax.shard_map(
        local_for(mesh.shape["dp"]),
        mesh=mesh,
        in_specs=placed,
        out_specs=(rows, rows, P(), summed, summed, summed, turned, P(), summed, summed, turned),
        check_vma=False,
    )
```

```python
import jax
import jax.numpy as jnp
from jax import lax
from jax.experimental import pallas as pl
from jax.experimental.pallas import tpu as pltpu
from jax.sharding import PartitionSpec as P

HD = 64
EPSILON = 1e-05
MASKED_SCORE = -1e30
BLOCK = 256
TILE = 128
SWAP = ((0, 1), (1, 0))


def positions(segment_ids):
    indices = jnp.arange(segment_ids.shape[-1], dtype=jnp.int32)
    previous = jnp.concatenate([segment_ids[..., :1] - 1, segment_ids[..., :-1]], axis=-1)
    starts = jnp.where(segment_ids != previous, indices, 0)
    return indices - lax.cummax(starts, axis=segment_ids.ndim - 1)


def rope_tables(position):
    exponent = jnp.arange(HD // 2, dtype=jnp.float32) * (-2.0 / HD)
    angles = position.astype(jnp.float32)[:, None] * (10000.0**exponent)[None, :]
    cosine, sine = jnp.cos(angles), jnp.sin(angles)
    return (
        jnp.concatenate([cosine] * 4, axis=1),
        jnp.concatenate([-sine, sine, -sine, sine], axis=1),
    )


def nt(left, right):
    return lax.dot_general(
        left, right, (((1,), (1,)), ((), ())), preferred_element_type=jnp.float32
    )


def nn(left, right):
    return lax.dot_general(
        left, right, (((1,), (0,)), ((), ())), preferred_element_type=jnp.float32
    )


def tn(left, right):
    return lax.dot_general(
        left, right, (((0,), (0,)), ((), ())), preferred_element_type=jnp.float32
    )


def lane_marks():
    lane = lax.broadcasted_iota(jnp.int32, (BLOCK, TILE), 1)
    return lane, lane < HD, lane % HD < HD // 2


def turn_by(values, cosine, sine, first):
    turned = jnp.where(
        first, pltpu.roll(values, TILE - HD // 2, 1), pltpu.roll(values, HD // 2, 1)
    )
    return values * cosine + turned * sine


def rows_of(places, block):
    return pl.ds(pl.multiple_of(places[block], BLOCK), BLOCK)


def segment_column(seg_row, at):
    return jnp.broadcast_to(seg_row[:, at], (TILE, BLOCK)).T


def attend_block(block, places, rotated, keys, values, seg_row, mixed, target, log_sums):
    width = mixed.shape[1]
    lane, low, _ = lane_marks()
    rows = rows_of(places, block)
    at = slice(block * BLOCK, (block + 1) * BLOCK)
    begin = max(0, block - 2) * BLOCK
    span = slice(begin, (block + 1) * BLOCK)
    count = (block + 1) * BLOCK - begin
    key_at = begin + lax.broadcasted_iota(jnp.int32, (BLOCK, count), 1)
    query_at = block * BLOCK + lax.broadcasted_iota(jnp.int32, (BLOCK, count), 0)
    seg_col = segment_column(seg_row, at)[:, :1]
    allowed = (seg_col == seg_row[:, span]) & (key_at <= query_at)
    bias = jnp.where(allowed, 0.0, MASKED_SCORE)
    key_span = keys[span]
    value_span = values[span]

    def one_pair(number, logs):
        columns = pl.ds(pl.multiple_of(number * TILE, TILE), TILE)
        query = rotated[rows, columns]
        results = []
        for half in range(2):
            chosen = jnp.where(low if half == 0 else ~low, query, jnp.zeros_like(query))
            scores = nt(chosen, key_span) + bias
            largest = jnp.max(scores, axis=1, keepdims=True)
            shifted = jnp.exp(scores - largest)
            total = jnp.sum(shifted, axis=1, keepdims=True)
            results.append(nn(shifted.astype(jnp.bfloat16), value_span) * (1.0 / total))
            logs = jnp.where(lane == 2 * number + half, largest + jnp.log(total), logs)
        mixed[target, columns] = jnp.where(low, results[0], results[1]).astype(jnp.bfloat16)
        return logs

    logs = lax.fori_loop(0, width // TILE, one_pair, jnp.zeros((BLOCK, TILE), jnp.float32))
    log_sums[:, at] = logs.T[: log_sums.shape[0]]


def key_value_rows(rotated, rows, keys, values, at, low):
    width = rotated.shape[1] - TILE
    pair = rotated[rows, width:].astype(jnp.float32)
    swapped = pltpu.roll(pair, HD, 1)
    keys[at] = jnp.where(low, pair, swapped).astype(jnp.bfloat16)
    values[at] = jnp.where(low, swapped, pair).astype(jnp.bfloat16)


def attend_side(side, places, rotated, keys, values, seg_row, mixed, log_sums):
    blocks = rotated.shape[0] // BLOCK
    for parity in range(2):

        @pl.when((places[blocks] ^ side) == parity)
        def _():
            for block in range(parity, blocks, 2):
                start = places[block] - side * 2 * BLOCK
                target = pl.ds(pl.multiple_of(start, BLOCK), BLOCK)
                attend_block(
                    block, places, rotated, keys, values, seg_row, mixed, target, log_sums
                )


def attend_far_kernel(
    places, near, across, diagonal, weight, w_out, cosine, sine, seg_row,
    mixed, rotated, log_sums, out_across, out_diagonal, keys, values,
):
    length, total = rotated.shape
    width = total - TILE
    blocks = length // BLOCK
    _, low, first = lane_marks()
    for block in range(blocks):
        rows = rows_of(places, block)
        at = slice(block * BLOCK, (block + 1) * BLOCK)

        def turn_all(proj):
            for start in range(0, width, TILE):
                query = turn_by(proj[:, start : start + TILE], cosine[at], sine[at], first)
                rotated[rows, start : start + TILE] = (query * HD ** (-0.5)).astype(jnp.bfloat16)
            pair = proj[:, width:]
            turned = jnp.where(low, turn_by(pair, cosine[at], sine[at], first), pair)
            rotated[rows, width:] = turned.astype(jnp.bfloat16)

        for piece, source in ((0, None), (1, None), (2, across), (3, diagonal)):

            @pl.when(places[block] == piece * BLOCK)
            def _(piece=piece, source=source):
                if source is None:
                    turn_all(near[piece * BLOCK : (piece + 1) * BLOCK])
                else:
                    turn_all(nn(source[...], weight[...]))

        key_value_rows(rotated, rows, keys, values, at, low)
    attend_side(1, places, rotated, keys, values, seg_row, mixed, log_sums)
    out_diagonal[...] = nn(mixed[BLOCK:], w_out[...]).astype(jnp.bfloat16)
    out_across[...] = nn(mixed[:BLOCK], w_out[...]).astype(jnp.bfloat16)


def attend_near_kernel(
    places, rotated, w_out, seg_row, mixed, log_sums, out_own, out_beside, keys, values
):
    blocks = rotated.shape[0] // BLOCK
    _, low, _ = lane_marks()
    for block in range(blocks):
        at = slice(block * BLOCK, (block + 1) * BLOCK)
        key_value_rows(rotated, rows_of(places, block), keys, values, at, low)
    attend_side(0, places, rotated, keys, values, seg_row, mixed, log_sums)
    out_beside[...] = nn(mixed[BLOCK:], w_out[...]).astype(jnp.bfloat16)
    out_own[...] = nn(mixed[:BLOCK], w_out[...]).astype(jnp.bfloat16)


def attend_back_kernel(
    places, rotated, near_logs, far_logs, cosine, sine, seg_row, w_out, weight,
    from_own, from_beside, from_across, from_diagonal,
    grads, back_own, back_across, back_others,
    keys, values, key_sum, value_sum, grad_mixed, seg_col,
):
    length = rotated.shape[0]
    width = grad_mixed.shape[1]
    blocks = length // BLOCK
    _, low, first = lane_marks()
    for piece, source in enumerate((from_own, from_beside, from_across, from_diagonal)):
        grad_mixed[piece * BLOCK : (piece + 1) * BLOCK] = nt(source[...], w_out[...]).astype(
            jnp.bfloat16
        )
    key_sum[...] = jnp.zeros_like(key_sum)
    value_sum[...] = jnp.zeros_like(value_sum)
    for block in range(blocks):
        at = slice(block * BLOCK, (block + 1) * BLOCK)
        key_value_rows(rotated, rows_of(places, block), keys, values, at, low)
        seg_col[at] = segment_column(seg_row, at)
    def block_back(block, begin):
        rows = rows_of(places, block)
        at = slice(block * BLOCK, (block + 1) * BLOCK)
        is_near = places[blocks] == block % 2
        span = slice(begin, (block + 1) * BLOCK)
        count = (block + 1) * BLOCK - begin
        key_at = begin + lax.broadcasted_iota(jnp.int32, (count, BLOCK), 0)
        query_at = block * BLOCK + lax.broadcasted_iota(jnp.int32, (count, BLOCK), 1)
        allowed = (seg_col[span, :1] == seg_row[:, at]) & (key_at <= query_at)
        bias = jnp.where(allowed, 0.0, MASKED_SCORE)
        key_span = keys[span]
        value_span = values[span]

        def one_pair(number, carry):
            columns = pl.ds(pl.multiple_of(number * TILE, TILE), TILE)
            query = rotated[rows, columns]
            grad = grad_mixed[rows, columns]
            results = []
            for half in range(2):
                side = low if half == 0 else ~low
                chosen = jnp.where(side, query, jnp.zeros_like(query))
                chosen_grad = jnp.where(side, grad, jnp.zeros_like(grad))
                head = pl.ds(2 * number + half, 1)
                logs = jnp.where(is_near, near_logs[head, at], far_logs[head, at])
                probs = jnp.exp(nt(key_span, chosen) + bias - logs)
                grad_probs = nt(value_span, chosen_grad)
                inner = jnp.sum(probs * grad_probs, axis=0, keepdims=True)
                grad_scores = (probs * (grad_probs - inner)).astype(jnp.bfloat16)
                value_sum[span] += nn(probs.astype(jnp.bfloat16), chosen_grad)
                key_sum[span] += nn(grad_scores, chosen)
                results.append(tn(grad_scores, key_span))
            grad_query = jnp.where(low, results[0], results[1]) * HD ** (-0.5)
            grads[rows, columns] = turn_by(grad_query, cosine[at], -sine[at], first).astype(
                jnp.bfloat16
            )
            return carry

        lax.fori_loop(0, width // TILE, one_pair, 0)
    for block in range(blocks):
        if block < 2:
            block_back(block, 0)
            continue
        for back in (1, 2):

            @pl.when(places[blocks - 1 + block] == back - 1)
            def _(block=block, back=back):
                block_back(block, (block - back) * BLOCK)

    for block in range(blocks):
        rows = rows_of(places, block)
        at = slice(block * BLOCK, (block + 1) * BLOCK)
        grad_key = key_sum[at]
        grad_key = turn_by(grad_key + pltpu.roll(grad_key, HD, 1), cosine[at], -sine[at], first)
        grad_value = value_sum[at]
        grad_value = grad_value + pltpu.roll(grad_value, HD, 1)
        grads[rows, width:] = jnp.where(low, grad_key, grad_value).astype(jnp.bfloat16)
    targets = (back_own, back_others.at[:BLOCK], back_across, back_others.at[BLOCK:])
    for piece, target in enumerate(targets):
        grad_rows = grads[piece * BLOCK : (piece + 1) * BLOCK]
        target[...] = nt(grad_rows, weight[...]).astype(jnp.bfloat16)


SMEM = pl.BlockSpec(memory_space=pltpu.SMEM)
VMEM = pl.BlockSpec(memory_space=pltpu.VMEM)


ANY = pl.BlockSpec(memory_space=pl.ANY)
LITTLE = pl.CostEstimate(flops=1 << 20, bytes_accessed=1 << 12, transcendentals=0)


def params(limit):
    return pltpu.CompilerParams(vmem_limit_bytes=limit << 20)


def attend_far(places, near, across, diagonal, weight, w_out, cosine, sine, seg_row):
    length, total = 2 * near.shape[0], near.shape[1]
    width = total - TILE
    depth = w_out.shape[1]
    block = jax.ShapeDtypeStruct((BLOCK, depth), jnp.bfloat16)
    return pl.pallas_call(
        attend_far_kernel,
        out_shape=(
            jax.ShapeDtypeStruct((length // 2, width), jnp.bfloat16),
            jax.ShapeDtypeStruct((length, total), jnp.bfloat16),
            jax.ShapeDtypeStruct((width // HD, length), jnp.float32),
            block,
            block,
        ),
        in_specs=[SMEM] + [VMEM] * 8,
        out_specs=(VMEM,) * 5,
        scratch_shapes=[pltpu.VMEM((length, TILE), jnp.bfloat16)] * 2,
        compiler_params=params(48),
        cost_estimate=LITTLE,
        name="attend_far",
    )(places, near, across, diagonal, weight, w_out, cosine, sine, seg_row)


def attend_near(places, rotated, w_out, seg_row):
    length, total = rotated.shape
    width = total - TILE
    depth = w_out.shape[1]
    block = jax.ShapeDtypeStruct((BLOCK, depth), jnp.bfloat16)
    return pl.pallas_call(
        attend_near_kernel,
        out_shape=(
            jax.ShapeDtypeStruct((length // 2, width), jnp.bfloat16),
            jax.ShapeDtypeStruct((width // HD, length), jnp.float32),
            block,
            block,
        ),
        in_specs=[SMEM] + [VMEM] * 3,
        out_specs=(VMEM,) * 4,
        scratch_shapes=[pltpu.VMEM((length, TILE), jnp.bfloat16)] * 2,
        compiler_params=params(48),
        cost_estimate=LITTLE,
        name="attend_near",
    )(places, rotated, w_out, seg_row)


def attend_back(
    places, rotated, near_logs, far_logs, cosine, sine, seg_row, w_out, weight, pieces
):
    length, total = rotated.shape
    return pl.pallas_call(
        attend_back_kernel,
        out_shape=(jax.ShapeDtypeStruct((length, total), jnp.bfloat16),)
        + (jax.ShapeDtypeStruct(pieces[0].shape, jnp.bfloat16),) * 2
        + (jax.ShapeDtypeStruct((2 * BLOCK, pieces[0].shape[1]), jnp.bfloat16),),
        in_specs=[SMEM] + [VMEM] * 12,
        out_specs=(VMEM,) * 4,
        scratch_shapes=[pltpu.VMEM((length, TILE), jnp.bfloat16)] * 2
        + [pltpu.VMEM((length, TILE), jnp.float32)] * 2
        + [
            pltpu.VMEM((length, total - TILE), jnp.bfloat16),
            pltpu.VMEM((length, TILE), jnp.int32),
        ],
        compiler_params=params(52),
        cost_estimate=LITTLE,
        name="attend_back",
    )(
        places, rotated, near_logs, far_logs, cosine, sine, seg_row, w_out, weight, *pieces
    )


def terms_kernel(starts, units, one, two, three, four, right, *outs):
    left = jnp.concatenate([one[...], two[...], three[...], four[...]], axis=0)
    total = tn(left, right[...]).astype(jnp.bfloat16)
    step = pl.program_id(0)
    for out, start, end in zip(outs, starts, starts[1:]):

        @pl.when((step >= start) & (step < end))
        def _(out=out):
            out[0] = total


def weight_terms(pieces, right, units, first, sizes):
    count = pieces[0].shape[0]
    rows, width = right.shape
    starts = [sum(sizes[:number]) for number in range(len(sizes) + 1)]
    return pl.pallas_call(
        lambda *refs: terms_kernel(starts, *refs),
        grid_spec=pltpu.PrefetchScalarGridSpec(
            num_scalar_prefetch=1,
            grid=(starts[-1],),
            in_specs=[pl.BlockSpec((count, BLOCK), lambda i, units: (0, units[first + i]))] * 4
            + [pl.BlockSpec((rows, width), lambda i, units: (0, 0))],
            out_specs=[
                pl.BlockSpec(
                    (1, BLOCK, width),
                    lambda i, units, start=start, size=size: (
                        jnp.clip(i - start, 0, size - 1),
                        0,
                        0,
                    ),
                )
                for start, size in zip(starts, sizes)
            ],
        ),
        out_shape=[jax.ShapeDtypeStruct((size, BLOCK, width), jnp.bfloat16) for size in sizes],
        compiler_params=params(60),
        cost_estimate=LITTLE,
        name="weight_terms",
    )(units, *pieces, right)


def pair_kernel(each, units, *refs):
    left, right, outs = refs[:8], refs[8:10], refs[10:]
    for number, out in enumerate(outs):

        @pl.when(pl.program_id(0) // each == number)
        def _(number=number, out=out):
            pieces = [ref[...] for ref in left[4 * number : 4 * number + 4]]
            total = tn(jnp.concatenate(pieces, axis=0), right[number][...])
            out[0] = total.astype(jnp.bfloat16)


def weight_pair(sums, first, size):
    count = sums[0].pieces[0].shape[0]
    rows, width = sums[0].right.shape

    def step(i, number):
        return jnp.clip(i - number * size, 0, size - 1)

    specs = []
    for number, each in enumerate(sums):
        specs += [
            pl.BlockSpec(
                (count, BLOCK),
                lambda i, units, number=number, start=each.base + first: (
                    0,
                    units[start + step(i, number)],
                ),
            )
        ] * 4
    return pl.pallas_call(
        lambda *refs: pair_kernel(size, *refs),
        grid_spec=pltpu.PrefetchScalarGridSpec(
            num_scalar_prefetch=1,
            grid=(2 * size,),
            in_specs=specs + [pl.BlockSpec((rows, width), lambda i, units: (0, 0))] * 2,
            out_specs=[
                pl.BlockSpec(
                    (1, BLOCK, width), lambda i, units, number=number: (step(i, number), 0, 0)
                )
                for number in range(2)
            ],
        ),
        out_shape=[jax.ShapeDtypeStruct((size, BLOCK, width), jnp.bfloat16)] * 2,
        compiler_params=params(60),
        cost_estimate=LITTLE,
        name="weight_pair",
    )(sums[0].units, *sums[0].pieces, *sums[1].pieces, sums[0].right, sums[1].right)


def exchange(values, dp, distance):
    return lax.ppermute(values, "dp", [(device, device ^ distance) for device in range(dp)])


def numbered(bits, values, free):
    fixed = jnp.zeros((), jnp.int32)
    for bit, value in zip(bits, values):
        fixed = fixed + bit * value
    numbers = [fixed]
    for bit in free:
        numbers = [number + add for number in numbers for add in (0, bit)]
    return jnp.stack(numbers).astype(jnp.int32)


ORDERS = ((1, 2, 4), (2, 1, 4))


def unit_table(dp):
    unit = lax.axis_index("dp") // (dp // 8)
    numbers = []
    for order in ORDERS:
        one, two, three = ((unit // bit) % 2 for bit in order)
        numbers += [
            sum(bit * value for bit, value in zip(order, values))
            for values in (
                (first, second, third)
                for first in (1 - one, one)
                for second in (1 - two, two)
                for third in (1 - three, three)
            )
        ]
    return jnp.stack(numbers).astype(jnp.int32)


class DpSum:
    def __init__(self, pieces, right, order, dp, units):
        self.pieces, self.right, self.order, self.dp, self.units = pieces, right, order, dp, units
        self.base = 8 * ORDERS.index(order)

    def terms(self, first, *sizes):
        return weight_terms(self.pieces, self.right, self.units, self.base + first, sizes)

    def whole(self):
        return self.terms(0, 4)[0]

    def halves(self):
        return self.terms(0, 2, 2)

    def keep(self):
        return self.terms(4, 4)[0]

    def whole_and_keep(self):
        return self.terms(0, 4, 4)

    def send(self, values, step):
        return exchange(values, self.dp, self.order[step] * (self.dp // 8))

    def second(self, keep, early):
        return add_up([keep[:2], early[:2]]).astype(jnp.bfloat16)

    def second_unit(self, number, keep, early):
        return add_up([keep[number : number + 1], early[number : number + 1]]).astype(jnp.bfloat16)

    def third(self, keep, late, middle):
        at = late.shape[0] - 2
        return add_up([keep[2], late[at], middle[0]]).astype(jnp.bfloat16)

    def finish(self, keep, late, middle, *ends, turned=False):
        if self.dp == 8:
            return finish_sum(keep, late, middle, ends, turned)
        total = finish_sum(keep, late, middle, ends, False)
        index, left = lax.axis_index("dp"), self.dp // 8
        while left > 1:
            left //= 2
            bit = (index // left) % 2
            parts = total.reshape(2, total.shape[0] // 2, total.shape[1])
            there = exchange(pick(parts, 1 - bit, 0).astype(jnp.bfloat16), self.dp, left)
            total = pick(parts, bit, 0) + there.astype(jnp.float32)
        return total.T if turned else total


def finish_kernel(turned, ends, keep, late, middle, *refs):
    out = refs[-1]
    end = refs[0][...].astype(jnp.float32)
    if ends == 2:
        end = jnp.where(pl.program_id(0) == 0, end, refs[1][...].astype(jnp.float32))
    total = keep[0].astype(jnp.float32) + late[0].astype(jnp.float32)
    total = total + middle[0].astype(jnp.float32) + end
    out[...] = total.T if turned else total


def finish_sum(keep, late, middle, ends, turned):
    _, rows, columns = keep.shape
    size = rows // 2
    specs = [
        pl.BlockSpec((1, size, columns), lambda i, at=array.shape[0] - 1: (at, i, 0))
        for array in (keep, late, middle)
    ]
    end = pl.BlockSpec((size, columns), lambda i: (0 if len(ends) == 2 else i, 0))
    shape = (columns, rows) if turned else (rows, columns)
    out = (
        pl.BlockSpec((columns, size), lambda i: (0, i))
        if turned
        else pl.BlockSpec((size, columns), lambda i: (i, 0))
    )
    return pl.pallas_call(
        lambda *refs: finish_kernel(turned, len(ends), *refs),
        grid=(2,),
        in_specs=specs + [end] * len(ends),
        out_specs=out,
        out_shape=jax.ShapeDtypeStruct(shape, jnp.float32),
        compiler_params=params(40),
        cost_estimate=LITTLE,
        name="finish_sum",
    )(keep, late, middle, *ends)


def row_call(kernel, rows, wholes, outs, totals=0):
    count, depth = rows[0].shape
    size = 64
    block = pl.BlockSpec((size, depth), lambda i: (i, 0))
    whole = pl.BlockSpec((1, depth), lambda i: (0, 0))
    return pl.pallas_call(
        kernel,
        grid=(count // size,),
        in_specs=[block] * len(rows) + [whole] * len(wholes),
        out_specs=(block,) * len(outs) + (whole,) * totals,
        out_shape=tuple(jax.ShapeDtypeStruct((count, depth), kind) for kind in outs)
        + (jax.ShapeDtypeStruct((1, depth), jnp.float32),) * totals,
        compiler_params=params(40),
        cost_estimate=LITTLE,
        name=kernel.__name__,
    )(*rows, *(array.reshape(1, depth) for array in wholes))


def normalize_two(one, two, gain, *outs):
    for rows, out in zip((one, two), outs):
        values = rows[...].astype(jnp.float32)
        inverse = lax.rsqrt(jnp.mean(values * values, axis=-1, keepdims=True) + EPSILON)
        out[...] = (values * inverse * gain[...]).astype(jnp.bfloat16)


def scale_back(values, grads, gain):
    inverse = lax.rsqrt(jnp.mean(values * values, axis=-1, keepdims=True) + EPSILON)
    unit = values * inverse
    scaled = grads * gain
    return unit, inverse * (scaled - unit * jnp.mean(scaled * unit, axis=-1, keepdims=True))


def middle_back(middle, cot, one, two, three, gain, grad_middle, rounded, gain_grad):
    grads = one[...].astype(jnp.float32) + two[...].astype(jnp.float32) + three[...].astype(jnp.float32)
    unit, back = scale_back(middle[...], grads, gain[...])
    total = cot[...].astype(jnp.float32) + back
    grad_middle[...] = total
    rounded[...] = total.astype(jnp.bfloat16)

    @pl.when(pl.program_id(0) == 0)
    def _():
        gain_grad[...] = jnp.zeros_like(gain_grad)

    gain_grad[...] += jnp.sum(grads * unit, axis=0, keepdims=True)


def input_back(tokens, grad_middle, one, two, three, gain, input_grad):
    grads = one[...].astype(jnp.float32) + two[...].astype(jnp.float32) + three[...].astype(jnp.float32)
    _, back = scale_back(tokens[...].astype(jnp.float32), grads, gain[...])
    input_grad[...] = grad_middle[...] + back


def add_output(middle, one, two, three, output):
    total = middle[...] + one[...].astype(jnp.float32) + two[...].astype(jnp.float32)
    output[...] = (total + three[...].astype(jnp.float32)).astype(jnp.bfloat16)


def sync(*values):
    return lax.optimization_barrier(values)


def column_tiles(width, most=256):
    return [(at, min(most, width - at)) for at in range(0, width, most)]


def feed_near_kernel(one, two, cot_one, cot_two, w_gate, w_up, w_down, *rest):
    hidden, grad_gate, grad_up, back_one, back_two = rest[:5]
    rows, cots, gate, up, down, gates, ups, sems = rest[5:]
    sources = (one, two, w_gate, w_up, cot_one, cot_two, w_down)
    feed_steps(sources, rest[5:], hidden, grad_gate, grad_up)
    count = back_one.shape[0]
    for at, size in column_tiles(gate.shape[0]):
        span = slice(at, at + size)
        total = nt(grad_gate[...], gate[span]) + nt(grad_up[...], up[span])
        back_one[:, span] = total[:count].astype(jnp.bfloat16)
        back_two[:, span] = total[count:].astype(jnp.bfloat16)


def feed_far_kernel(units, one, two, cot_one, cot_two, w_gate, w_up, w_down, *rest):
    near_one, near_two, near_cot_one, near_cot_two, held_hidden, held_gate, _ = rest[:7]
    results, (gate_early, down_early) = rest[7:10], rest[10:12]
    near_rows, near_cots, near_hidden, near_gate, near_sems = rest[12:17]
    hidden, grad_gate, grad_up, out_sems = made = rest[17:21]
    scratch = rest[21:]
    rows, cots = scratch[:2]
    count = one.shape[0]
    moves = [
        pltpu.make_async_copy(held_hidden.at[: 2 * count], near_hidden, near_sems.at[0]),
        pltpu.make_async_copy(held_gate.at[: 2 * count], near_gate, near_sems.at[1]),
    ]
    lefts = (
        (near_one, near_rows, 0, 0),
        (near_two, near_rows, count, 0),
        (near_cot_one, near_cots, 0, 8),
        (near_cot_two, near_cots, count, 8),
    )
    for number, (source, target, start, first) in enumerate(lefts):
        for unit in range(2):
            columns = pl.ds(pl.multiple_of(units[first + unit] * BLOCK, BLOCK), BLOCK)
            moves.append(
                pltpu.make_async_copy(
                    source.at[:, columns],
                    target.at[unit, start : start + count],
                    near_sems.at[2 + 2 * number + unit],
                )
            )
    sources = (one, two, w_gate, w_up, cot_one, cot_two, w_down)
    feed_steps(sources, scratch, hidden, grad_gate, grad_up, moves)
    stores = [
        pltpu.make_async_copy(source, target.at[2 * count :], out_sems.at[number])
        for number, (source, target) in enumerate(zip(made[:3], results))
    ]
    for store in stores:
        store.start()
    for first, left, far_left, near_right, far_right, out in (
        (0, near_rows, rows, near_gate, grad_gate, gate_early),
        (8, near_cots, cots, near_hidden, hidden, down_early),
    ):
        for unit in range(2):
            columns = pl.ds(pl.multiple_of(units[first + unit] * BLOCK, BLOCK), BLOCK)
            total = tn(left[unit], near_right[...]) + tn(far_left[:, columns], far_right[...])
            out[unit] = total.astype(jnp.bfloat16)
    for store in stores:
        store.wait()


def feed_steps(sources, scratch, hidden, grad_gate, grad_up, more=()):
    rows, cots, gate, up, down, gates, ups, sems = scratch
    count = sources[0].shape[0]
    targets = (
        rows.at[:count], rows.at[count:], gate, up, cots.at[:count], cots.at[count:], down,
    )
    moves = [
        pltpu.make_async_copy(source, target, sems.at[number])
        for number, (source, target) in enumerate(zip(sources, targets))
    ]
    for move in (*moves, *more):
        move.start()
    for move in moves[:3]:
        move.wait()
    tiles = column_tiles(gate.shape[1])
    for at, size in tiles:
        gates[:, at : at + size] = nn(rows[...], gate[:, at : at + size])
    moves[3].wait()
    for at, size in tiles:
        ups[:, at : at + size] = nn(rows[...], up[:, at : at + size])
    for move in moves[4:]:
        move.wait()
    for at, size in tiles:
        span = slice(at, at + size)
        grad_hidden = nt(cots[...], down[span])
        gate_pre = gates[:, span]
        up_pre = ups[:, span]
        sigmoid = jax.nn.sigmoid(gate_pre)
        silu = gate_pre * sigmoid
        hidden[:, span] = (silu * up_pre).astype(jnp.bfloat16)
        slope = sigmoid + silu * (1.0 - sigmoid)
        grad_gate[:, span] = (grad_hidden * up_pre * slope).astype(jnp.bfloat16)
        grad_up[:, span] = (grad_hidden * silu).astype(jnp.bfloat16)
    for move in more:
        move.wait()


def feed_scratch(count, depth, width):
    return (
        [pltpu.VMEM((2 * count, depth), jnp.bfloat16)] * 2
        + [pltpu.VMEM((depth, width), jnp.bfloat16)] * 2
        + [
            pltpu.VMEM((width, depth), jnp.bfloat16),
            pltpu.VMEM((2 * count, width), jnp.float32),
            pltpu.VMEM((2 * count, width), jnp.float32),
            pltpu.SemaphoreType.DMA((7,)),
        ]
    )


def feed_near(pair, cots, w_gate, w_up, w_down):
    count, depth = pair[0].shape
    width = w_gate.shape[1]
    return pl.pallas_call(
        feed_near_kernel,
        grid=(1,),
        out_shape=(jax.ShapeDtypeStruct((4 * count, width), jnp.bfloat16),) * 3
        + (jax.ShapeDtypeStruct((count, depth), jnp.bfloat16),) * 2,
        in_specs=[ANY] * 7,
        out_specs=(pl.BlockSpec((2 * count, width), lambda i: (0, 0)),) * 3
        + (pl.BlockSpec((count, depth), lambda i: (0, 0)),) * 2,
        scratch_shapes=feed_scratch(count, depth, width),
        compiler_params=params(56),
        cost_estimate=LITTLE,
        name="feed_near",
    )(*pair, *cots, w_gate, w_up, w_down)


def feed_far(units, blocks, cots, w_gate, w_up, w_down, held):
    count, depth = blocks[0].shape
    width = w_gate.shape[1]
    early = jax.ShapeDtypeStruct((2, BLOCK, width), jnp.bfloat16)
    return pl.pallas_call(
        feed_far_kernel,
        grid_spec=pltpu.PrefetchScalarGridSpec(
            num_scalar_prefetch=1,
            grid=(1,),
            in_specs=[ANY] * 14,
            out_specs=(ANY,) * 3 + (pl.BlockSpec((2, BLOCK, width), lambda i, units: (0, 0, 0)),) * 2,
            scratch_shapes=[pltpu.VMEM((2, 2 * count, BLOCK), jnp.bfloat16)] * 2
            + [pltpu.VMEM((2 * count, width), jnp.bfloat16)] * 2
            + [pltpu.SemaphoreType.DMA((10,))]
            + [pltpu.VMEM((2 * count, width), jnp.bfloat16)] * 3
            + [pltpu.SemaphoreType.DMA((3,))]
            + feed_scratch(count, depth, width),
        ),
        out_shape=(jax.ShapeDtypeStruct((4 * count, width), jnp.bfloat16),) * 3 + (early,) * 2,
        input_output_aliases={12: 0, 13: 1, 14: 2},
        compiler_params=params(60),
        cost_estimate=LITTLE,
        name="feed_far",
    )(units, *blocks[2:], *cots[2:], w_gate, w_up, w_down, *blocks[:2], *cots[:2], *held)


def feed_back_kernel(grad_gate, grad_up, w_gate, w_up, one, two):
    total = nt(grad_gate[...], w_gate[...]) + nt(grad_up[...], w_up[...])
    total = total.astype(jnp.bfloat16)
    one[...] = total[: one.shape[0]]
    two[...] = total[one.shape[0] :]


def feed_back(side, grad_gate, grad_up, w_gate, w_up):
    count = grad_gate.shape[0] // 4
    depth, width = w_gate.shape
    size = 256
    rows = pl.BlockSpec((2 * count, width), lambda i: (side, 0))
    weights = pl.BlockSpec((size, width), lambda i: (i, 0))
    outs = pl.BlockSpec((count, size), lambda i: (0, i))
    return pl.pallas_call(
        feed_back_kernel,
        grid=(depth // size,),
        out_shape=(jax.ShapeDtypeStruct((count, depth), jnp.bfloat16),) * 2,
        in_specs=[rows, rows, weights, weights],
        out_specs=(outs, outs),
        compiler_params=params(60),
        cost_estimate=LITTLE,
        name="feed_back",
    )(grad_gate, grad_up, w_gate, w_up)


def feed_down_kernel(hidden, w_down, own, across, others):
    total = nn(hidden[...], w_down[...]).astype(jnp.bfloat16)
    count = own.shape[0]
    own[...] = total[:count]
    others[:count] = total[count : 2 * count]
    across[...] = total[2 * count : 3 * count]
    others[count:] = total[3 * count :]


def feed_down(hidden, w_down):
    count = hidden.shape[0] // 4
    width, depth = w_down.shape
    size = 512
    block = pl.BlockSpec((count, size), lambda i: (0, i))
    return pl.pallas_call(
        feed_down_kernel,
        grid=(depth // size,),
        out_shape=(jax.ShapeDtypeStruct((count, depth), jnp.bfloat16),) * 2
        + (jax.ShapeDtypeStruct((2 * count, depth), jnp.bfloat16),),
        in_specs=[
            pl.BlockSpec((4 * count, width), lambda i: (0, 0)),
            pl.BlockSpec((width, size), lambda i: (0, i)),
        ],
        out_specs=(block, block, pl.BlockSpec((2 * count, size), lambda i: (0, i))),
        compiler_params=params(60),
        cost_estimate=LITTLE,
        name="feed_down",
    )(hidden, w_down)


def to_core(values):
    return lax.ppermute(values, "row", SWAP)


def to_chip(values):
    return lax.ppermute(values, "col", SWAP)


def gather_blocks(own):
    across = to_chip(own)
    return own, to_core(own), across, to_core(across)


def scatter_far(across, diagonal):
    return to_chip((across + to_core(diagonal)).astype(jnp.bfloat16))


def pick(values, index, axis):
    return lax.dynamic_index_in_dim(values, index, axis, keepdims=False)


def add_up(terms):
    total = terms[0].astype(jnp.float32)
    for term in terms[1:]:
        total = total + term.astype(jnp.float32)
    return total


def local_for(dp):
    def local(
        tokens,
        segments,
        attn_gain,
        w_query,
        w_key,
        w_value,
        w_out,
        ffn_gain,
        w_gate,
        w_up,
        w_down,
        out_cotangent,
    ):
        query_width = w_query.shape[1]
        kv_width = w_key.shape[1]
        length = segments.shape[1]
        row, col = lax.axis_index("row"), lax.axis_index("col")
        places = [
            (((block // 2) ^ row) + 2 * ((block % 2) ^ col)) * (length // 4) for block in range(4)
        ]
        reaches = [
            segments[0, (block - 1) * BLOCK - 1] == segments[0, block * BLOCK]
            for block in range(2, length // BLOCK)
        ]
        places = jnp.stack([number.astype(jnp.int32) for number in places + [col] + reaches])

        across_raw = to_chip(tokens)
        inputs = tokens.astype(jnp.float32)
        inverse_one = lax.rsqrt(jnp.mean(inputs * inputs, axis=-1, keepdims=True) + EPSILON)
        unit_one = inputs * inverse_one
        normed_one = (unit_one * attn_gain).astype(jnp.bfloat16)
        beside_one = to_core(normed_one)
        qkv_weight = jnp.concatenate([w_query, w_key, w_value], axis=1)
        cosine, sine = rope_tables(positions(segments).reshape(length))
        seg_row = segments.reshape(1, length)
        near = nn(jnp.concatenate([normed_one, beside_one], axis=0), qkv_weight)
        across_raw, near, cot, cosine, sine, units = sync(
            across_raw, near, out_cotangent, cosine, sine, unit_table(dp)
        )
        across_cot = to_chip(cot)
        beside_cot = to_core(cot)
        diagonal_raw = to_core(across_raw)
        across_one, diagonal_one = row_call(
            normalize_two, (across_raw, diagonal_raw), (attn_gain,), (jnp.bfloat16, jnp.bfloat16)
        )
        blocks_one = (normed_one, beside_one, across_one, diagonal_one)
        far_mixed, rotated, far_logs, out_across, out_diagonal = attend_far(
            places, near, across_one, diagonal_one, qkv_weight, w_out, cosine, sine, seg_row
        )
        out_across, out_diagonal, rotated, across_cot, beside_cot = sync(
            out_across, out_diagonal, rotated, across_cot, beside_cot
        )
        out_diagonal = to_core(out_diagonal)
        out_across, out_diagonal, rotated, across_cot = sync(
            out_across, out_diagonal, rotated, across_cot
        )
        diagonal_cot = to_core(across_cot)
        far_out = to_chip((out_across + out_diagonal).astype(jnp.bfloat16))
        near_mixed, near_logs, out_own, out_beside = attend_near(
            places, rotated, w_out, seg_row
        )
        far_out, out_own, out_beside, diagonal_cot = sync(
            far_out, out_own, out_beside, diagonal_cot
        )
        cots = (out_cotangent, beside_cot, across_cot, diagonal_cot)
        out_beside = to_core(out_beside)
        middle = add_up([inputs, out_own, out_beside, far_out])
        inverse_two = lax.rsqrt(jnp.mean(middle * middle, axis=-1, keepdims=True) + EPSILON)
        unit_two = middle * inverse_two
        normed_two = (unit_two * ffn_gain).astype(jnp.bfloat16)
        across_two = to_chip(normed_two)
        beside_two = to_core(normed_two)
        mixed = jnp.concatenate([near_mixed, far_mixed], axis=0)
        *parts, back_own, back_beside = feed_near(
            (normed_two, beside_two), cots[:2], w_gate, w_up, w_down
        )
        parts, across_two, mixed, back_own, back_beside = sync(
            parts, across_two, mixed, back_own, back_beside
        )
        diagonal_two = to_core(across_two)
        back_beside = to_core(back_beside)
        blocks_two = (normed_two, beside_two, across_two, diagonal_two)
        gate = DpSum(blocks_two, None, (1, 2, 4), dp, units)
        down = DpSum(cots, None, (2, 1, 4), dp, units)
        hidden, grad_gate, grad_up, gate_early, down_early = feed_far(
            units, blocks_two, cots, w_gate, w_up, w_down, parts
        )
        gate_early, down_early, grad_gate, grad_up, hidden, back_beside = sync(
            gate_early, down_early, grad_gate, grad_up, hidden, back_beside
        )

        gate.right, down.right = grad_gate, hidden
        up = DpSum(blocks_two, grad_up, (1, 2, 4), dp, units)
        gate_early = gate.send(gate_early, 0)
        down_early = down.send(down_early, 0)
        far_across, far_diagonal = feed_back(1, grad_gate, grad_up, w_gate, w_up)
        far_diagonal = to_core(far_diagonal)
        gate_late, down_late = weight_pair((gate, down), 2, 2)
        back_far = (far_across + far_diagonal).astype(jnp.bfloat16)
        gate_early, down_early, back_far, gate_late, down_late, gate.right, down.right, up.right = sync(
            gate_early, down_early, back_far, gate_late, down_late, grad_gate, hidden, grad_up
        )

        gate_late = gate.send(gate_late, 0)
        down_late = down.send(down_late, 0)
        back_far = to_chip(back_far)
        gate_keep, down_keep = weight_pair((gate, down), 4, 4)
        gate_middle = gate.second(gate_keep, gate_early)
        down_middle = down.second(down_keep, down_early)
        down_own, down_across, down_others = feed_down(down.right, w_down)
        (
            gate_late, down_late, back_far, gate_middle, down_middle, up.right, down_own, down_across,
            down_others,
        ) = sync(
            gate_late, down_late, back_far, gate_middle, down_middle, up.right, down_own, down_across,
            down_others,
        )

        gate_middle = gate.send(gate_middle, 1)
        down_middle = down.send(down_middle, 1)
        grad_middle, from_own, gain_two_grad = row_call(
            middle_back,
            (middle, out_cotangent, back_own, back_beside, back_far),
            (ffn_gain,),
            (jnp.float32, jnp.bfloat16),
            1,
        )
        from_across = to_chip(from_own)
        from_beside = to_core(from_own)
        up_whole, up_keep = up.whole_and_keep()
        down_others = to_core(down_others)
        down_far = (down_across + down_others[BLOCK:]).astype(jnp.bfloat16)
        (
            gate_middle, down_middle, from_across, from_beside, up_whole, up_keep, down_others, down_far,
        ) = sync(
            gate_middle, down_middle, from_across, from_beside, up_whole, up_keep, down_others, down_far
        )

        up_whole = up.send(up_whole, 0)
        gate_end = gate.third(gate_keep, gate_late, gate_middle)
        gate_end, from_across, down_keep = sync(gate_end, from_across, down_keep)
        gate_end = gate.send(gate_end, 2)
        from_diagonal = to_core(from_across)
        half = BLOCK // 2
        down_end = tuple(
            down.third(down_keep[:, rows], down_late[:, rows], down_middle[:, rows])
            for rows in (slice(0, half), slice(half, BLOCK))
        )
        down_end, from_diagonal = sync(down_end, from_diagonal)
        down_ends = down.send(down_end[0], 2)
        down_far = to_chip(down_far)
        grad_attn = (from_own, from_beside, from_across, from_diagonal)
        out = DpSum(grad_attn, mixed, (2, 1, 4), dp, units)
        out_whole = out.send(out.whole(), 0)
        grad_qkv, back_own, back_across, back_others = attend_back(
            places, rotated, near_logs, far_logs, cosine, sine, seg_row, w_out, qkv_weight, grad_attn
        )
        qkv = DpSum(blocks_one, grad_qkv, (1, 2, 4), dp, units)
        qkv_early, qkv_late = qkv.halves()
        gain_one_grad = sum(
            jnp.sum(part.astype(jnp.float32) * block.astype(jnp.float32), axis=0)
            for part, block in zip(
                (back_own, back_others[:BLOCK], back_across, back_others[BLOCK:]), blocks_one
            )
        )
        gains = jnp.stack([gain_one_grad / attn_gain, gain_two_grad[0]])
        (
            up_whole, gate_end, down_ends, out_whole, qkv_early, qkv_late, qkv.right, back_own,
            back_across, back_others, down_far, gains, out.right, down_end,
        ) = sync(
            up_whole, gate_end, down_ends, out_whole, qkv_early, qkv_late, grad_qkv, back_own,
            back_across, back_others, down_far, gains, mixed, down_end[1],
        )

        qkv_early = qkv.send(qkv_early, 0)
        down_end = down.send(down_end, 2)
        up_first = up.second_unit(0, up_keep, up_whole)
        up_first, up_keep, back_others, gains, out.right, qkv.right = sync(
            up_first, up_keep, back_others, gains, out.right, qkv.right
        )
        up_first = up.send(up_first, 1)
        others = to_core(back_others)
        gains_there = to_core(gains)
        up_second = up.second_unit(1, up_keep, up_whole)
        out_keep, qkv_keep = out.keep(), qkv.keep()
        both = jnp.concatenate([qkv_late, out.second(out_keep, out_whole)], axis=2)
        others, back_across, down_end = sync(others, back_across, down_end)
        qkv_middle = qkv.second(qkv_keep, qkv_early)
        one_far = (back_across + others[BLOCK:]).astype(jnp.bfloat16)
        (
            qkv_middle, up_first, others, gains, up_second, out_keep, qkv_keep, both, one_far, down_end,
        ) = sync(
            qkv_middle, up_first, others, gains + gains_there, up_second, out_keep, qkv_keep, both,
            one_far, down_end,
        )

        up_end = up.third(up_keep, up_whole, up_first)
        up_end, qkv_middle, both, one_far, gains, gate_end, down_end, down_far = sync(
            up_end, qkv_middle, both, one_far, gains, gate_end, down_end, down_far
        )
        up_end = up.send(up_end, 2)
        qkv_middle = qkv.send(qkv_middle, 1)
        both = qkv.send(both, 0)
        one_far = to_chip(one_far)
        gains_there = to_chip(gains)
        gate_grad = gate.finish(gate_keep, gate_late, gate_middle, gate_end)
        down_grad = down.finish(
            down_keep, down_late, down_middle, down_ends, down_end, turned=True
        )
        (output,) = row_call(
            add_output, (middle, down_own, down_others, down_far), (), (jnp.bfloat16,)
        )
        (
            up_end, qkv_middle, both, one_far, gains, gate_grad, down_grad, up_second, output,
        ) = sync(
            up_end, qkv_middle, both, one_far, gains + gains_there, gate_grad, down_grad, up_second,
            output,
        )
        width = qkv_weight.shape[1]
        qkv_late, out_middle = both[:, :, :width], both[:, :, width:]

        up_second = up.send(up_second, 1)
        ends = jnp.concatenate(
            [
                qkv.third(qkv_keep, qkv_late, qkv_middle),
                out.third(out_keep, out_whole, out_middle),
            ],
            axis=1,
        )
        ends, gains, one_far = sync(ends, gains, one_far)
        ends = qkv.send(ends, 2)
        gains_there = exchange(gains, dp, 1)
        (input_grad,) = row_call(
            input_back,
            (tokens, grad_middle, back_own, others, one_far),
            (attn_gain,),
            (jnp.float32,),
        )
        up_grad = up.finish(up_keep, up_whole, up_second, up_end)
        gains = gains + gains_there
        gains = gains + exchange(gains, dp, 2)
        ends, gains, input_grad, up_grad = sync(ends, gains, input_grad, up_grad)
        step = 4
        while step < dp:
            gains = gains + exchange(gains, dp, step)
            step *= 2
        qkv_grad = qkv.finish(qkv_keep, qkv_late, qkv_middle, ends[:, :width])
        out_grad = out.finish(out_keep, out_whole, out_middle, ends[:, width:], turned=True)
        key_end = query_width + kv_width
        return (
            output,
            input_grad,
            gains[0],
            qkv_grad[:, :query_width],
            qkv_grad[:, query_width:key_end],
            qkv_grad[:, key_end:],
            out_grad,
            gains[1],
            gate_grad,
            up_grad,
            down_grad,
        )

    return local


def solution(mesh):
    rows = P(("dp", "row", "col"), None)
    columns = P(None, ("row", "col"))
    placed = (
        rows,
        P("dp", None),
        P(),
        columns,
        columns,
        columns,
        P(("row", "col"), None),
        P(),
        columns,
        columns,
        P(("row", "col"), None),
        rows,
    )
    summed = P("dp", ("row", "col"))
    turned = P(("row", "col"), "dp")
    return jax.shard_map(
        local_for(mesh.shape["dp"]),
        mesh=mesh,
        in_specs=placed,
        out_specs=(rows, rows, P(), summed, summed, summed, turned, P(), summed, summed, turned),
        check_vma=False,
    )
```

```python
import jax
import jax.numpy as jnp
from jax import lax
from jax.experimental import pallas as pl
from jax.experimental.pallas import tpu as pltpu
from jax.sharding import PartitionSpec as P

HD = 64
EPSILON = 1e-05
MASKED_SCORE = -1e30
BLOCK = 256
TILE = 128
SWAP = ((0, 1), (1, 0))


def positions(segment_ids):
    indices = jnp.arange(segment_ids.shape[-1], dtype=jnp.int32)
    previous = jnp.concatenate([segment_ids[..., :1] - 1, segment_ids[..., :-1]], axis=-1)
    starts = jnp.where(segment_ids != previous, indices, 0)
    return indices - lax.cummax(starts, axis=segment_ids.ndim - 1)


def rope_tables(position):
    exponent = jnp.arange(HD // 2, dtype=jnp.float32) * (-2.0 / HD)
    angles = position.astype(jnp.float32)[:, None] * (10000.0**exponent)[None, :]
    cosine, sine = jnp.cos(angles), jnp.sin(angles)
    return (
        jnp.concatenate([cosine] * 4, axis=1),
        jnp.concatenate([-sine, sine, -sine, sine], axis=1),
    )


def nt(left, right):
    return lax.dot_general(
        left, right, (((1,), (1,)), ((), ())), preferred_element_type=jnp.float32
    )


def nn(left, right):
    return lax.dot_general(
        left, right, (((1,), (0,)), ((), ())), preferred_element_type=jnp.float32
    )


def tn(left, right):
    return lax.dot_general(
        left, right, (((0,), (0,)), ((), ())), preferred_element_type=jnp.float32
    )


def lane_marks():
    lane = lax.broadcasted_iota(jnp.int32, (BLOCK, TILE), 1)
    return lane, lane < HD, lane % HD < HD // 2


def turn_by(values, cosine, sine, first):
    turned = jnp.where(
        first, pltpu.roll(values, TILE - HD // 2, 1), pltpu.roll(values, HD // 2, 1)
    )
    return values * cosine + turned * sine


def rows_of(places, block):
    return pl.ds(pl.multiple_of(places[block], BLOCK), BLOCK)


def segment_column(seg_row, at):
    return jnp.broadcast_to(seg_row[:, at], (TILE, BLOCK)).T


def attend_block(block, places, rotated, keys, values, seg_row, mixed, target, log_sums):
    width = mixed.shape[1]
    lane, low, _ = lane_marks()
    rows = rows_of(places, block)
    at = slice(block * BLOCK, (block + 1) * BLOCK)
    begin = max(0, block - 2) * BLOCK
    span = slice(begin, (block + 1) * BLOCK)
    count = (block + 1) * BLOCK - begin
    key_at = begin + lax.broadcasted_iota(jnp.int32, (BLOCK, count), 1)
    query_at = block * BLOCK + lax.broadcasted_iota(jnp.int32, (BLOCK, count), 0)
    seg_col = segment_column(seg_row, at)[:, :1]
    allowed = (seg_col == seg_row[:, span]) & (key_at <= query_at)
    bias = jnp.where(allowed, 0.0, MASKED_SCORE)
    key_span = keys[span]
    value_span = values[span]

    def one_pair(number, logs):
        columns = pl.ds(pl.multiple_of(number * TILE, TILE), TILE)
        query = rotated[rows, columns]
        results = []
        for half in range(2):
            chosen = jnp.where(low if half == 0 else ~low, query, jnp.zeros_like(query))
            scores = nt(chosen, key_span) + bias
            largest = jnp.max(scores, axis=1, keepdims=True)
            shifted = jnp.exp(scores - largest)
            total = jnp.sum(shifted, axis=1, keepdims=True)
            results.append(nn(shifted.astype(jnp.bfloat16), value_span) * (1.0 / total))
            logs = jnp.where(lane == 2 * number + half, largest + jnp.log(total), logs)
        mixed[target, columns] = jnp.where(low, results[0], results[1]).astype(jnp.bfloat16)
        return logs

    logs = lax.fori_loop(0, width // TILE, one_pair, jnp.zeros((BLOCK, TILE), jnp.float32))
    log_sums[:, at] = logs.T[: log_sums.shape[0]]


def key_value_rows(rotated, rows, keys, values, at, low):
    width = rotated.shape[1] - TILE
    pair = rotated[rows, width:].astype(jnp.float32)
    swapped = pltpu.roll(pair, HD, 1)
    keys[at] = jnp.where(low, pair, swapped).astype(jnp.bfloat16)
    values[at] = jnp.where(low, swapped, pair).astype(jnp.bfloat16)


def attend_side(side, places, rotated, keys, values, seg_row, mixed, log_sums):
    blocks = rotated.shape[0] // BLOCK
    for parity in range(2):

        @pl.when((places[blocks] ^ side) == parity)
        def _():
            for block in range(parity, blocks, 2):
                start = places[block] - side * 2 * BLOCK
                target = pl.ds(pl.multiple_of(start, BLOCK), BLOCK)
                attend_block(
                    block, places, rotated, keys, values, seg_row, mixed, target, log_sums
                )


def attend_far_kernel(
    places, near, across, diagonal, weight, w_out, cosine, sine, seg_row,
    mixed, rotated, log_sums, out_across, out_diagonal, keys, values,
):
    length, total = rotated.shape
    width = total - TILE
    blocks = length // BLOCK
    _, low, first = lane_marks()
    for block in range(blocks):
        rows = rows_of(places, block)
        at = slice(block * BLOCK, (block + 1) * BLOCK)

        def turn_all(proj):
            for start in range(0, width, TILE):
                query = turn_by(proj[:, start : start + TILE], cosine[at], sine[at], first)
                rotated[rows, start : start + TILE] = (query * HD ** (-0.5)).astype(jnp.bfloat16)
            pair = proj[:, width:]
            turned = jnp.where(low, turn_by(pair, cosine[at], sine[at], first), pair)
            rotated[rows, width:] = turned.astype(jnp.bfloat16)

        for piece, source in ((0, None), (1, None), (2, across), (3, diagonal)):

            @pl.when(places[block] == piece * BLOCK)
            def _(piece=piece, source=source):
                if source is None:
                    turn_all(near[piece * BLOCK : (piece + 1) * BLOCK])
                else:
                    turn_all(nn(source[...], weight[...]))

        key_value_rows(rotated, rows, keys, values, at, low)
    attend_side(1, places, rotated, keys, values, seg_row, mixed, log_sums)
    out_diagonal[...] = nn(mixed[BLOCK:], w_out[...]).astype(jnp.bfloat16)
    out_across[...] = nn(mixed[:BLOCK], w_out[...]).astype(jnp.bfloat16)


def attend_near_kernel(
    places, rotated, w_out, seg_row, mixed, log_sums, out_own, out_beside, keys, values
):
    blocks = rotated.shape[0] // BLOCK
    _, low, _ = lane_marks()
    for block in range(blocks):
        at = slice(block * BLOCK, (block + 1) * BLOCK)
        key_value_rows(rotated, rows_of(places, block), keys, values, at, low)
    attend_side(0, places, rotated, keys, values, seg_row, mixed, log_sums)
    out_beside[...] = nn(mixed[BLOCK:], w_out[...]).astype(jnp.bfloat16)
    out_own[...] = nn(mixed[:BLOCK], w_out[...]).astype(jnp.bfloat16)


def attend_back_kernel(
    places, rotated, near_logs, far_logs, cosine, sine, seg_row, w_out, weight,
    from_own, from_beside, from_across, from_diagonal,
    grads, back_own, back_across, back_others,
    keys, values, key_sum, value_sum, grad_mixed, seg_col,
):
    length = rotated.shape[0]
    width = grad_mixed.shape[1]
    blocks = length // BLOCK
    _, low, first = lane_marks()
    for piece, source in enumerate((from_own, from_beside, from_across, from_diagonal)):
        grad_mixed[piece * BLOCK : (piece + 1) * BLOCK] = nt(source[...], w_out[...]).astype(
            jnp.bfloat16
        )
    key_sum[...] = jnp.zeros_like(key_sum)
    value_sum[...] = jnp.zeros_like(value_sum)
    for block in range(blocks):
        at = slice(block * BLOCK, (block + 1) * BLOCK)
        key_value_rows(rotated, rows_of(places, block), keys, values, at, low)
        seg_col[at] = segment_column(seg_row, at)
    def block_back(block, begin):
        rows = rows_of(places, block)
        at = slice(block * BLOCK, (block + 1) * BLOCK)
        is_near = places[blocks] == block % 2
        span = slice(begin, (block + 1) * BLOCK)
        count = (block + 1) * BLOCK - begin
        key_at = begin + lax.broadcasted_iota(jnp.int32, (count, BLOCK), 0)
        query_at = block * BLOCK + lax.broadcasted_iota(jnp.int32, (count, BLOCK), 1)
        allowed = (seg_col[span, :1] == seg_row[:, at]) & (key_at <= query_at)
        bias = jnp.where(allowed, 0.0, MASKED_SCORE)
        key_span = keys[span]
        value_span = values[span]

        def one_pair(number, carry):
            columns = pl.ds(pl.multiple_of(number * TILE, TILE), TILE)
            query = rotated[rows, columns]
            grad = grad_mixed[rows, columns]
            results = []
            for half in range(2):
                side = low if half == 0 else ~low
                chosen = jnp.where(side, query, jnp.zeros_like(query))
                chosen_grad = jnp.where(side, grad, jnp.zeros_like(grad))
                head = pl.ds(2 * number + half, 1)
                logs = jnp.where(is_near, near_logs[head, at], far_logs[head, at])
                probs = jnp.exp(nt(key_span, chosen) + bias - logs)
                grad_probs = nt(value_span, chosen_grad)
                inner = jnp.sum(probs * grad_probs, axis=0, keepdims=True)
                grad_scores = (probs * (grad_probs - inner)).astype(jnp.bfloat16)
                value_sum[span] += nn(probs.astype(jnp.bfloat16), chosen_grad)
                key_sum[span] += nn(grad_scores, chosen)
                results.append(tn(grad_scores, key_span))
            grad_query = jnp.where(low, results[0], results[1]) * HD ** (-0.5)
            grads[rows, columns] = turn_by(grad_query, cosine[at], -sine[at], first).astype(
                jnp.bfloat16
            )
            return carry

        lax.fori_loop(0, width // TILE, one_pair, 0)
    for block in range(blocks):
        if block < 2:
            block_back(block, 0)
            continue
        for back in (1, 2):

            @pl.when(places[blocks - 1 + block] == back - 1)
            def _(block=block, back=back):
                block_back(block, (block - back) * BLOCK)

    for block in range(blocks):
        rows = rows_of(places, block)
        at = slice(block * BLOCK, (block + 1) * BLOCK)
        grad_key = key_sum[at]
        grad_key = turn_by(grad_key + pltpu.roll(grad_key, HD, 1), cosine[at], -sine[at], first)
        grad_value = value_sum[at]
        grad_value = grad_value + pltpu.roll(grad_value, HD, 1)
        grads[rows, width:] = jnp.where(low, grad_key, grad_value).astype(jnp.bfloat16)
    targets = (back_own, back_others.at[:BLOCK], back_across, back_others.at[BLOCK:])
    for piece, target in enumerate(targets):
        grad_rows = grads[piece * BLOCK : (piece + 1) * BLOCK]
        target[...] = nt(grad_rows, weight[...]).astype(jnp.bfloat16)


SMEM = pl.BlockSpec(memory_space=pltpu.SMEM)
VMEM = pl.BlockSpec(memory_space=pltpu.VMEM)


ANY = pl.BlockSpec(memory_space=pl.ANY)
LITTLE = pl.CostEstimate(flops=1 << 20, bytes_accessed=1 << 12, transcendentals=0)


def params(limit):
    return pltpu.CompilerParams(vmem_limit_bytes=limit << 20)


def attend_far(places, near, across, diagonal, weight, w_out, cosine, sine, seg_row):
    length, total = 2 * near.shape[0], near.shape[1]
    width = total - TILE
    depth = w_out.shape[1]
    block = jax.ShapeDtypeStruct((BLOCK, depth), jnp.bfloat16)
    return pl.pallas_call(
        attend_far_kernel,
        out_shape=(
            jax.ShapeDtypeStruct((length // 2, width), jnp.bfloat16),
            jax.ShapeDtypeStruct((length, total), jnp.bfloat16),
            jax.ShapeDtypeStruct((width // HD, length), jnp.float32),
            block,
            block,
        ),
        in_specs=[SMEM] + [VMEM] * 8,
        out_specs=(VMEM,) * 5,
        scratch_shapes=[pltpu.VMEM((length, TILE), jnp.bfloat16)] * 2,
        compiler_params=params(48),
        cost_estimate=LITTLE,
        name="attend_far",
    )(places, near, across, diagonal, weight, w_out, cosine, sine, seg_row)


def attend_near(places, rotated, w_out, seg_row):
    length, total = rotated.shape
    width = total - TILE
    depth = w_out.shape[1]
    block = jax.ShapeDtypeStruct((BLOCK, depth), jnp.bfloat16)
    return pl.pallas_call(
        attend_near_kernel,
        out_shape=(
            jax.ShapeDtypeStruct((length // 2, width), jnp.bfloat16),
            jax.ShapeDtypeStruct((width // HD, length), jnp.float32),
            block,
            block,
        ),
        in_specs=[SMEM] + [VMEM] * 3,
        out_specs=(VMEM,) * 4,
        scratch_shapes=[pltpu.VMEM((length, TILE), jnp.bfloat16)] * 2,
        compiler_params=params(48),
        cost_estimate=LITTLE,
        name="attend_near",
    )(places, rotated, w_out, seg_row)


def attend_back(
    places, rotated, near_logs, far_logs, cosine, sine, seg_row, w_out, weight, pieces
):
    length, total = rotated.shape
    return pl.pallas_call(
        attend_back_kernel,
        out_shape=(jax.ShapeDtypeStruct((length, total), jnp.bfloat16),)
        + (jax.ShapeDtypeStruct(pieces[0].shape, jnp.bfloat16),) * 2
        + (jax.ShapeDtypeStruct((2 * BLOCK, pieces[0].shape[1]), jnp.bfloat16),),
        in_specs=[SMEM] + [VMEM] * 12,
        out_specs=(VMEM,) * 4,
        scratch_shapes=[pltpu.VMEM((length, TILE), jnp.bfloat16)] * 2
        + [pltpu.VMEM((length, TILE), jnp.float32)] * 2
        + [
            pltpu.VMEM((length, total - TILE), jnp.bfloat16),
            pltpu.VMEM((length, TILE), jnp.int32),
        ],
        compiler_params=params(52),
        cost_estimate=LITTLE,
        name="attend_back",
    )(
        places, rotated, near_logs, far_logs, cosine, sine, seg_row, w_out, weight, *pieces
    )


def terms_kernel(starts, units, one, two, three, four, right, *outs):
    left = jnp.concatenate([one[...], two[...], three[...], four[...]], axis=0)
    total = tn(left, right[...]).astype(jnp.bfloat16)
    step = pl.program_id(0)
    for out, start, end in zip(outs, starts, starts[1:]):

        @pl.when((step >= start) & (step < end))
        def _(out=out):
            out[0] = total


def weight_terms(pieces, right, units, first, sizes):
    count = pieces[0].shape[0]
    rows, width = right.shape
    starts = [sum(sizes[:number]) for number in range(len(sizes) + 1)]
    return pl.pallas_call(
        lambda *refs: terms_kernel(starts, *refs),
        grid_spec=pltpu.PrefetchScalarGridSpec(
            num_scalar_prefetch=1,
            grid=(starts[-1],),
            in_specs=[pl.BlockSpec((count, BLOCK), lambda i, units: (0, units[first + i]))] * 4
            + [pl.BlockSpec((rows, width), lambda i, units: (0, 0))],
            out_specs=[
                pl.BlockSpec(
                    (1, BLOCK, width),
                    lambda i, units, start=start, size=size: (
                        jnp.clip(i - start, 0, size - 1),
                        0,
                        0,
                    ),
                )
                for start, size in zip(starts, sizes)
            ],
        ),
        out_shape=[jax.ShapeDtypeStruct((size, BLOCK, width), jnp.bfloat16) for size in sizes],
        compiler_params=params(60),
        cost_estimate=LITTLE,
        name="weight_terms",
    )(units, *pieces, right)


def pair_kernel(each, units, *refs):
    left, right, outs = refs[:8], refs[8:10], refs[10:]
    for number, out in enumerate(outs):

        @pl.when(pl.program_id(0) // each == number)
        def _(number=number, out=out):
            pieces = [ref[...] for ref in left[4 * number : 4 * number + 4]]
            total = tn(jnp.concatenate(pieces, axis=0), right[number][...])
            out[0] = total.astype(jnp.bfloat16)


def weight_pair(sums, first, size):
    count = sums[0].pieces[0].shape[0]
    rows, width = sums[0].right.shape

    def step(i, number):
        return jnp.clip(i - number * size, 0, size - 1)

    specs = []
    for number, each in enumerate(sums):
        specs += [
            pl.BlockSpec(
                (count, BLOCK),
                lambda i, units, number=number, start=each.base + first: (
                    0,
                    units[start + step(i, number)],
                ),
            )
        ] * 4
    return pl.pallas_call(
        lambda *refs: pair_kernel(size, *refs),
        grid_spec=pltpu.PrefetchScalarGridSpec(
            num_scalar_prefetch=1,
            grid=(2 * size,),
            in_specs=specs + [pl.BlockSpec((rows, width), lambda i, units: (0, 0))] * 2,
            out_specs=[
                pl.BlockSpec(
                    (1, BLOCK, width), lambda i, units, number=number: (step(i, number), 0, 0)
                )
                for number in range(2)
            ],
        ),
        out_shape=[jax.ShapeDtypeStruct((size, BLOCK, width), jnp.bfloat16)] * 2,
        compiler_params=params(60),
        cost_estimate=LITTLE,
        name="weight_pair",
    )(sums[0].units, *sums[0].pieces, *sums[1].pieces, sums[0].right, sums[1].right)


def exchange(values, dp, distance):
    return lax.ppermute(values, "dp", [(device, device ^ distance) for device in range(dp)])


def numbered(bits, values, free):
    fixed = jnp.zeros((), jnp.int32)
    for bit, value in zip(bits, values):
        fixed = fixed + bit * value
    numbers = [fixed]
    for bit in free:
        numbers = [number + add for number in numbers for add in (0, bit)]
    return jnp.stack(numbers).astype(jnp.int32)


ORDERS = ((1, 2, 4), (2, 1, 4))


def unit_table(dp):
    unit = lax.axis_index("dp") // (dp // 8)
    numbers = []
    for order in ORDERS:
        one, two, three = ((unit // bit) % 2 for bit in order)
        numbers += [
            sum(bit * value for bit, value in zip(order, values))
            for values in (
                (first, second, third)
                for first in (1 - one, one)
                for second in (1 - two, two)
                for third in (1 - three, three)
            )
        ]
    return jnp.stack(numbers).astype(jnp.int32)


class DpSum:
    def __init__(self, pieces, right, order, dp, units):
        self.pieces, self.right, self.order, self.dp, self.units = pieces, right, order, dp, units
        self.base = 8 * ORDERS.index(order)

    def terms(self, first, *sizes):
        return weight_terms(self.pieces, self.right, self.units, self.base + first, sizes)

    def whole(self):
        return self.terms(0, 4)[0]

    def halves(self):
        return self.terms(0, 2, 2)

    def keep(self):
        return self.terms(4, 4)[0]

    def whole_and_keep(self):
        return self.terms(0, 4, 4)

    def send(self, values, step):
        return exchange(values, self.dp, self.order[step] * (self.dp // 8))

    def second(self, keep, early):
        return add_up([keep[:2], early[:2]]).astype(jnp.bfloat16)

    def second_unit(self, number, keep, early):
        return add_up([keep[number : number + 1], early[number : number + 1]]).astype(jnp.bfloat16)

    def third(self, keep, late, middle):
        at = late.shape[0] - 2
        return add_up([keep[2], late[at], middle[0]]).astype(jnp.bfloat16)

    def finish(self, keep, late, middle, *ends, turned=False):
        if self.dp == 8:
            return finish_sum(keep, late, middle, ends, turned)
        total = finish_sum(keep, late, middle, ends, False)
        index, left = lax.axis_index("dp"), self.dp // 8
        while left > 1:
            left //= 2
            bit = (index // left) % 2
            parts = total.reshape(2, total.shape[0] // 2, total.shape[1])
            there = exchange(pick(parts, 1 - bit, 0).astype(jnp.bfloat16), self.dp, left)
            total = pick(parts, bit, 0) + there.astype(jnp.float32)
        return total.T if turned else total


def finish_kernel(turned, ends, keep, late, middle, *refs):
    out = refs[-1]
    end = refs[0][...].astype(jnp.float32)
    if ends == 2:
        end = jnp.where(pl.program_id(0) == 0, end, refs[1][...].astype(jnp.float32))
    total = keep[0].astype(jnp.float32) + late[0].astype(jnp.float32)
    total = total + middle[0].astype(jnp.float32) + end
    out[...] = total.T if turned else total


def finish_sum(keep, late, middle, ends, turned):
    _, rows, columns = keep.shape
    size = rows // 2
    specs = [
        pl.BlockSpec((1, size, columns), lambda i, at=array.shape[0] - 1: (at, i, 0))
        for array in (keep, late, middle)
    ]
    end = pl.BlockSpec((size, columns), lambda i: (0 if len(ends) == 2 else i, 0))
    shape = (columns, rows) if turned else (rows, columns)
    out = (
        pl.BlockSpec((columns, size), lambda i: (0, i))
        if turned
        else pl.BlockSpec((size, columns), lambda i: (i, 0))
    )
    return pl.pallas_call(
        lambda *refs: finish_kernel(turned, len(ends), *refs),
        grid=(2,),
        in_specs=specs + [end] * len(ends),
        out_specs=out,
        out_shape=jax.ShapeDtypeStruct(shape, jnp.float32),
        compiler_params=params(40),
        cost_estimate=LITTLE,
        name="finish_sum",
    )(keep, late, middle, *ends)


def finish_three_kernel(keep, late, middle, end, *outs):
    total = keep[0].astype(jnp.float32) + late[0].astype(jnp.float32)
    total = total + middle[0].astype(jnp.float32) + end[...].astype(jnp.float32)
    at = 0
    for out in outs:
        out[...] = total[:, at : at + out.shape[1]]
        at += out.shape[1]


def finish_three(keep, late, middle, end, widths):
    _, rows, columns = keep.shape
    size = rows // 2
    specs = [
        pl.BlockSpec((1, size, columns), lambda i, at=array.shape[0] - 1: (at, i, 0))
        for array in (keep, late, middle)
    ]
    return pl.pallas_call(
        finish_three_kernel,
        grid=(2,),
        in_specs=specs + [pl.BlockSpec((size, columns), lambda i: (i, 0))],
        out_specs=[pl.BlockSpec((size, width), lambda i: (i, 0)) for width in widths],
        out_shape=[jax.ShapeDtypeStruct((rows, width), jnp.float32) for width in widths],
        compiler_params=params(40),
        cost_estimate=LITTLE,
        name="finish_three",
    )(keep, late, middle, end)


def row_call(kernel, rows, wholes, outs, totals=0):
    count, depth = rows[0].shape
    size = 64
    block = pl.BlockSpec((size, depth), lambda i: (i, 0))
    whole = pl.BlockSpec((1, depth), lambda i: (0, 0))
    return pl.pallas_call(
        kernel,
        grid=(count // size,),
        in_specs=[block] * len(rows) + [whole] * len(wholes),
        out_specs=(block,) * len(outs) + (whole,) * totals,
        out_shape=tuple(jax.ShapeDtypeStruct((count, depth), kind) for kind in outs)
        + (jax.ShapeDtypeStruct((1, depth), jnp.float32),) * totals,
        compiler_params=params(40),
        cost_estimate=LITTLE,
        name=kernel.__name__,
    )(*rows, *(array.reshape(1, depth) for array in wholes))


def normalize_two(one, two, gain, *outs):
    for rows, out in zip((one, two), outs):
        values = rows[...].astype(jnp.float32)
        inverse = lax.rsqrt(jnp.mean(values * values, axis=-1, keepdims=True) + EPSILON)
        out[...] = (values * inverse * gain[...]).astype(jnp.bfloat16)


def scale_back(values, grads, gain):
    inverse = lax.rsqrt(jnp.mean(values * values, axis=-1, keepdims=True) + EPSILON)
    unit = values * inverse
    scaled = grads * gain
    return unit, inverse * (scaled - unit * jnp.mean(scaled * unit, axis=-1, keepdims=True))


def middle_back(middle, cot, one, two, three, gain, grad_middle, rounded, gain_grad):
    grads = one[...].astype(jnp.float32) + two[...].astype(jnp.float32) + three[...].astype(jnp.float32)
    unit, back = scale_back(middle[...], grads, gain[...])
    total = cot[...].astype(jnp.float32) + back
    grad_middle[...] = total
    rounded[...] = total.astype(jnp.bfloat16)

    @pl.when(pl.program_id(0) == 0)
    def _():
        gain_grad[...] = jnp.zeros_like(gain_grad)

    gain_grad[...] += jnp.sum(grads * unit, axis=0, keepdims=True)


def input_back(tokens, grad_middle, one, two, three, gain, input_grad):
    grads = one[...].astype(jnp.float32) + two[...].astype(jnp.float32) + three[...].astype(jnp.float32)
    _, back = scale_back(tokens[...].astype(jnp.float32), grads, gain[...])
    input_grad[...] = grad_middle[...] + back


def add_output(middle, one, two, three, output):
    total = middle[...] + one[...].astype(jnp.float32) + two[...].astype(jnp.float32)
    output[...] = (total + three[...].astype(jnp.float32)).astype(jnp.bfloat16)


def sync(*values):
    return lax.optimization_barrier(values)


def column_tiles(width, most=256):
    return [(at, min(most, width - at)) for at in range(0, width, most)]


def feed_near_kernel(one, two, cot_one, cot_two, w_gate, w_up, w_down, *rest):
    hidden, grad_gate, grad_up, back_one, back_two = rest[:5]
    rows, cots, gate, up, down, gates, ups, sems = rest[5:]
    sources = (one, two, w_gate, w_up, cot_one, cot_two, w_down)
    feed_steps(sources, rest[5:], hidden, grad_gate, grad_up)
    count = back_one.shape[0]
    for at, size in column_tiles(gate.shape[0]):
        span = slice(at, at + size)
        total = nt(grad_gate[...], gate[span]) + nt(grad_up[...], up[span])
        back_one[:, span] = total[:count].astype(jnp.bfloat16)
        back_two[:, span] = total[count:].astype(jnp.bfloat16)


def feed_far_kernel(units, one, two, cot_one, cot_two, w_gate, w_up, w_down, *rest):
    near_one, near_two, near_cot_one, near_cot_two, held_hidden, held_gate, _ = rest[:7]
    hidden, grad_gate, grad_up, gate_early, down_early = rest[7:12]
    near_rows, near_cots, near_hidden, near_gate, near_sems = rest[12:17]
    scratch = rest[17:]
    rows, cots = scratch[:2]
    count = one.shape[0]
    moves = [
        pltpu.make_async_copy(held_hidden.at[: 2 * count], near_hidden, near_sems.at[0]),
        pltpu.make_async_copy(held_gate.at[: 2 * count], near_gate, near_sems.at[1]),
    ]
    lefts = (
        (near_one, near_rows, 0, 0),
        (near_two, near_rows, count, 0),
        (near_cot_one, near_cots, 0, 8),
        (near_cot_two, near_cots, count, 8),
    )
    for number, (source, target, start, first) in enumerate(lefts):
        for unit in range(2):
            columns = pl.ds(pl.multiple_of(units[first + unit] * BLOCK, BLOCK), BLOCK)
            moves.append(
                pltpu.make_async_copy(
                    source.at[:, columns],
                    target.at[unit, start : start + count],
                    near_sems.at[2 + 2 * number + unit],
                )
            )
    sources = (one, two, w_gate, w_up, cot_one, cot_two, w_down)
    feed_steps(sources, scratch, hidden, grad_gate, grad_up, moves)
    for first, left, far_left, near_right, far_right, out in (
        (0, near_rows, rows, near_gate, grad_gate, gate_early),
        (8, near_cots, cots, near_hidden, hidden, down_early),
    ):
        for unit in range(2):
            columns = pl.ds(pl.multiple_of(units[first + unit] * BLOCK, BLOCK), BLOCK)
            total = tn(left[unit], near_right[...]) + tn(far_left[:, columns], far_right[...])
            out[unit] = total.astype(jnp.bfloat16)


def feed_steps(sources, scratch, hidden, grad_gate, grad_up, more=()):
    rows, cots, gate, up, down, gates, ups, sems = scratch
    count = sources[0].shape[0]
    targets = (
        rows.at[:count], rows.at[count:], gate, up, cots.at[:count], cots.at[count:], down,
    )
    moves = [
        pltpu.make_async_copy(source, target, sems.at[number])
        for number, (source, target) in enumerate(zip(sources, targets))
    ]
    for move in (*moves, *more):
        move.start()
    for move in moves[:3]:
        move.wait()
    tiles = column_tiles(gate.shape[1])
    for at, size in tiles:
        gates[:, at : at + size] = nn(rows[...], gate[:, at : at + size])
    moves[3].wait()
    for at, size in tiles:
        ups[:, at : at + size] = nn(rows[...], up[:, at : at + size])
    for move in moves[4:]:
        move.wait()
    for at, size in tiles:
        span = slice(at, at + size)
        grad_hidden = nt(cots[...], down[span])
        gate_pre = gates[:, span]
        up_pre = ups[:, span]
        sigmoid = jax.nn.sigmoid(gate_pre)
        silu = gate_pre * sigmoid
        hidden[:, span] = (silu * up_pre).astype(jnp.bfloat16)
        slope = sigmoid + silu * (1.0 - sigmoid)
        grad_gate[:, span] = (grad_hidden * up_pre * slope).astype(jnp.bfloat16)
        grad_up[:, span] = (grad_hidden * silu).astype(jnp.bfloat16)
    for move in more:
        move.wait()


def feed_scratch(count, depth, width):
    return (
        [pltpu.VMEM((2 * count, depth), jnp.bfloat16)] * 2
        + [pltpu.VMEM((depth, width), jnp.bfloat16)] * 2
        + [
            pltpu.VMEM((width, depth), jnp.bfloat16),
            pltpu.VMEM((2 * count, width), jnp.float32),
            pltpu.VMEM((2 * count, width), jnp.float32),
            pltpu.SemaphoreType.DMA((7,)),
        ]
    )


def feed_near(pair, cots, w_gate, w_up, w_down):
    count, depth = pair[0].shape
    width = w_gate.shape[1]
    return pl.pallas_call(
        feed_near_kernel,
        grid=(1,),
        out_shape=(jax.ShapeDtypeStruct((4 * count, width), jnp.bfloat16),) * 3
        + (jax.ShapeDtypeStruct((count, depth), jnp.bfloat16),) * 2,
        in_specs=[ANY] * 7,
        out_specs=(pl.BlockSpec((2 * count, width), lambda i: (0, 0)),) * 3
        + (pl.BlockSpec((count, depth), lambda i: (0, 0)),) * 2,
        scratch_shapes=feed_scratch(count, depth, width),
        compiler_params=params(56),
        cost_estimate=LITTLE,
        name="feed_near",
    )(*pair, *cots, w_gate, w_up, w_down)


def feed_far(units, blocks, cots, w_gate, w_up, w_down, held):
    count, depth = blocks[0].shape
    width = w_gate.shape[1]
    early = jax.ShapeDtypeStruct((2, BLOCK, width), jnp.bfloat16)
    return pl.pallas_call(
        feed_far_kernel,
        grid_spec=pltpu.PrefetchScalarGridSpec(
            num_scalar_prefetch=1,
            grid=(1,),
            in_specs=[ANY] * 14,
            out_specs=(pl.BlockSpec((2 * count, width), lambda i, units: (1, 0)),) * 3
            + (pl.BlockSpec((2, BLOCK, width), lambda i, units: (0, 0, 0)),) * 2,
            scratch_shapes=[pltpu.VMEM((2, 2 * count, BLOCK), jnp.bfloat16)] * 2
            + [pltpu.VMEM((2 * count, width), jnp.bfloat16)] * 2
            + [pltpu.SemaphoreType.DMA((10,))]
            + feed_scratch(count, depth, width),
        ),
        out_shape=(jax.ShapeDtypeStruct((4 * count, width), jnp.bfloat16),) * 3 + (early,) * 2,
        input_output_aliases={12: 0, 13: 1, 14: 2},
        compiler_params=params(60),
        cost_estimate=LITTLE,
        name="feed_far",
    )(units, *blocks[2:], *cots[2:], w_gate, w_up, w_down, *blocks[:2], *cots[:2], *held)


def feed_back_kernel(grad_gate, grad_up, w_gate, w_up, one, two):
    total = nt(grad_gate[...], w_gate[...]) + nt(grad_up[...], w_up[...])
    total = total.astype(jnp.bfloat16)
    one[...] = total[: one.shape[0]]
    two[...] = total[one.shape[0] :]


def feed_back(side, grad_gate, grad_up, w_gate, w_up):
    count = grad_gate.shape[0] // 4
    depth, width = w_gate.shape
    size = 256
    rows = pl.BlockSpec((2 * count, width), lambda i: (side, 0))
    weights = pl.BlockSpec((size, width), lambda i: (i, 0))
    outs = pl.BlockSpec((count, size), lambda i: (0, i))
    return pl.pallas_call(
        feed_back_kernel,
        grid=(depth // size,),
        out_shape=(jax.ShapeDtypeStruct((count, depth), jnp.bfloat16),) * 2,
        in_specs=[rows, rows, weights, weights],
        out_specs=(outs, outs),
        compiler_params=params(60),
        cost_estimate=LITTLE,
        name="feed_back",
    )(grad_gate, grad_up, w_gate, w_up)


def feed_down_kernel(hidden, w_down, own, across, others):
    total = nn(hidden[...], w_down[...]).astype(jnp.bfloat16)
    count = own.shape[0]
    own[...] = total[:count]
    others[:count] = total[count : 2 * count]
    across[...] = total[2 * count : 3 * count]
    others[count:] = total[3 * count :]


def feed_down(hidden, w_down):
    count = hidden.shape[0] // 4
    width, depth = w_down.shape
    size = 512
    block = pl.BlockSpec((count, size), lambda i: (0, i))
    return pl.pallas_call(
        feed_down_kernel,
        grid=(depth // size,),
        out_shape=(jax.ShapeDtypeStruct((count, depth), jnp.bfloat16),) * 2
        + (jax.ShapeDtypeStruct((2 * count, depth), jnp.bfloat16),),
        in_specs=[
            pl.BlockSpec((4 * count, width), lambda i: (0, 0)),
            pl.BlockSpec((width, size), lambda i: (0, i)),
        ],
        out_specs=(block, block, pl.BlockSpec((2 * count, size), lambda i: (0, i))),
        compiler_params=params(60),
        cost_estimate=LITTLE,
        name="feed_down",
    )(hidden, w_down)


def to_core(values):
    return lax.ppermute(values, "row", SWAP)


def to_chip(values):
    return lax.ppermute(values, "col", SWAP)


def gather_blocks(own):
    across = to_chip(own)
    return own, to_core(own), across, to_core(across)


def scatter_far(across, diagonal):
    return to_chip((across + to_core(diagonal)).astype(jnp.bfloat16))


def pick(values, index, axis):
    return lax.dynamic_index_in_dim(values, index, axis, keepdims=False)


def add_up(terms):
    total = terms[0].astype(jnp.float32)
    for term in terms[1:]:
        total = total + term.astype(jnp.float32)
    return total


def local_for(dp):
    def local(
        tokens,
        segments,
        attn_gain,
        w_query,
        w_key,
        w_value,
        w_out,
        ffn_gain,
        w_gate,
        w_up,
        w_down,
        out_cotangent,
    ):
        query_width = w_query.shape[1]
        kv_width = w_key.shape[1]
        length = segments.shape[1]
        row, col = lax.axis_index("row"), lax.axis_index("col")
        places = [
            (((block // 2) ^ row) + 2 * ((block % 2) ^ col)) * (length // 4) for block in range(4)
        ]
        reaches = [
            segments[0, (block - 1) * BLOCK - 1] == segments[0, block * BLOCK]
            for block in range(2, length // BLOCK)
        ]
        places = jnp.stack([number.astype(jnp.int32) for number in places + [col] + reaches])

        across_raw = to_chip(tokens)
        inputs = tokens.astype(jnp.float32)
        inverse_one = lax.rsqrt(jnp.mean(inputs * inputs, axis=-1, keepdims=True) + EPSILON)
        unit_one = inputs * inverse_one
        normed_one = (unit_one * attn_gain).astype(jnp.bfloat16)
        beside_one = to_core(normed_one)
        qkv_weight = jnp.concatenate([w_query, w_key, w_value], axis=1)
        cosine, sine = rope_tables(positions(segments).reshape(length))
        seg_row = segments.reshape(1, length)
        near = nn(jnp.concatenate([normed_one, beside_one], axis=0), qkv_weight)
        across_raw, near, cot, cosine, sine, units = sync(
            across_raw, near, out_cotangent, cosine, sine, unit_table(dp)
        )
        across_cot = to_chip(cot)
        beside_cot = to_core(cot)
        diagonal_raw = to_core(across_raw)
        across_one, diagonal_one = row_call(
            normalize_two, (across_raw, diagonal_raw), (attn_gain,), (jnp.bfloat16, jnp.bfloat16)
        )
        blocks_one = (normed_one, beside_one, across_one, diagonal_one)
        far_mixed, rotated, far_logs, out_across, out_diagonal = attend_far(
            places, near, across_one, diagonal_one, qkv_weight, w_out, cosine, sine, seg_row
        )
        out_across, out_diagonal, rotated, across_cot, beside_cot = sync(
            out_across, out_diagonal, rotated, across_cot, beside_cot
        )
        out_diagonal = to_core(out_diagonal)
        out_across, out_diagonal, rotated, across_cot = sync(
            out_across, out_diagonal, rotated, across_cot
        )
        diagonal_cot = to_core(across_cot)
        far_out = to_chip((out_across + out_diagonal).astype(jnp.bfloat16))
        near_mixed, near_logs, out_own, out_beside = attend_near(
            places, rotated, w_out, seg_row
        )
        far_out, out_own, out_beside, diagonal_cot = sync(
            far_out, out_own, out_beside, diagonal_cot
        )
        cots = (out_cotangent, beside_cot, across_cot, diagonal_cot)
        out_beside = to_core(out_beside)
        middle = add_up([inputs, out_own, out_beside, far_out])
        inverse_two = lax.rsqrt(jnp.mean(middle * middle, axis=-1, keepdims=True) + EPSILON)
        unit_two = middle * inverse_two
        normed_two = (unit_two * ffn_gain).astype(jnp.bfloat16)
        across_two = to_chip(normed_two)
        beside_two = to_core(normed_two)
        mixed = jnp.concatenate([near_mixed, far_mixed], axis=0)
        *parts, back_own, back_beside = feed_near(
            (normed_two, beside_two), cots[:2], w_gate, w_up, w_down
        )
        parts, across_two, mixed, back_own, back_beside = sync(
            parts, across_two, mixed, back_own, back_beside
        )
        diagonal_two = to_core(across_two)
        back_beside = to_core(back_beside)
        blocks_two = (normed_two, beside_two, across_two, diagonal_two)
        gate = DpSum(blocks_two, None, (1, 2, 4), dp, units)
        down = DpSum(cots, None, (2, 1, 4), dp, units)
        hidden, grad_gate, grad_up, gate_early, down_early = feed_far(
            units, blocks_two, cots, w_gate, w_up, w_down, parts
        )
        gate_early, down_early, grad_gate, grad_up, hidden, back_beside = sync(
            gate_early, down_early, grad_gate, grad_up, hidden, back_beside
        )

        gate.right, down.right = grad_gate, hidden
        up = DpSum(blocks_two, grad_up, (1, 2, 4), dp, units)
        gate_early = gate.send(gate_early, 0)
        down_early = down.send(down_early, 0)
        far_across, far_diagonal = feed_back(1, grad_gate, grad_up, w_gate, w_up)
        far_diagonal = to_core(far_diagonal)
        gate_late, down_late = weight_pair((gate, down), 2, 2)
        back_far = (far_across + far_diagonal).astype(jnp.bfloat16)
        gate_early, down_early, back_far, gate_late, down_late, gate.right, down.right, up.right = sync(
            gate_early, down_early, back_far, gate_late, down_late, grad_gate, hidden, grad_up
        )

        gate_late = gate.send(gate_late, 0)
        down_late = down.send(down_late, 0)
        back_far = to_chip(back_far)
        gate_keep, down_keep = weight_pair((gate, down), 4, 4)
        gate_middle = gate.second(gate_keep, gate_early)
        down_middle = down.second(down_keep, down_early)
        down_own, down_across, down_others = feed_down(down.right, w_down)
        (
            gate_late, down_late, back_far, gate_middle, down_middle, up.right, down_own, down_across,
            down_others,
        ) = sync(
            gate_late, down_late, back_far, gate_middle, down_middle, up.right, down_own, down_across,
            down_others,
        )

        gate_middle = gate.send(gate_middle, 1)
        down_middle = down.send(down_middle, 1)
        grad_middle, from_own, gain_two_grad = row_call(
            middle_back,
            (middle, out_cotangent, back_own, back_beside, back_far),
            (ffn_gain,),
            (jnp.float32, jnp.bfloat16),
            1,
        )
        from_across = to_chip(from_own)
        from_beside = to_core(from_own)
        up_whole, up_keep = up.whole_and_keep()
        down_others = to_core(down_others)
        down_far = (down_across + down_others[BLOCK:]).astype(jnp.bfloat16)
        (
            gate_middle, down_middle, from_across, from_beside, up_whole, up_keep, down_others, down_far,
        ) = sync(
            gate_middle, down_middle, from_across, from_beside, up_whole, up_keep, down_others, down_far
        )

        up_whole = up.send(up_whole, 0)
        gate_end = gate.third(gate_keep, gate_late, gate_middle)
        gate_end, from_across, down_keep = sync(gate_end, from_across, down_keep)
        gate_end = gate.send(gate_end, 2)
        from_diagonal = to_core(from_across)
        half = BLOCK // 2
        down_end = tuple(
            down.third(down_keep[:, rows], down_late[:, rows], down_middle[:, rows])
            for rows in (slice(0, half), slice(half, BLOCK))
        )
        down_end, from_diagonal = sync(down_end, from_diagonal)
        down_ends = down.send(down_end[0], 2)
        down_far = to_chip(down_far)
        grad_attn = (from_own, from_beside, from_across, from_diagonal)
        out = DpSum(grad_attn, mixed, (2, 1, 4), dp, units)
        out_whole = out.send(out.whole(), 0)
        grad_qkv, back_own, back_across, back_others = attend_back(
            places, rotated, near_logs, far_logs, cosine, sine, seg_row, w_out, qkv_weight, grad_attn
        )
        qkv = DpSum(blocks_one, grad_qkv, (1, 2, 4), dp, units)
        qkv_early, qkv_late = qkv.halves()
        gain_one_grad = sum(
            jnp.sum(part.astype(jnp.float32) * block.astype(jnp.float32), axis=0)
            for part, block in zip(
                (back_own, back_others[:BLOCK], back_across, back_others[BLOCK:]), blocks_one
            )
        )
        gains = jnp.stack([gain_one_grad / attn_gain, gain_two_grad[0]])
        (
            up_whole, gate_end, down_ends, out_whole, qkv_early, qkv_late, qkv.right, back_own,
            back_across, back_others, down_far, gains, out.right, down_end,
        ) = sync(
            up_whole, gate_end, down_ends, out_whole, qkv_early, qkv_late, grad_qkv, back_own,
            back_across, back_others, down_far, gains, mixed, down_end[1],
        )

        qkv_early = qkv.send(qkv_early, 0)
        down_end = down.send(down_end, 2)
        up_first = up.second_unit(0, up_keep, up_whole)
        up_first, up_keep, back_others, gains, out.right, qkv.right = sync(
            up_first, up_keep, back_others, gains, out.right, qkv.right
        )
        up_first = up.send(up_first, 1)
        others = to_core(back_others)
        gains_there = to_core(gains)
        up_second = up.second_unit(1, up_keep, up_whole)
        out_keep, qkv_keep = out.keep(), qkv.keep()
        both = jnp.concatenate([qkv_late, out.second(out_keep, out_whole)], axis=2)
        others, back_across, down_end = sync(others, back_across, down_end)
        qkv_middle = qkv.second(qkv_keep, qkv_early)
        one_far = (back_across + others[BLOCK:]).astype(jnp.bfloat16)
        (
            qkv_middle, up_first, others, gains, up_second, out_keep, qkv_keep, both, one_far, down_end,
        ) = sync(
            qkv_middle, up_first, others, gains + gains_there, up_second, out_keep, qkv_keep, both,
            one_far, down_end,
        )

        up_end = up.third(up_keep, up_whole, up_first)
        up_end, qkv_middle, both, one_far, gains, gate_end, down_end, down_far = sync(
            up_end, qkv_middle, both, one_far, gains, gate_end, down_end, down_far
        )
        up_end = up.send(up_end, 2)
        qkv_middle = qkv.send(qkv_middle, 1)
        both = qkv.send(both, 0)
        one_far = to_chip(one_far)
        gains_there = to_chip(gains)
        gate_grad = gate.finish(gate_keep, gate_late, gate_middle, gate_end)
        down_grad = down.finish(
            down_keep, down_late, down_middle, down_ends, down_end, turned=True
        )
        (output,) = row_call(
            add_output, (middle, down_own, down_others, down_far), (), (jnp.bfloat16,)
        )
        (
            up_end, qkv_middle, both, one_far, gains, gate_grad, down_grad, up_second, output,
        ) = sync(
            up_end, qkv_middle, both, one_far, gains + gains_there, gate_grad, down_grad, up_second,
            output,
        )
        width = qkv_weight.shape[1]
        qkv_late, out_middle = both[:, :, :width], both[:, :, width:]

        up_second = up.send(up_second, 1)
        ends = jnp.concatenate(
            [
                qkv.third(qkv_keep, qkv_late, qkv_middle),
                out.third(out_keep, out_whole, out_middle),
            ],
            axis=1,
        )
        ends, gains, one_far = sync(ends, gains, one_far)
        ends = qkv.send(ends, 2)
        gains_there = exchange(gains, dp, 1)
        (input_grad,) = row_call(
            input_back,
            (tokens, grad_middle, back_own, others, one_far),
            (attn_gain,),
            (jnp.float32,),
        )
        up_grad = up.finish(up_keep, up_whole, up_second, up_end)
        gains = gains + gains_there
        gains = gains + exchange(gains, dp, 2)
        ends, gains, input_grad, up_grad = sync(ends, gains, input_grad, up_grad)
        step = 4
        while step < dp:
            gains = gains + exchange(gains, dp, step)
            step *= 2
        widths = (query_width, kv_width, kv_width)
        if dp == 8:
            qkv_grads = finish_three(qkv_keep, qkv_late, qkv_middle, ends[:, :width], widths)
        else:
            qkv_grad = qkv.finish(qkv_keep, qkv_late, qkv_middle, ends[:, :width])
            key_end = query_width + kv_width
            qkv_grads = (
                qkv_grad[:, :query_width], qkv_grad[:, query_width:key_end], qkv_grad[:, key_end:],
            )
        out_grad = out.finish(out_keep, out_whole, out_middle, ends[:, width:], turned=True)
        return (
            output,
            input_grad,
            gains[0],
            *qkv_grads,
            out_grad,
            gains[1],
            gate_grad,
            up_grad,
            down_grad,
        )

    return local


def solution(mesh):
    rows = P(("dp", "row", "col"), None)
    columns = P(None, ("row", "col"))
    placed = (
        rows,
        P("dp", None),
        P(),
        columns,
        columns,
        columns,
        P(("row", "col"), None),
        P(),
        columns,
        columns,
        P(("row", "col"), None),
        rows,
    )
    summed = P("dp", ("row", "col"))
    turned = P(("row", "col"), "dp")
    return jax.shard_map(
        local_for(mesh.shape["dp"]),
        mesh=mesh,
        in_specs=placed,
        out_specs=(rows, rows, P(), summed, summed, summed, turned, P(), summed, summed, turned),
        check_vma=False,
    )
```
